32 devices in a mesh: groups: 2 (over x), row: 16 (over z, y, core).
Axes of the slice: x: 2, y: 2, z: 4, core: 2. Of those that a mesh axis runs over, the one named last changes fastest.
Arguments:
- features: bfloat16 [64, 32, 4, 256], P('groups', 'row'), parts along dimension 0, may hold values from -6 to 6
- axial_taps: float32 [31, 256], replicated, may hold values from -1 to 1
- radial_taps: float32 [31, 256], replicated, may hold values from -1 to 1
- conv_bias: float32 [256], replicated, may hold values from -6 to 6
- ln_gain: float32 [256], replicated, may hold values from 0.5 to 1.5
- ln_bias: float32 [256], replicated, may hold values from -3 to 3
- w_in: bfloat16 [1024, 256], P('row'), may hold values from -0.375 to 0.375
- b_in: bfloat16 [1024], P('row'), may hold values from -3 to 3
- w_out: bfloat16 [1024, 256], P('row'), may hold values from -0.1875 to 0.1875
- b_out: float32 [256], replicated, may hold values from -1.75 to 1.75
- layer_scale: float32 [256], replicated, may hold values from 0.5 to 2
Outputs:
- block_out: bfloat16 [64, 32, 4, 256], P('groups', 'row'), parts along dimension 0
The draws below stay inside these ranges and needn't reach their ends.
There are 2 independent parts, one for each index of `groups`. The reference program is written for one: setup_inputs(seed, part) draws one part's arguments, and reference() takes and returns one part's arrays. A program takes and returns all parts, laid end to end along the dimension named above; an argument that names none is the same for every part. Nothing has to cross between parts.
All inputs are finite; a program needn't handle non-finite values.
Results may differ from the reference program's by a relative error of at most 0.01.
Values may be sent and summed in bfloat16 or wider, within the bound.
No kernel may reach another device: no remote copies, remote signals or barrier semaphores. Data moves between devices by JAX's collectives and lax.ppermute only.
A program may use at most 64 MiB of HBM per device.

```python
import math
from functools import partial
import jax
import jax.numpy as jnp
from jax import lax

C = 256
HID = 1024
TAPS = 31
AX_DEV = 2
THETA = 4
AXIAL = 32
RADIAL = 32


def shard_levels(key, shape, pieces, least, largest):
    loudness = 1.0
    for axis_at, parts in pieces:
        draws = jax.random.uniform(jax.random.fold_in(jax.random.fold_in(key, 6), axis_at), (parts,), jnp.float32, least / len(pieces), largest / len(pieces))
        loudness = loudness * jnp.repeat(jnp.exp(draws), shape[axis_at] // parts).reshape((-1,) + (1,) * (len(shape) - 1 - axis_at))
    return loudness


def normal_values(rng, dims, width, reach, pieces=(), dtype=jnp.bfloat16):
    level = shard_levels(rng, dims, pieces, -0.22, 0.18) if pieces else 1.0
    entries = jax.random.normal(rng, dims, jnp.float32) * width * level
    return jnp.minimum(jnp.maximum(entries, -reach), reach).astype(dtype)


def setup_inputs(seed: int = 0, part: int = 0) -> dict:
    key_of = jax.random.split(jax.random.key(seed), 12)
    part_splits = jax.random.split(jax.random.fold_in(key_of[11], part), 12)
    features = normal_values(part_splits[0], (AXIAL, RADIAL, THETA, C), 1.0, 6.0, ((1, 16),))
    axial_taps = normal_values(key_of[1], (TAPS, C), TAPS ** -0.5, 1.0, (), jnp.float32)
    radial_taps = normal_values(key_of[2], (TAPS, C), TAPS ** -0.5, 1.0, (), jnp.float32)
    conv_bias = normal_values(key_of[3], (C,), 1.0, 6.0, (), jnp.float32)
    ln_gain = jnp.clip(jax.random.uniform(key_of[4], (C,), jnp.float32, 0.5, 1.5), 0.5, 1.5)
    ln_bias = normal_values(key_of[5], (C,), 0.5, 3.0, (), jnp.float32)
    w_in = normal_values(key_of[6], (HID, C), C ** -0.5, 0.375, ((0, 16),))
    b_in = normal_values(key_of[7], (HID,), 0.5, 3.0, ((0, 16),))
    w_out = normal_values(key_of[8], (HID, C), HID ** -0.5, 0.1875, ((0, 16),))
    b_out = normal_values(key_of[9], (C,), 0.3, 1.75, (), jnp.float32)
    layer_scale = jnp.clip(jnp.exp(jax.random.uniform(key_of[10], (C,), jnp.float32, math.log(0.5), math.log(2.0))), 0.5, 2.0)
    return {"features": features, "axial_taps": axial_taps, "radial_taps": radial_taps, "conv_bias": conv_bias, "ln_gain": ln_gain, "ln_bias": ln_bias, "w_in": w_in, "b_in": b_in, "w_out": w_out, "b_out": b_out, "layer_scale": layer_scale}


def shifted_sum(source, tap_table, along_dim):
    half_span = tap_table.shape[0] // 2
    pad_widths = [(0, 0)] * source.ndim
    pad_widths[along_dim] = (half_span, half_span)
    padded = jnp.pad(source, pad_widths)
    extent = source.shape[along_dim]
    total_sum = jnp.zeros(source.shape, jnp.float32)
    for offset in range(tap_table.shape[0]):
        window = lax.slice_in_dim(padded, offset, offset + extent, axis=along_dim)
        total_sum = total_sum + window.astype(jnp.float32) * tap_table[offset]
    return total_sum

def block_mlp(params, row_block):
    w_in, b_in, w_out, ln_gain, ln_bias, b_out, layer_scale = params
    values = row_block.astype(jnp.float32)
    average = lax.optimization_barrier(jnp.mean(values, axis=-1, keepdims=True))
    centred = values - average
    variance = lax.optimization_barrier(jnp.mean(centred * centred, axis=-1, keepdims=True))
    normed = (centred * lax.rsqrt(variance + 1e-06) * ln_gain + ln_bias).astype(jnp.bfloat16)
    pre_act = lax.dot_general(normed, w_in, (((1,), (1,)), ((), ())), preferred_element_type=jnp.float32)
    pre_act = pre_act + b_in.astype(jnp.float32)
    hidden = jax.nn.gelu(pre_act, approximate=True).astype(jnp.bfloat16)
    projected = jnp.dot(hidden, w_out, preferred_element_type=jnp.float32) + b_out
    return (layer_scale * projected).astype(jnp.bfloat16)

def reference(features, axial_taps, radial_taps, conv_bias, ln_gain, ln_bias, w_in, b_in, w_out, b_out, layer_scale):
    params = (w_in, b_in, w_out, ln_gain, ln_bias, b_out, layer_scale)
    planes = jnp.moveaxis(features, 2, 0)
    channels = features.shape[-1]

    def one_plane(theta_plane):
        axial_mixed = shifted_sum(theta_plane, axial_taps, 0).astype(jnp.bfloat16)
        radial_mixed = (shifted_sum(axial_mixed, radial_taps, 1) + conv_bias).astype(jnp.bfloat16)
        groups = radial_mixed.reshape(AXIAL // AX_DEV, AX_DEV * RADIAL, channels)
        branch = lax.map(partial(block_mlp, params), groups).reshape(AXIAL, RADIAL, channels)
        return (theta_plane.astype(jnp.float32) + branch.astype(jnp.float32)).astype(jnp.bfloat16)
    result = lax.map(one_plane, planes)
    return jnp.moveaxis(result, 0, 2)
```

```python
from functools import partial

import jax
import jax.numpy as jnp
from jax import lax
from jax.experimental import pallas as pl
from jax.experimental.pallas import tpu as pltpu
from jax.sharding import PartitionSpec as P

SLOT = 64
EXTRA = 16


def vmem():
    return pl.BlockSpec(memory_space=pltpu.VMEM)


def pack_kernel(w_in_ref, w_out_ref, b_ref, out_ref):
    out_ref[0:SLOT, :] = w_in_ref[...]
    out_ref[SLOT : 2 * SLOT, :] = w_out_ref[...]
    out_ref[2 * SLOT : 2 * SLOT + EXTRA, :] = jnp.broadcast_to(b_ref[...], (EXTRA, out_ref.shape[1]))


def radial_kernel(x_ref, taps_ref, out_ref, even, odd):
    n, a_loc, _, theta, c = x_ref.shape
    taps = taps_ref.shape[0]
    pad = (taps + 1) // 4
    zeros = jnp.zeros((pad, a_loc, 2 * theta, c), jnp.float32)
    even[0:pad] = zeros
    even[pad + n : 2 * pad + n] = zeros
    odd[0:pad] = zeros
    odd[pad + n - 1 : 2 * pad + n - 1] = zeros
    odd[2 * pad + n - 1 :] = zeros[:1]
    first = x_ref[:, :, 0].astype(jnp.float32)
    second = x_ref[:, :, 1].astype(jnp.float32)
    even[pad : pad + n, :, 0:theta] = first
    even[pad : pad + n, :, theta:] = second
    odd[pad : pad + n, :, 0:theta] = second
    odd[pad - 1 : pad + n - 1, :, theta:] = first

    def step(s, carry):
        total = jnp.zeros((a_loc, 2 * theta, c), jnp.float32)
        for k in range(taps):
            shift = k - taps // 2
            source = even if shift % 2 == 0 else odd
            total = total + source[s + (pad + shift // 2)] * taps_ref[k : k + 1, :]
        out_ref[s] = total.astype(out_ref.dtype)
        return carry

    lax.fori_loop(0, n, step, 0)


def mlp_kernel(z_ref, feat_ref, w_ref, taps_ref, conv_b_ref, gain_ref, lnb_ref, b_out_ref, scale_ref, out_ref, padded, branch):
    axial, rows, c = z_ref.shape
    theta = rows // 2
    taps = taps_ref.shape[0]
    half = taps // 2
    zeros = jnp.zeros((half, rows, c), jnp.float32)
    padded[0:half] = zeros
    padded[half + axial :] = zeros
    padded[half : half + axial] = z_ref[...].astype(jnp.float32)
    slots = w_ref.shape[0]
    per = c // SLOT
    lane_slot = lax.broadcasted_iota(jnp.int32, (1, c), 1) // SLOT
    block = 4
    token_block = 32

    def conv(i, carry):
        base = i * block
        total = jnp.zeros((block, rows, c), jnp.float32)
        for k in range(taps):
            total = total + padded[pl.ds(base + k, block)] * taps_ref[k : k + 1, :]
        branch[pl.ds(base, block)] = total + conv_b_ref[...]
        return carry

    lax.fori_loop(0, axial // block, conv, 0)

    def mlp(i, carry):
        base = i * token_block
        v = branch[pl.ds(base, token_block)].reshape(token_block * rows, c)
        v = v.astype(jnp.bfloat16).astype(jnp.float32)
        mean = jnp.mean(v, axis=-1, keepdims=True)
        centred = v - mean
        var = jnp.mean(centred * centred, axis=-1, keepdims=True)
        normed = (centred * lax.rsqrt(var + 1e-06) * gain_ref[...] + lnb_ref[...]).astype(jnp.bfloat16)
        total = jnp.zeros(v.shape, jnp.float32)
        for g in range(slots // per):
            own = slice(g * per, (g + 1) * per)
            w_in = w_ref[own, 0:SLOT, :].reshape(per * SLOT, c)
            w_out = w_ref[own, SLOT : 2 * SLOT, :].reshape(per * SLOT, c)
            bias = jnp.zeros((1, c), jnp.float32)
            for j in range(per):
                piece = w_ref[g * per + j, 2 * SLOT : 2 * SLOT + EXTRA, :].astype(jnp.float32)[0:1]
                bias = jnp.where(lane_slot == j, piece, bias)
            u = lax.dot_general(normed, w_in, (((1,), (1,)), ((), ())), preferred_element_type=jnp.float32)
            u = u + bias
            hidden = (0.5 * u * (1.0 + jnp.tanh(0.7978845608028654 * (u + 0.044715 * u * u * u)))).astype(jnp.bfloat16)
            total = total + jnp.dot(hidden, w_out, preferred_element_type=jnp.float32)
        result = (scale_ref[...] * (total + b_out_ref[...])).astype(jnp.bfloat16).astype(jnp.float32)
        branch[pl.ds(base, token_block)] = result.reshape(token_block, rows, c)
        return carry

    lax.fori_loop(0, axial // token_block, mlp, 0)
    for r in range(2):
        got = branch[:, r * theta : (r + 1) * theta, :]
        out_ref[:, r] = (feat_ref[:, r].astype(jnp.float32) + got).astype(out_ref.dtype)


def digits(n):
    chips = n // 2
    inner = 1
    while inner * inner * 4 <= chips:
        inner *= 2
    return chips // inner, inner, 2


def shifted(n, digit, by):
    sizes = digits(n)
    stride = [sizes[1] * sizes[2], sizes[2], 1][digit]
    pairs = []
    for i in range(n):
        at = (i // stride) % sizes[digit]
        to = (at + by) % sizes[digit]
        pairs.append((i, i + (to - at) * stride))
    return pairs


def gather_slots(slot, n):
    held = slot[None]
    for digit, size in enumerate(digits(n)):
        parts = [held]
        for by in range(1, size):
            parts.append(lax.ppermute(held, "row", shifted(n, digit, by)))
        held = jnp.concatenate(parts, axis=0)
    return held


def local(n, features, axial_taps, radial_taps, conv_bias, ln_gain, ln_bias, w_in, b_in, w_out, b_out, layer_scale):
    axial, r_loc, theta, c = features.shape
    hid_loc = w_in.shape[0]
    a_loc = axial // n
    if hid_loc == SLOT:
        packed = pl.pallas_call(
            pack_kernel,
            out_shape=jax.ShapeDtypeStruct((2 * SLOT + EXTRA, c), jnp.bfloat16),
            in_specs=[vmem()] * 3,
            out_specs=vmem(),
            name="pack",
        )(w_in, w_out, jnp.tile(b_in, c // SLOT)[None, :])
        slots = gather_slots(packed, n)
    else:
        w_all = lax.all_gather(w_in, "row", axis=0, tiled=True).reshape(-1, SLOT, c)
        o_all = lax.all_gather(w_out, "row", axis=0, tiled=True).reshape(-1, SLOT, c)
        b_all = lax.all_gather(b_in, "row", axis=0, tiled=True).reshape(-1, 1, SLOT)
        b_all = jnp.broadcast_to(jnp.tile(b_all, (1, 1, c // SLOT)), (w_all.shape[0], EXTRA, c))
        slots = jnp.concatenate([w_all, o_all, b_all], axis=1)

    got = lax.all_to_all(features, "row", split_axis=0, concat_axis=0, tiled=True)
    pad = (radial_taps.shape[0] + 1) // 4
    mixed = pl.pallas_call(
        radial_kernel,
        out_shape=jax.ShapeDtypeStruct((n, a_loc, r_loc * theta, c), jnp.bfloat16),
        in_specs=[vmem()] * 2,
        out_specs=vmem(),
        scratch_shapes=[pltpu.VMEM((n + 2 * pad, a_loc, r_loc * theta, c), jnp.float32)] * 2,
        compiler_params=pltpu.CompilerParams(vmem_limit_bytes=48 * 1024 * 1024),
        name="radial",
    )(got.reshape(n, a_loc, r_loc, theta, c), radial_taps)
    back = lax.all_to_all(mixed.reshape(axial, r_loc * theta, c), "row", split_axis=0, concat_axis=0, tiled=True)
    return pl.pallas_call(
        mlp_kernel,
        out_shape=jax.ShapeDtypeStruct(features.shape, jnp.bfloat16),
        in_specs=[vmem()] * 9,
        out_specs=vmem(),
        scratch_shapes=[
            pltpu.VMEM((axial + axial_taps.shape[0] - 1, r_loc * theta, c), jnp.float32),
            pltpu.VMEM((axial, r_loc * theta, c), jnp.float32),
        ],
        compiler_params=pltpu.CompilerParams(vmem_limit_bytes=48 * 1024 * 1024),
        name="mlp",
    )(back, features, slots, axial_taps, conv_bias[None, :], ln_gain[None, :], ln_bias[None, :], b_out[None, :], layer_scale[None, :])


def solution(mesh):
    in_specs = (
        P("groups", "row", None, None),
        P(),
        P(),
        P(),
        P(),
        P(),
        P("row", None),
        P("row"),
        P("row", None),
        P(),
        P(),
    )
    out_specs = P("groups", "row", None, None)
    return jax.shard_map(partial(local, mesh.shape["row"]), mesh=mesh, in_specs=in_specs, out_specs=out_specs, check_vma=False)
```

```python
from functools import partial

import jax
import jax.numpy as jnp
from jax import lax
from jax.experimental import pallas as pl
from jax.experimental.pallas import tpu as pltpu
from jax.sharding import PartitionSpec as P

SLOT = 64
EXTRA = 16


def vmem():
    return pl.BlockSpec(memory_space=pltpu.VMEM)


def pack_kernel(w_in_ref, w_out_ref, b_ref, out_ref):
    out_ref[0:SLOT, :] = w_in_ref[...]
    out_ref[SLOT : 2 * SLOT, :] = w_out_ref[...]
    bias = b_ref[...].astype(jnp.float32)[None, :]
    wide = jnp.concatenate([bias] * (out_ref.shape[1] // SLOT), axis=1)
    out_ref[2 * SLOT : 2 * SLOT + EXTRA, :] = jnp.broadcast_to(wide, (EXTRA, out_ref.shape[1])).astype(out_ref.dtype)


def radial_kernel(x_ref, taps_ref, out_ref, even, odd):
    n, a_loc, _, theta, c = x_ref.shape
    taps = taps_ref.shape[0]
    pad = (taps + 1) // 4
    zeros = jnp.zeros((pad, a_loc, 2 * theta, c), jnp.float32)
    even[0:pad] = zeros
    even[pad + n : 2 * pad + n] = zeros
    odd[0:pad] = zeros
    odd[pad + n - 1 : 2 * pad + n - 1] = zeros
    odd[2 * pad + n - 1 :] = zeros[:1]
    first = x_ref[:, :, 0].astype(jnp.float32)
    second = x_ref[:, :, 1].astype(jnp.float32)
    even[pad : pad + n, :, 0:theta] = first
    even[pad : pad + n, :, theta:] = second
    odd[pad : pad + n, :, 0:theta] = second
    odd[pad - 1 : pad + n - 1, :, theta:] = first

    def step(s, carry):
        total = jnp.zeros((a_loc, 2 * theta, c), jnp.float32)
        for k in range(taps):
            shift = k - taps // 2
            source = even if shift % 2 == 0 else odd
            total = total + source[s + (pad + shift // 2)] * taps_ref[k : k + 1, :]
        out_ref[s] = total.astype(out_ref.dtype)
        return carry

    lax.fori_loop(0, n, step, 0)


def mlp_kernel(z_ref, feat_ref, taps_ref, conv_b_ref, gain_ref, lnb_ref, b_out_ref, scale_ref, *rest):
    *w_refs, out_ref, padded, branch = rest
    axial, rows, c = z_ref.shape
    theta = rows // 2
    taps = taps_ref.shape[0]
    half = taps // 2
    zeros = jnp.zeros((half, rows, c), jnp.float32)
    padded[0:half] = zeros
    padded[half + axial :] = zeros
    padded[half : half + axial] = z_ref[...].astype(jnp.float32)
    per = c // SLOT
    groups = [(w, g) for w in w_refs for g in range(w.shape[0] // per)]
    lane_slot = lax.broadcasted_iota(jnp.int32, (1, c), 1) // SLOT
    block = 4
    token_block = 32

    def conv(i, carry):
        base = i * block
        total = jnp.zeros((block, rows, c), jnp.float32)
        for k in range(taps):
            total = total + padded[pl.ds(base + k, block)] * taps_ref[k : k + 1, :]
        branch[pl.ds(base, block)] = total + conv_b_ref[...]
        return carry

    lax.fori_loop(0, axial // block, conv, 0)

    def mlp(i, carry):
        base = i * token_block
        v = branch[pl.ds(base, token_block)].reshape(token_block * rows, c)
        v = v.astype(jnp.bfloat16).astype(jnp.float32)
        mean = jnp.mean(v, axis=-1, keepdims=True)
        centred = v - mean
        var = jnp.mean(centred * centred, axis=-1, keepdims=True)
        normed = (centred * lax.rsqrt(var + 1e-06) * gain_ref[...] + lnb_ref[...]).astype(jnp.bfloat16)
        total = jnp.zeros(v.shape, jnp.float32)
        for w_ref, g in groups:
            own = slice(g * per, (g + 1) * per)
            w_in = w_ref[own, 0:SLOT, :].reshape(per * SLOT, c)
            w_out = w_ref[own, SLOT : 2 * SLOT, :].reshape(per * SLOT, c)
            bias = jnp.zeros((1, c), jnp.float32)
            for j in range(per):
                piece = w_ref[g * per + j, 2 * SLOT : 2 * SLOT + EXTRA, :].astype(jnp.float32)[0:1]
                bias = jnp.where(lane_slot == j, piece, bias)
            u = lax.dot_general(normed, w_in, (((1,), (1,)), ((), ())), preferred_element_type=jnp.float32)
            u = u + bias
            hidden = (0.5 * u * (1.0 + jnp.tanh(0.7978845608028654 * (u + 0.044715 * u * u * u)))).astype(jnp.bfloat16)
            total = total + jnp.dot(hidden, w_out, preferred_element_type=jnp.float32)
        result = (scale_ref[...] * (total + b_out_ref[...])).astype(jnp.bfloat16).astype(jnp.float32)
        branch[pl.ds(base, token_block)] = result.reshape(token_block, rows, c)
        return carry

    lax.fori_loop(0, axial // token_block, mlp, 0)
    for r in range(2):
        got = branch[:, r * theta : (r + 1) * theta, :]
        out_ref[:, r] = (feat_ref[:, r].astype(jnp.float32) + got).astype(out_ref.dtype)


def digits(n):
    chips = n // 2
    inner = 1
    while inner * inner * 4 <= chips:
        inner *= 2
    return chips // inner, inner, 2


def shifted(n, digit, by):
    sizes = digits(n)
    stride = [sizes[1] * sizes[2], sizes[2], 1][digit]
    pairs = []
    for i in range(n):
        at = (i // stride) % sizes[digit]
        to = (at + by) % sizes[digit]
        pairs.append((i, i + (to - at) * stride))
    return pairs


def join_kernel(*refs):
    out_ref = refs[-1]
    for i, ref in enumerate(refs[:-1]):
        out_ref[i] = ref[...]


def line_slots(slot, n):
    outer = digits(n)[0]
    line = [slot] + [lax.ppermute(slot, "row", shifted(n, 0, by)) for by in range(1, outer)]
    return pl.pallas_call(
        join_kernel,
        out_shape=jax.ShapeDtypeStruct((outer,) + slot.shape, slot.dtype),
        in_specs=[vmem()] * outer,
        out_specs=vmem(),
        name="join",
    )(*line)


def local(n, features, axial_taps, radial_taps, conv_bias, ln_gain, ln_bias, w_in, b_in, w_out, b_out, layer_scale):
    axial, r_loc, theta, c = features.shape
    hid_loc = w_in.shape[0]
    a_loc = axial // n
    if hid_loc == SLOT:
        packed = pl.pallas_call(
            pack_kernel,
            out_shape=jax.ShapeDtypeStruct((2 * SLOT + EXTRA, c), jnp.bfloat16),
            in_specs=[vmem()] * 3,
            out_specs=vmem(),
            name="pack",
        )(w_in, w_out, b_in)
        line = line_slots(packed, n)
    else:
        w_all = lax.all_gather(w_in, "row", axis=0, tiled=True).reshape(-1, SLOT, c)
        o_all = lax.all_gather(w_out, "row", axis=0, tiled=True).reshape(-1, SLOT, c)
        b_all = lax.all_gather(b_in, "row", axis=0, tiled=True).reshape(-1, 1, SLOT)
        b_all = jnp.broadcast_to(jnp.tile(b_all, (1, 1, c // SLOT)), (w_all.shape[0], EXTRA, c))
        slots = [jnp.concatenate([w_all, o_all, b_all], axis=1)]

    got = lax.all_to_all(features, "row", split_axis=0, concat_axis=0, tiled=True)
    if hid_loc == SLOT:
        line, got = lax.optimization_barrier((line, got))
        inner = [lax.ppermute(line, "row", shifted(n, 1, by)) for by in range(1, digits(n)[1])]
    pad = (radial_taps.shape[0] + 1) // 4
    mixed = pl.pallas_call(
        radial_kernel,
        out_shape=jax.ShapeDtypeStruct((n, a_loc, r_loc * theta, c), jnp.bfloat16),
        in_specs=[vmem()] * 2,
        out_specs=vmem(),
        scratch_shapes=[pltpu.VMEM((n + 2 * pad, a_loc, r_loc * theta, c), jnp.float32)] * 2,
        compiler_params=pltpu.CompilerParams(vmem_limit_bytes=48 * 1024 * 1024),
        name="radial",
    )(got.reshape(n, a_loc, r_loc, theta, c), radial_taps)
    if hid_loc == SLOT:
        inner = [lax.optimization_barrier((h, mixed))[0] for h in inner]
        slots = [line] + inner
        slots = slots + [lax.ppermute(h, "row", shifted(n, 2, 1)) for h in slots]
    back = lax.all_to_all(mixed.reshape(axial, r_loc * theta, c), "row", split_axis=0, concat_axis=0, tiled=True)
    return pl.pallas_call(
        mlp_kernel,
        out_shape=jax.ShapeDtypeStruct(features.shape, jnp.bfloat16),
        in_specs=[vmem()] * (8 + len(slots)),
        out_specs=vmem(),
        scratch_shapes=[
            pltpu.VMEM((axial + axial_taps.shape[0] - 1, r_loc * theta, c), jnp.float32),
            pltpu.VMEM((axial, r_loc * theta, c), jnp.float32),
        ],
        compiler_params=pltpu.CompilerParams(vmem_limit_bytes=48 * 1024 * 1024),
        name="mlp",
    )(back, features, axial_taps, conv_bias[None, :], ln_gain[None, :], ln_bias[None, :], b_out[None, :], layer_scale[None, :], *slots)


def solution(mesh):
    in_specs = (
        P("groups", "row", None, None),
        P(),
        P(),
        P(),
        P(),
        P(),
        P("row", None),
        P("row"),
        P("row", None),
        P(),
        P(),
    )
    out_specs = P("groups", "row", None, None)
    return jax.shard_map(partial(local, mesh.shape["row"]), mesh=mesh, in_specs=in_specs, out_specs=out_specs, check_vma=False)
```

```python
from functools import partial

import jax
import jax.numpy as jnp
from jax import lax
from jax.experimental import pallas as pl
from jax.experimental.pallas import tpu as pltpu
from jax.sharding import PartitionSpec as P

SLOT = 64
EXTRA = 16


def vmem():
    return pl.BlockSpec(memory_space=pltpu.VMEM)


def pack_kernel(w_in_ref, w_out_ref, b_ref, out_ref):
    out_ref[0, 0:SLOT, :] = w_in_ref[...]
    out_ref[0, SLOT : 2 * SLOT, :] = w_out_ref[...]
    bias = b_ref[...].astype(jnp.float32)[None, :]
    c = out_ref.shape[2]
    wide = jnp.concatenate([bias] * (c // SLOT), axis=1)
    out_ref[0, 2 * SLOT : 2 * SLOT + EXTRA, :] = jnp.broadcast_to(wide, (EXTRA, c)).astype(out_ref.dtype)


def radial_kernel(pieces, x_ref, taps_ref, *rest):
    if pieces:
        joined_ref, even, odd, sems = rest[pieces + 1 :]
        copies = [pltpu.make_async_copy(rest[i], joined_ref.at[i : i + 1], sems.at[i]) for i in range(pieces)]
    else:
        even, odd = rest[1:]
        copies = []
    out_ref = rest[pieces]
    for copy in copies:
        copy.start()
    n, a_loc, _, theta, c = x_ref.shape
    taps = taps_ref.shape[0]
    pad = (taps + 1) // 4
    zeros = jnp.zeros((pad, a_loc, 2 * theta, c), jnp.float32)
    even[0:pad] = zeros
    even[pad + n : 2 * pad + n] = zeros
    odd[0:pad] = zeros
    odd[pad + n - 1 : 2 * pad + n - 1] = zeros
    odd[2 * pad + n - 1 :] = zeros[:1]
    first = x_ref[:, :, 0].astype(jnp.float32)
    second = x_ref[:, :, 1].astype(jnp.float32)
    even[pad : pad + n, :, 0:theta] = first
    even[pad : pad + n, :, theta:] = second
    odd[pad : pad + n, :, 0:theta] = second
    odd[pad - 1 : pad + n - 1, :, theta:] = first

    def step(s, carry):
        total = jnp.zeros((a_loc, 2 * theta, c), jnp.float32)
        for k in range(taps):
            shift = k - taps // 2
            source = even if shift % 2 == 0 else odd
            total = total + source[s + (pad + shift // 2)] * taps_ref[k : k + 1, :]
        out_ref[s] = total.astype(out_ref.dtype)
        return carry

    lax.fori_loop(0, n, step, 0)
    for copy in copies:
        copy.wait()


def axial_kernel(z_ref, taps_ref, conv_b_ref, gain_ref, lnb_ref, out_ref, padded):
    axial, rows, c = z_ref.shape
    taps = taps_ref.shape[0]
    half = taps // 2
    zeros = jnp.zeros((half, rows, c), jnp.float32)
    padded[0:half] = zeros
    padded[half + axial :] = zeros
    padded[half : half + axial] = z_ref[...].astype(jnp.float32)
    block = 4

    def conv(i, carry):
        base = i * block
        total = jnp.zeros((block, rows, c), jnp.float32)
        for k in range(taps):
            total = total + padded[pl.ds(base + k, block)] * taps_ref[k : k + 1, :]
        v = (total + conv_b_ref[...]).reshape(block * rows, c)
        v = v.astype(jnp.bfloat16).astype(jnp.float32)
        mean = jnp.mean(v, axis=-1, keepdims=True)
        centred = v - mean
        var = jnp.mean(centred * centred, axis=-1, keepdims=True)
        normed = centred * lax.rsqrt(var + 1e-06) * gain_ref[...] + lnb_ref[...]
        at = pl.multiple_of(base * rows, block * rows)
        out_ref[pl.ds(at, block * rows), :] = normed.astype(out_ref.dtype)
        return carry

    lax.fori_loop(0, axial // block, conv, 0)


def mlp_kernel(normed_ref, feat_ref, b_out_ref, scale_ref, *rest):
    *w_refs, out_ref, slots, branch, sems = rest
    axial, _, theta, c = feat_ref.shape
    rows = 2 * theta
    per = c // SLOT
    lane_slot = lax.broadcasted_iota(jnp.int32, (1, c), 1) // SLOT
    token_block = 32 * rows
    copies, at = [], 0
    for i, w_ref in enumerate(w_refs):
        copies.append(pltpu.make_async_copy(w_ref, slots.at[at : at + w_ref.shape[0]], sems.at[i]))
        at += w_ref.shape[0]
    for copy in copies:
        copy.start()
    for copy in copies:
        copy.wait()

    def mlp(i, carry):
        base = pl.multiple_of(i * token_block, token_block)
        normed = normed_ref[pl.ds(base, token_block), :]
        total = jnp.zeros((token_block, c), jnp.float32)
        for g in range(slots.shape[0] // per):
            own = slice(g * per, (g + 1) * per)
            w_in = slots[own, 0:SLOT, :].reshape(per * SLOT, c)
            w_out = slots[own, SLOT : 2 * SLOT, :].reshape(per * SLOT, c)
            bias = jnp.zeros((1, c), jnp.float32)
            for j in range(per):
                piece = slots[g * per + j, 2 * SLOT : 2 * SLOT + EXTRA, :].astype(jnp.float32)[0:1]
                bias = jnp.where(lane_slot == j, piece, bias)
            u = lax.dot_general(normed, w_in, (((1,), (1,)), ((), ())), preferred_element_type=jnp.float32)
            u = u + bias
            hidden = (0.5 * u * (1.0 + jnp.tanh(0.7978845608028654 * (u + 0.044715 * u * u * u)))).astype(jnp.bfloat16)
            total = total + jnp.dot(hidden, w_out, preferred_element_type=jnp.float32)
        result = (scale_ref[...] * (total + b_out_ref[...])).astype(jnp.bfloat16).astype(jnp.float32)
        branch[pl.ds(i * 32, 32)] = result.reshape(32, rows, c)
        return carry

    lax.fori_loop(0, axial // 32, mlp, 0)
    for r in range(2):
        got = branch[:, r * theta : (r + 1) * theta, :]
        out_ref[:, r] = (feat_ref[:, r].astype(jnp.float32) + got).astype(out_ref.dtype)


def digits(n):
    chips = n // 2
    inner = 1
    while inner * inner * 4 <= chips:
        inner *= 2
    return chips // inner, inner, 2


def shifted(n, digit, by):
    sizes = digits(n)
    stride = [sizes[1] * sizes[2], sizes[2], 1][digit]
    pairs = []
    for i in range(n):
        at = (i // stride) % sizes[digit]
        to = (at + by) % sizes[digit]
        pairs.append((i, i + (to - at) * stride))
    return pairs


def local(n, features, axial_taps, radial_taps, conv_bias, ln_gain, ln_bias, w_in, b_in, w_out, b_out, layer_scale):
    axial, r_loc, theta, c = features.shape
    rows = r_loc * theta
    hid_loc = w_in.shape[0]
    a_loc = axial // n
    spread = hid_loc == SLOT
    params = pltpu.CompilerParams(vmem_limit_bytes=48 * 1024 * 1024)

    def move(piece, digit, by=1):
        return lax.ppermute(piece, "row", shifted(n, digit, by))

    outer, inner, _ = digits(n)
    if spread:
        own = pl.pallas_call(
            pack_kernel,
            out_shape=jax.ShapeDtypeStruct((1, 2 * SLOT + EXTRA, c), jnp.bfloat16),
            in_specs=[vmem()] * 3,
            out_specs=vmem(),
            name="pack",
        )(w_in, w_out, b_in)
        line = [own] + [move(own, 0, by) for by in range(1, outer)]
    else:
        line = []
        w_all = lax.all_gather(w_in, "row", axis=0, tiled=True).reshape(-1, SLOT, c)
        o_all = lax.all_gather(w_out, "row", axis=0, tiled=True).reshape(-1, SLOT, c)
        b_all = lax.all_gather(b_in, "row", axis=0, tiled=True).reshape(-1, 1, SLOT)
        b_all = jnp.broadcast_to(jnp.tile(b_all, (1, 1, c // SLOT)), (w_all.shape[0], EXTRA, c))
        slots = [jnp.concatenate([w_all, o_all, b_all], axis=1)]

    got = lax.all_to_all(features, "row", split_axis=0, concat_axis=0, tiled=True)
    pad = (radial_taps.shape[0] + 1) // 4
    anywhere = pl.BlockSpec(memory_space=pl.ANY)
    pieces = len(line)
    slot_shape = (2 * SLOT + EXTRA, c)
    out_shape = [jax.ShapeDtypeStruct((n, a_loc, rows, c), jnp.bfloat16)]
    scratch = [pltpu.VMEM((n + 2 * pad, a_loc, rows, c), jnp.float32)] * 2
    if spread:
        out_shape.append(jax.ShapeDtypeStruct((pieces,) + slot_shape, jnp.bfloat16))
        scratch.append(pltpu.SemaphoreType.DMA((pieces,)))
    mixed, *joined = pl.pallas_call(
        partial(radial_kernel, pieces),
        out_shape=out_shape,
        in_specs=[vmem()] * 2 + [anywhere] * pieces,
        out_specs=[vmem()] + [anywhere] * (len(out_shape) - 1),
        scratch_shapes=scratch,
        compiler_params=params,
        name="radial",
    )(got.reshape(n, a_loc, r_loc, theta, c), radial_taps, *line)
    if spread:
        across = [move(h, 1, by) for by in range(1, inner) for h in joined]
        twin = [move(h, 2) for h in joined]
    back = lax.all_to_all(mixed.reshape(axial, rows, c), "row", split_axis=0, concat_axis=0, tiled=True)
    if spread:
        across, back = lax.optimization_barrier((across, back))
        slots = joined + across + twin + [move(h, 2) for h in across]
    normed = pl.pallas_call(
        axial_kernel,
        out_shape=jax.ShapeDtypeStruct((axial * rows, c), jnp.bfloat16),
        in_specs=[vmem()] * 5,
        out_specs=vmem(),
        scratch_shapes=[pltpu.VMEM((axial + axial_taps.shape[0] - 1, rows, c), jnp.float32)],
        compiler_params=params,
        name="axial",
    )(back, axial_taps, conv_bias[None, :], ln_gain[None, :], ln_bias[None, :])
    count = sum(h.shape[0] for h in slots)
    return pl.pallas_call(
        mlp_kernel,
        out_shape=jax.ShapeDtypeStruct(features.shape, jnp.bfloat16),
        in_specs=[vmem()] * 4 + [anywhere] * len(slots),
        out_specs=vmem(),
        scratch_shapes=[
            pltpu.VMEM((count,) + slot_shape, jnp.bfloat16),
            pltpu.VMEM((axial, rows, c), jnp.float32),
            pltpu.SemaphoreType.DMA((len(slots),)),
        ],
        compiler_params=params,
        name="mlp",
    )(normed, features, b_out[None, :], layer_scale[None, :], *slots)


def solution(mesh):
    in_specs = (
        P("groups", "row", None, None),
        P(),
        P(),
        P(),
        P(),
        P(),
        P("row", None),
        P("row"),
        P("row", None),
        P(),
        P(),
    )
    out_specs = P("groups", "row", None, None)
    return jax.shard_map(partial(local, mesh.shape["row"]), mesh=mesh, in_specs=in_specs, out_specs=out_specs, check_vma=False)
```

```python
from functools import partial

import jax
import jax.numpy as jnp
from jax import lax
from jax.experimental import pallas as pl
from jax.experimental.pallas import tpu as pltpu
from jax.sharding import PartitionSpec as P

SLOT = 64
EXTRA = 16


def vmem():
    return pl.BlockSpec(memory_space=pltpu.VMEM)


def pack_kernel(b_ref, w_in_ref, w_out_ref, taps_ref, *rest):
    vectors = rest[:5]
    slot_ref, taps_out, consts_out, staged, sems = rest[5:]
    copies = [
        pltpu.make_async_copy(w_in_ref, slot_ref.at[0, 0:SLOT], sems.at[0]),
        pltpu.make_async_copy(w_out_ref, slot_ref.at[0, SLOT : 2 * SLOT], sems.at[1]),
        pltpu.make_async_copy(taps_ref, taps_out, sems.at[2]),
    ]
    for i, vector in enumerate(vectors):
        copies.append(pltpu.make_async_copy(vector, staged.at[i], sems.at[3 + i]))
    for copy in copies:
        copy.start()
    bias = b_ref[...].astype(jnp.float32)[None, :]
    c = slot_ref.shape[2]
    wide = jnp.concatenate([bias] * (c // SLOT), axis=1)
    slot_ref[0, 2 * SLOT : 2 * SLOT + EXTRA, :] = jnp.broadcast_to(wide, (EXTRA, c)).astype(slot_ref.dtype)
    for copy in copies:
        copy.wait()
    for i in range(5):
        consts_out[i : i + 1, :] = staged[i]


def radial_kernel(x_ref, taps_ref, out_ref, even, odd):
    n, a_loc, _, theta, c = x_ref.shape
    taps = taps_ref.shape[0]
    pad = (taps + 1) // 4
    zeros = jnp.zeros((pad, a_loc, 2 * theta, c), jnp.float32)
    even[0:pad] = zeros
    even[pad + n : 2 * pad + n] = zeros
    odd[0:pad] = zeros
    odd[pad + n - 1 : 2 * pad + n - 1] = zeros
    odd[2 * pad + n - 1 :] = zeros[:1]
    first = x_ref[:, :, 0].astype(jnp.float32)
    second = x_ref[:, :, 1].astype(jnp.float32)
    even[pad : pad + n, :, 0:theta] = first
    even[pad : pad + n, :, theta:] = second
    odd[pad : pad + n, :, 0:theta] = second
    odd[pad - 1 : pad + n - 1, :, theta:] = first

    def step(s, carry):
        total = jnp.zeros((a_loc, 2 * theta, c), jnp.float32)
        for k in range(taps):
            shift = k - taps // 2
            source = even if shift % 2 == 0 else odd
            total = total + source[s + (pad + shift // 2)] * taps_ref[k : k + 1, :]
        out_ref[s] = total.astype(out_ref.dtype)
        return carry

    lax.fori_loop(0, n, step, 0)


def join_kernel(pieces, *refs):
    out_ref, sems = refs[pieces + 1 :]
    copies = [pltpu.make_async_copy(refs[i], out_ref.at[i : i + 1], sems.at[i]) for i in range(pieces)]
    for copy in copies:
        copy.start()
    for copy in copies:
        copy.wait()


def axial_kernel(z_ref, taps_ref, consts_ref, out_ref, padded, summed):
    axial, rows, c = z_ref.shape
    taps = taps_ref.shape[0]
    half = taps // 2
    zeros = jnp.zeros((half, rows, c), jnp.float32)
    padded[0:half] = zeros
    padded[half + axial :] = zeros
    padded[half : half + axial] = z_ref[...].astype(jnp.float32)
    block = 4

    def conv(i, carry):
        base = i * block
        total = jnp.zeros((block, rows, c), jnp.float32)
        for k in range(taps):
            total = total + padded[pl.ds(base + k, block)] * taps_ref[k : k + 1, :]
        summed[pl.ds(base, block)] = total
        return carry

    lax.fori_loop(0, axial // block, conv, 0)

    def norm(i, carry):
        v = (summed[pl.ds(i * 32, 32)] + consts_ref[0:1, :]).reshape(32 * rows, c)
        v = v.astype(jnp.bfloat16).astype(jnp.float32)
        mean = jnp.mean(v, axis=-1, keepdims=True)
        centred = v - mean
        var = jnp.mean(centred * centred, axis=-1, keepdims=True)
        normed = centred * lax.rsqrt(var + 1e-06) * consts_ref[1:2, :] + consts_ref[2:3, :]
        at = pl.multiple_of(i * 32 * rows, 32 * rows)
        out_ref[pl.ds(at, 32 * rows), :] = normed.astype(out_ref.dtype)
        return carry

    lax.fori_loop(0, axial // 32, norm, 0)


def mlp_kernel(normed_ref, feat_ref, consts_ref, *rest):
    *w_refs, out_ref, slots, branch, sems = rest
    axial, _, theta, c = feat_ref.shape
    rows = 2 * theta
    per = c // SLOT
    lane_slot = lax.broadcasted_iota(jnp.int32, (1, c), 1) // SLOT
    token_block = 32 * rows
    copies, begins = [], []
    for i, w_ref in enumerate(w_refs):
        begins.append(sum(w.shape[0] for w in w_refs[:i]))
        copies.append(pltpu.make_async_copy(w_ref, slots.at[begins[i] : begins[i] + w_ref.shape[0]], sems.at[i]))
    for copy in copies:
        copy.start()
    single = axial == 32
    if not single:
        for copy in copies:
            copy.wait()

    def mlp(i, carry):
        base = pl.multiple_of(i * token_block, token_block)
        normed = normed_ref[pl.ds(base, token_block), :]
        total = jnp.zeros((token_block, c), jnp.float32)
        for g in range(slots.shape[0] // per):
            own = slice(g * per, (g + 1) * per)
            for at, copy in zip(begins, copies):
                if single and own.start <= at < own.stop:
                    copy.wait()
            w_in = slots[own, 0:SLOT, :].reshape(per * SLOT, c)
            w_out = slots[own, SLOT : 2 * SLOT, :].reshape(per * SLOT, c)
            bias = jnp.zeros((1, c), jnp.float32)
            for j in range(per):
                piece = slots[g * per + j, 2 * SLOT : 2 * SLOT + EXTRA, :].astype(jnp.float32)[0:1]
                bias = jnp.where(lane_slot == j, piece, bias)
            u = lax.dot_general(normed, w_in, (((1,), (1,)), ((), ())), preferred_element_type=jnp.float32)
            u = u + bias
            hidden = (0.5 * u * (1.0 + jnp.tanh(0.7978845608028654 * (u + 0.044715 * u * u * u)))).astype(jnp.bfloat16)
            total = total + jnp.dot(hidden, w_out, preferred_element_type=jnp.float32)
        result = (consts_ref[4:5, :] * (total + consts_ref[3:4, :])).astype(jnp.bfloat16).astype(jnp.float32)
        branch[pl.ds(i * 32, 32)] = result.reshape(32, rows, c)
        return carry

    if single:
        mlp(0, 0)
    else:
        lax.fori_loop(0, axial // 32, mlp, 0)
    for r in range(2):
        got = branch[:, r * theta : (r + 1) * theta, :]
        out_ref[:, r] = (feat_ref[:, r].astype(jnp.float32) + got).astype(out_ref.dtype)


def digits(n):
    chips = n // 2
    inner = 1
    while inner * inner * 4 <= chips:
        inner *= 2
    return chips // inner, inner, 2


def shifted(n, digit, by):
    sizes = digits(n)
    stride = [sizes[1] * sizes[2], sizes[2], 1][digit]
    pairs = []
    for i in range(n):
        at = (i // stride) % sizes[digit]
        to = (at + by) % sizes[digit]
        pairs.append((i, i + (to - at) * stride))
    return pairs


def local(n, features, axial_taps, radial_taps, conv_bias, ln_gain, ln_bias, w_in, b_in, w_out, b_out, layer_scale):
    axial, r_loc, theta, c = features.shape
    rows = r_loc * theta
    hid_loc = w_in.shape[0]
    a_loc = axial // n
    spread = hid_loc == SLOT
    params = pltpu.CompilerParams(vmem_limit_bytes=48 * 1024 * 1024)

    def move(piece, digit, by=1):
        return lax.ppermute(piece, "row", shifted(n, digit, by))

    outer, inner, _ = digits(n)
    anywhere = pl.BlockSpec(memory_space=pl.ANY)
    vectors = [v[None, :] for v in (conv_bias, ln_gain, ln_bias, b_out, layer_scale)]
    slot_shape = (2 * SLOT + EXTRA, c)
    if spread:
        own, axial_taps, consts = pl.pallas_call(
            pack_kernel,
            out_shape=[
                jax.ShapeDtypeStruct((1,) + slot_shape, jnp.bfloat16),
                jax.ShapeDtypeStruct(axial_taps.shape, jnp.float32),
                jax.ShapeDtypeStruct((8, c), jnp.float32),
            ],
            in_specs=[vmem()] + [anywhere] * 8,
            out_specs=[vmem()] * 3,
            scratch_shapes=[pltpu.VMEM((5, 1, c), jnp.float32), pltpu.SemaphoreType.DMA((8,))],
            name="pack",
        )(b_in, w_in, w_out, axial_taps, *vectors)
        line = [own] + [move(own, 0, by) for by in range(1, outer)]
    else:
        consts = jnp.concatenate(vectors + [jnp.zeros((3, c), jnp.float32)], axis=0)
        w_all = lax.all_gather(w_in, "row", axis=0, tiled=True).reshape(-1, SLOT, c)
        o_all = lax.all_gather(w_out, "row", axis=0, tiled=True).reshape(-1, SLOT, c)
        b_all = lax.all_gather(b_in, "row", axis=0, tiled=True).reshape(-1, 1, SLOT)
        b_all = jnp.broadcast_to(jnp.tile(b_all, (1, 1, c // SLOT)), (w_all.shape[0], EXTRA, c))
        slots = [jnp.concatenate([w_all, o_all, b_all], axis=1)]

    got = lax.all_to_all(features, "row", split_axis=0, concat_axis=0, tiled=True)
    pad = (radial_taps.shape[0] + 1) // 4
    mixed = pl.pallas_call(
        radial_kernel,
        out_shape=jax.ShapeDtypeStruct((n, a_loc, rows, c), jnp.bfloat16),
        in_specs=[vmem()] * 2,
        out_specs=vmem(),
        scratch_shapes=[pltpu.VMEM((n + 2 * pad, a_loc, rows, c), jnp.float32)] * 2,
        compiler_params=params,
        name="radial",
    )(got.reshape(n, a_loc, r_loc, theta, c), radial_taps)
    if spread:
        joined = pl.pallas_call(
            partial(join_kernel, outer),
            out_shape=jax.ShapeDtypeStruct((outer,) + slot_shape, jnp.bfloat16),
            in_specs=[anywhere] * (outer + 1),
            out_specs=vmem(),
            scratch_shapes=[pltpu.SemaphoreType.DMA((outer,))],
            name="join",
        )(*line, mixed)
        across = [move(joined, 1, by) for by in range(1, inner)]
        twin = [move(joined, 2)]
    back = lax.all_to_all(mixed.reshape(axial, rows, c), "row", split_axis=0, concat_axis=0, tiled=True)
    if spread:
        across, back = lax.optimization_barrier((across, back))
        slots = [joined] + across + twin + [move(h, 2) for h in across]
    normed = pl.pallas_call(
        axial_kernel,
        out_shape=jax.ShapeDtypeStruct((axial * rows, c), jnp.bfloat16),
        in_specs=[vmem()] * 3,
        out_specs=vmem(),
        scratch_shapes=[
            pltpu.VMEM((axial + axial_taps.shape[0] - 1, rows, c), jnp.float32),
            pltpu.VMEM((axial, rows, c), jnp.float32),
        ],
        compiler_params=params,
        name="axial",
    )(back, axial_taps, consts)
    count = sum(h.shape[0] for h in slots)
    return pl.pallas_call(
        mlp_kernel,
        out_shape=jax.ShapeDtypeStruct(features.shape, jnp.bfloat16),
        in_specs=[vmem()] * 3 + [anywhere] * len(slots),
        out_specs=vmem(),
        scratch_shapes=[
            pltpu.VMEM((count,) + slot_shape, jnp.bfloat16),
            pltpu.VMEM((axial, rows, c), jnp.float32),
            pltpu.SemaphoreType.DMA((len(slots),)),
        ],
        compiler_params=params,
        name="mlp",
    )(normed, features, consts, *slots)


def solution(mesh):
    in_specs = (
        P("groups", "row", None, None),
        P(),
        P(),
        P(),
        P(),
        P(),
        P("row", None),
        P("row"),
        P("row", None),
        P(),
        P(),
    )
    out_specs = P("groups", "row", None, None)
    return jax.shard_map(partial(local, mesh.shape["row"]), mesh=mesh, in_specs=in_specs, out_specs=out_specs, check_vma=False)
```

```python
from functools import partial

import jax
import jax.numpy as jnp
from jax import lax
from jax.experimental import pallas as pl
from jax.experimental.pallas import tpu as pltpu
from jax.sharding import PartitionSpec as P

SLOT = 64
EXTRA = 16


def vmem():
    return pl.BlockSpec(memory_space=pltpu.VMEM)


def pack_kernel(b_ref, w_in_ref, w_out_ref, taps_ref, *rest):
    vectors = rest[:5]
    slot_ref, taps_out, consts_out, staged, sems = rest[5:]
    copies = [
        pltpu.make_async_copy(w_in_ref, slot_ref.at[0, 0:SLOT], sems.at[0]),
        pltpu.make_async_copy(w_out_ref, slot_ref.at[0, SLOT : 2 * SLOT], sems.at[1]),
        pltpu.make_async_copy(taps_ref, taps_out, sems.at[2]),
    ]
    for i, vector in enumerate(vectors):
        copies.append(pltpu.make_async_copy(vector, staged.at[i], sems.at[3 + i]))
    for copy in copies:
        copy.start()
    bias = b_ref[...].astype(jnp.float32)[None, :]
    c = slot_ref.shape[2]
    wide = jnp.concatenate([bias] * (c // SLOT), axis=1)
    slot_ref[0, 2 * SLOT : 2 * SLOT + EXTRA, :] = jnp.broadcast_to(wide, (EXTRA, c)).astype(slot_ref.dtype)
    for copy in copies:
        copy.wait()
    for i in range(5):
        consts_out[i : i + 1, :] = staged[i]


def radial_kernel(x_ref, taps_ref, out_ref, even, odd):
    n, a_loc, _, theta, c = x_ref.shape
    taps = taps_ref.shape[0]
    pad = (taps + 1) // 4
    zeros = jnp.zeros((pad, a_loc, 2 * theta, c), jnp.float32)
    even[0:pad] = zeros
    even[pad + n : 2 * pad + n] = zeros
    odd[0:pad] = zeros
    odd[pad + n - 1 : 2 * pad + n - 1] = zeros
    odd[2 * pad + n - 1 :] = zeros[:1]
    first = x_ref[:, :, 0].astype(jnp.float32)
    second = x_ref[:, :, 1].astype(jnp.float32)
    even[pad : pad + n, :, 0:theta] = first
    even[pad : pad + n, :, theta:] = second
    odd[pad : pad + n, :, 0:theta] = second
    odd[pad - 1 : pad + n - 1, :, theta:] = first

    def step(s, carry):
        total = jnp.zeros((a_loc, 2 * theta, c), jnp.float32)
        for k in range(taps):
            shift = k - taps // 2
            source = even if shift % 2 == 0 else odd
            total = total + source[s + (pad + shift // 2)] * taps_ref[k : k + 1, :]
        out_ref[s] = total.astype(out_ref.dtype)
        return carry

    lax.fori_loop(0, n, step, 0)


def axial_kernel(z_ref, taps_ref, consts_ref, out_ref, padded, summed):
    axial, rows, c = z_ref.shape
    taps = taps_ref.shape[0]
    half = taps // 2
    zeros = jnp.zeros((half, rows, c), jnp.float32)
    padded[0:half] = zeros
    padded[half + axial :] = zeros
    padded[half : half + axial] = z_ref[...].astype(jnp.float32)
    block = 4

    def conv(i, carry):
        base = i * block
        total = jnp.zeros((block, rows, c), jnp.float32)
        for k in range(taps):
            total = total + padded[pl.ds(base + k, block)] * taps_ref[k : k + 1, :]
        summed[pl.ds(base, block)] = total
        return carry

    lax.fori_loop(0, axial // block, conv, 0)

    def norm(i, carry):
        v = (summed[pl.ds(i * 32, 32)] + consts_ref[0:1, :]).reshape(32 * rows, c)
        v = v.astype(jnp.bfloat16).astype(jnp.float32)
        mean = jnp.mean(v, axis=-1, keepdims=True)
        centred = v - mean
        var = jnp.mean(centred * centred, axis=-1, keepdims=True)
        normed = centred * lax.rsqrt(var + 1e-06) * consts_ref[1:2, :] + consts_ref[2:3, :]
        at = pl.multiple_of(i * 32 * rows, 32 * rows)
        out_ref[pl.ds(at, 32 * rows), :] = normed.astype(out_ref.dtype)
        return carry

    lax.fori_loop(0, axial // 32, norm, 0)


def mlp_kernel(normed_ref, feat_ref, consts_ref, *rest):
    *w_refs, out_ref, slots, branch, sems = rest
    axial, _, theta, c = feat_ref.shape
    rows = 2 * theta
    per = c // SLOT
    lane_slot = lax.broadcasted_iota(jnp.int32, (1, c), 1) // SLOT
    token_block = 32 * rows
    copies, at = [], 0
    for i, w_ref in enumerate(w_refs):
        copies.append(pltpu.make_async_copy(w_ref, slots.at[at : at + w_ref.shape[0]], sems.at[i]))
        at += w_ref.shape[0]
    for copy in copies:
        copy.start()
    for copy in copies:
        copy.wait()

    def mlp(i, carry):
        base = pl.multiple_of(i * token_block, token_block)
        normed = normed_ref[pl.ds(base, token_block), :]
        total = jnp.zeros((token_block, c), jnp.float32)
        for g in range(slots.shape[0] // per):
            own = slice(g * per, (g + 1) * per)
            w_in = slots[own, 0:SLOT, :].reshape(per * SLOT, c)
            w_out = slots[own, SLOT : 2 * SLOT, :].reshape(per * SLOT, c)
            bias = jnp.zeros((1, c), jnp.float32)
            for j in range(per):
                piece = slots[g * per + j, 2 * SLOT : 2 * SLOT + EXTRA, :].astype(jnp.float32)[0:1]
                bias = jnp.where(lane_slot == j, piece, bias)
            u = lax.dot_general(normed, w_in, (((1,), (1,)), ((), ())), preferred_element_type=jnp.float32)
            u = u + bias
            hidden = (0.5 * u * (1.0 + jnp.tanh(0.7978845608028654 * (u + 0.044715 * u * u * u)))).astype(jnp.bfloat16)
            total = total + jnp.dot(hidden, w_out, preferred_element_type=jnp.float32)
        result = (consts_ref[4:5, :] * (total + consts_ref[3:4, :])).astype(jnp.bfloat16).astype(jnp.float32)
        branch[pl.ds(i * 32, 32)] = result.reshape(32, rows, c)
        return carry

    if axial == 32:
        mlp(0, 0)
    else:
        lax.fori_loop(0, axial // 32, mlp, 0)
    for r in range(2):
        got = branch[:, r * theta : (r + 1) * theta, :]
        out_ref[:, r] = (feat_ref[:, r].astype(jnp.float32) + got).astype(out_ref.dtype)


def digits(n):
    chips = n // 2
    inner = 1
    while inner * inner * 4 <= chips:
        inner *= 2
    return chips // inner, inner, 2


def shifted(n, digit, by):
    sizes = digits(n)
    stride = [sizes[1] * sizes[2], sizes[2], 1][digit]
    pairs = []
    for i in range(n):
        at = (i // stride) % sizes[digit]
        to = (at + by) % sizes[digit]
        pairs.append((i, i + (to - at) * stride))
    return pairs


def local(n, features, axial_taps, radial_taps, conv_bias, ln_gain, ln_bias, w_in, b_in, w_out, b_out, layer_scale):
    axial, r_loc, theta, c = features.shape
    rows = r_loc * theta
    hid_loc = w_in.shape[0]
    a_loc = axial // n
    spread = hid_loc == SLOT
    params = pltpu.CompilerParams(vmem_limit_bytes=48 * 1024 * 1024)

    def move(piece, digit, by=1):
        return lax.ppermute(piece, "row", shifted(n, digit, by))

    outer, inner, _ = digits(n)
    anywhere = pl.BlockSpec(memory_space=pl.ANY)
    vectors = [v[None, :] for v in (conv_bias, ln_gain, ln_bias, b_out, layer_scale)]
    slot_shape = (2 * SLOT + EXTRA, c)
    if spread:
        own, axial_taps, consts = pl.pallas_call(
            pack_kernel,
            out_shape=[
                jax.ShapeDtypeStruct((1,) + slot_shape, jnp.bfloat16),
                jax.ShapeDtypeStruct(axial_taps.shape, jnp.float32),
                jax.ShapeDtypeStruct((8, c), jnp.float32),
            ],
            in_specs=[vmem()] + [anywhere] * 8,
            out_specs=[vmem()] * 3,
            scratch_shapes=[pltpu.VMEM((5, 1, c), jnp.float32), pltpu.SemaphoreType.DMA((8,))],
            name="pack",
        )(b_in, w_in, w_out, axial_taps, *vectors)
        line = [move(own, 0, by) for by in range(1, outer)]
        side = [move(own, 1, by) for by in range(1, inner)]
    else:
        consts = jnp.concatenate(vectors + [jnp.zeros((3, c), jnp.float32)], axis=0)
        w_all = lax.all_gather(w_in, "row", axis=0, tiled=True).reshape(-1, SLOT, c)
        o_all = lax.all_gather(w_out, "row", axis=0, tiled=True).reshape(-1, SLOT, c)
        b_all = lax.all_gather(b_in, "row", axis=0, tiled=True).reshape(-1, 1, SLOT)
        b_all = jnp.broadcast_to(jnp.tile(b_all, (1, 1, c // SLOT)), (w_all.shape[0], EXTRA, c))
        slots = [jnp.concatenate([w_all, o_all, b_all], axis=1)]

    got = lax.all_to_all(features, "row", split_axis=0, concat_axis=0, tiled=True)
    pad = (radial_taps.shape[0] + 1) // 4
    mixed = pl.pallas_call(
        radial_kernel,
        out_shape=jax.ShapeDtypeStruct((n, a_loc, rows, c), jnp.bfloat16),
        in_specs=[vmem()] * 2,
        out_specs=vmem(),
        scratch_shapes=[pltpu.VMEM((n + 2 * pad, a_loc, rows, c), jnp.float32)] * 2,
        compiler_params=params,
        name="radial",
    )(got.reshape(n, a_loc, r_loc, theta, c), radial_taps)
    if spread:
        line = [lax.optimization_barrier((h, mixed))[0] for h in line]
        across = side + [move(h, 1, by) for by in range(1, inner) for h in line]
        twin = [move(h, 2) for h in [own] + line]
    back = lax.all_to_all(mixed.reshape(axial, rows, c), "row", split_axis=0, concat_axis=0, tiled=True)
    if spread:
        across, back = lax.optimization_barrier((across, back))
        slots = [own] + line + across + twin + [move(h, 2) for h in across]
    normed = pl.pallas_call(
        axial_kernel,
        out_shape=jax.ShapeDtypeStruct((axial * rows, c), jnp.bfloat16),
        in_specs=[vmem()] * 3,
        out_specs=vmem(),
        scratch_shapes=[
            pltpu.VMEM((axial + axial_taps.shape[0] - 1, rows, c), jnp.float32),
            pltpu.VMEM((axial, rows, c), jnp.float32),
        ],
        compiler_params=params,
        name="axial",
    )(back, axial_taps, consts)
    count = sum(h.shape[0] for h in slots)
    return pl.pallas_call(
        mlp_kernel,
        out_shape=jax.ShapeDtypeStruct(features.shape, jnp.bfloat16),
        in_specs=[vmem()] * 3 + [anywhere] * len(slots),
        out_specs=vmem(),
        scratch_shapes=[
            pltpu.VMEM((count,) + slot_shape, jnp.bfloat16),
            pltpu.VMEM((axial, rows, c), jnp.float32),
            pltpu.SemaphoreType.DMA((len(slots),)),
        ],
        compiler_params=params,
        name="mlp",
    )(normed, features, consts, *slots)


def solution(mesh):
    in_specs = (
        P("groups", "row", None, None),
        P(),
        P(),
        P(),
        P(),
        P(),
        P("row", None),
        P("row"),
        P("row", None),
        P(),
        P(),
    )
    out_specs = P("groups", "row", None, None)
    return jax.shard_map(partial(local, mesh.shape["row"]), mesh=mesh, in_specs=in_specs, out_specs=out_specs, check_vma=False)
```

```python
from functools import partial

import jax
import jax.numpy as jnp
from jax import lax
from jax.experimental import pallas as pl
from jax.experimental.pallas import tpu as pltpu
from jax.sharding import PartitionSpec as P

SLOT = 32
EXTRA = 16


def vmem():
    return pl.BlockSpec(memory_space=pltpu.VMEM)


def pack_kernel(b_ref, w_in_ref, w_out_ref, slot_ref, sems):
    half = lax.axis_index("groups")
    at = pl.multiple_of(half * SLOT, SLOT)
    copies = [
        pltpu.make_async_copy(w_in_ref.at[pl.ds(at, SLOT)], slot_ref.at[0, 0:SLOT], sems.at[0]),
        pltpu.make_async_copy(w_out_ref.at[pl.ds(at, SLOT)], slot_ref.at[0, SLOT : 2 * SLOT], sems.at[1]),
    ]
    for copy in copies:
        copy.start()
    bias = b_ref[...].astype(jnp.float32)[None, :]
    c = slot_ref.shape[2]
    low, high = bias[:, :SLOT], bias[:, SLOT:]
    wide = jnp.where(half == 0, jnp.concatenate([low] * (c // SLOT), axis=1), jnp.concatenate([high] * (c // SLOT), axis=1))
    slot_ref[0, 2 * SLOT : 2 * SLOT + EXTRA, :] = jnp.broadcast_to(wide, (EXTRA, c)).astype(slot_ref.dtype)
    for copy in copies:
        copy.wait()


def stage_kernel(order_ref, taps_ref, *rest):
    vectors = rest[:5]
    taps_out, consts_out, staged, sems = rest[5:]
    copies = [pltpu.make_async_copy(taps_ref, taps_out, sems.at[5])]
    for i, vector in enumerate(vectors):
        copies.append(pltpu.make_async_copy(vector, staged.at[i], sems.at[i]))
    for copy in copies:
        copy.start()
    for copy in copies:
        copy.wait()
    for i in range(5):
        consts_out[i : i + 1, :] = staged[i]


def radial_kernel(pieces, x_ref, taps_ref, *rest):
    out_ref = rest[pieces]
    copies = []
    if pieces:
        joined_ref, even, odd, sems = rest[pieces + 1 :]
        copies = [pltpu.make_async_copy(rest[i], joined_ref.at[i : i + 1], sems.at[i]) for i in range(pieces)]
    else:
        even, odd = rest[1:]
    for copy in copies:
        copy.start()
    n, a_loc, _, theta, c = x_ref.shape
    taps = taps_ref.shape[0]
    pad = (taps + 1) // 4
    zeros = jnp.zeros((pad, a_loc, 2 * theta, c), jnp.float32)
    even[0:pad] = zeros
    even[pad + n : 2 * pad + n] = zeros
    odd[0:pad] = zeros
    odd[pad + n - 1 : 2 * pad + n - 1] = zeros
    odd[2 * pad + n - 1 :] = zeros[:1]
    first = x_ref[:, :, 0].astype(jnp.float32)
    second = x_ref[:, :, 1].astype(jnp.float32)
    even[pad : pad + n, :, 0:theta] = first
    even[pad : pad + n, :, theta:] = second
    odd[pad : pad + n, :, 0:theta] = second
    odd[pad - 1 : pad + n - 1, :, theta:] = first

    def step(s, carry):
        total = jnp.zeros((a_loc, 2 * theta, c), jnp.float32)
        for k in range(taps):
            shift = k - taps // 2
            source = even if shift % 2 == 0 else odd
            total = total + source[s + (pad + shift // 2)] * taps_ref[k : k + 1, :]
        out_ref[s] = total.astype(out_ref.dtype)
        return carry

    lax.fori_loop(0, n, step, 0)
    for copy in copies:
        copy.wait()


def axial_kernel(z_ref, taps_ref, consts_ref, out_ref, padded, summed):
    axial, rows, c = z_ref.shape
    taps = taps_ref.shape[0]
    half = taps // 2
    zeros = jnp.zeros((half, rows, c), jnp.float32)
    padded[0:half] = zeros
    padded[half + axial :] = zeros
    padded[half : half + axial] = z_ref[...].astype(jnp.float32)
    block = 4

    def conv(i, carry):
        base = i * block
        total = jnp.zeros((block, rows, c), jnp.float32)
        for k in range(taps):
            total = total + padded[pl.ds(base + k, block)] * taps_ref[k : k + 1, :]
        summed[pl.ds(base, block)] = total
        return carry

    lax.fori_loop(0, axial // block, conv, 0)

    def norm(i, carry):
        v = (summed[pl.ds(i * 32, 32)] + consts_ref[0:1, :]).reshape(32 * rows, c)
        v = v.astype(jnp.bfloat16).astype(jnp.float32)
        mean = jnp.mean(v, axis=-1, keepdims=True)
        centred = v - mean
        var = jnp.mean(centred * centred, axis=-1, keepdims=True)
        normed = centred * lax.rsqrt(var + 1e-06) * consts_ref[1:2, :] + consts_ref[2:3, :]
        at = pl.multiple_of(i * 32 * rows, 32 * rows)
        out_ref[pl.ds(at, 32 * rows), :] = normed.astype(out_ref.dtype)
        return carry

    lax.fori_loop(0, axial // 32, norm, 0)


def mlp_kernel(normed_ref, feat_ref, consts_ref, *rest):
    *w_refs, out_ref, slots, branch, sems = rest
    axial, _, theta, c = feat_ref.shape
    rows = 2 * theta
    per = c // SLOT
    lane_slot = lax.broadcasted_iota(jnp.int32, (1, c), 1) // SLOT
    token_block = 32 * rows
    copies, at = [], 0
    for i, w_ref in enumerate(w_refs):
        copies.append(pltpu.make_async_copy(w_ref, slots.at[at : at + w_ref.shape[0]], sems.at[i]))
        at += w_ref.shape[0]
    for copy in copies:
        copy.start()
    for copy in copies:
        copy.wait()

    def mlp(i, carry):
        base = pl.multiple_of(i * token_block, token_block)
        normed = normed_ref[pl.ds(base, token_block), :]
        total = jnp.zeros((token_block, c), jnp.float32)
        for g in range(slots.shape[0] // per):
            own = slice(g * per, (g + 1) * per)
            w_in = slots[own, 0:SLOT, :].reshape(per * SLOT, c)
            w_out = slots[own, SLOT : 2 * SLOT, :].reshape(per * SLOT, c)
            bias = jnp.zeros((1, c), jnp.float32)
            for j in range(per):
                piece = slots[g * per + j, 2 * SLOT : 2 * SLOT + EXTRA, :].astype(jnp.float32)[0:1]
                bias = jnp.where(lane_slot == j, piece, bias)
            u = lax.dot_general(normed, w_in, (((1,), (1,)), ((), ())), preferred_element_type=jnp.float32)
            u = u + bias
            hidden = (0.5 * u * (1.0 + jnp.tanh(0.7978845608028654 * (u + 0.044715 * u * u * u)))).astype(jnp.bfloat16)
            total = total + jnp.dot(hidden, w_out, preferred_element_type=jnp.float32)
        result = (consts_ref[4:5, :] * (total + consts_ref[3:4, :])).astype(jnp.bfloat16).astype(jnp.float32)
        branch[pl.ds(i * 32, 32)] = result.reshape(32, rows, c)
        return carry

    if axial == 32:
        mlp(0, 0)
    else:
        lax.fori_loop(0, axial // 32, mlp, 0)
    for r in range(2):
        got = branch[:, r * theta : (r + 1) * theta, :]
        out_ref[:, r] = (feat_ref[:, r].astype(jnp.float32) + got).astype(out_ref.dtype)


def digits(n):
    chips = n // 2
    inner = 1
    while inner * inner * 4 <= chips:
        inner *= 2
    return chips // inner, inner, 2


def shifted(n, digit, by):
    sizes = digits(n)
    stride = [sizes[1] * sizes[2], sizes[2], 1][digit]
    targets = []
    for i in range(n):
        at = (i // stride) % sizes[digit]
        targets.append(i + ((at + by) % sizes[digit] - at) * stride)
    return targets


def local(parts, n, features, axial_taps, radial_taps, conv_bias, ln_gain, ln_bias, w_in, b_in, w_out, b_out, layer_scale):
    axial, r_loc, theta, c = features.shape
    rows = r_loc * theta
    hid_loc = w_in.shape[0]
    a_loc = axial // n
    outer, inner, _ = digits(n)
    spread = hid_loc == parts * SLOT and parts == 2 and inner == 2
    params = pltpu.CompilerParams(vmem_limit_bytes=48 * 1024 * 1024)
    anywhere = pl.BlockSpec(memory_space=pl.ANY)

    def move(piece, digit, by, swap=False):
        targets = shifted(n, digit, by)
        if not swap:
            return lax.ppermute(piece, "row", list(enumerate(targets)))
        pairs = [(g * n + i, (1 - g) * n + t) for g in range(2) for i, t in enumerate(targets)]
        return lax.ppermute(piece, ("groups", "row"), pairs)

    slot_shape = (2 * SLOT + EXTRA, c)
    line = []
    if spread:
        own = pl.pallas_call(
            pack_kernel,
            out_shape=jax.ShapeDtypeStruct((1,) + slot_shape, jnp.bfloat16),
            in_specs=[vmem()] + [anywhere] * 2,
            out_specs=vmem(),
            scratch_shapes=[pltpu.SemaphoreType.DMA((2,))],
            name="pack",
        )(b_in, w_in, w_out)
        line = [own] + [move(own, 0, by) for by in range(1, outer)]
    else:
        w_all = lax.all_gather(w_in, "row", axis=0, tiled=True).reshape(-1, SLOT, c)
        o_all = lax.all_gather(w_out, "row", axis=0, tiled=True).reshape(-1, SLOT, c)
        b_all = lax.all_gather(b_in, "row", axis=0, tiled=True).reshape(-1, 1, SLOT)
        b_all = jnp.broadcast_to(jnp.tile(b_all, (1, 1, c // SLOT)), (w_all.shape[0], EXTRA, c))
        slots = [jnp.concatenate([w_all, o_all, b_all], axis=1)]

    got = lax.all_to_all(features, "row", split_axis=0, concat_axis=0, tiled=True)
    pad = (radial_taps.shape[0] + 1) // 4
    pieces = len(line)
    out_shape = [jax.ShapeDtypeStruct((n, a_loc, rows, c), jnp.bfloat16)]
    scratch = [pltpu.VMEM((n + 2 * pad, a_loc, rows, c), jnp.float32)] * 2
    if spread:
        out_shape.append(jax.ShapeDtypeStruct((pieces,) + slot_shape, jnp.bfloat16))
        scratch.append(pltpu.SemaphoreType.DMA((pieces,)))
    mixed, *joined = pl.pallas_call(
        partial(radial_kernel, pieces),
        out_shape=out_shape,
        in_specs=[vmem()] * 2 + [anywhere] * pieces,
        out_specs=[vmem()] * len(out_shape),
        scratch_shapes=scratch,
        compiler_params=params,
        name="radial",
    )(got.reshape(n, a_loc, r_loc, theta, c), radial_taps, *line)
    back = lax.all_to_all(mixed.reshape(axial, rows, c), "row", split_axis=0, concat_axis=0, tiled=True)
    vectors = [v[None, :] for v in (conv_bias, ln_gain, ln_bias, b_out, layer_scale)]
    axial_taps, consts = pl.pallas_call(
        stage_kernel,
        out_shape=[jax.ShapeDtypeStruct(axial_taps.shape, jnp.float32), jax.ShapeDtypeStruct((8, c), jnp.float32)],
        in_specs=[anywhere] * 7,
        out_specs=[vmem()] * 2,
        scratch_shapes=[pltpu.VMEM((5, 1, c), jnp.float32), pltpu.SemaphoreType.DMA((6,))],
        name="stage",
    )(mixed, axial_taps, *vectors)
    if spread:
        (block,) = joined
        others = [move(block, 1, 0, swap=True), move(block, 1, 1), move(block, 1, 1, swap=True)]
        twin = [move(block, 2, 1)]
        others, back, axial_taps, consts = lax.optimization_barrier((others, back, axial_taps, consts))
        slots = [block] + others + twin + [move(h, 2, 1) for h in others]
    normed = pl.pallas_call(
        axial_kernel,
        out_shape=jax.ShapeDtypeStruct((axial * rows, c), jnp.bfloat16),
        in_specs=[vmem()] * 3,
        out_specs=vmem(),
        scratch_shapes=[
            pltpu.VMEM((axial + axial_taps.shape[0] - 1, rows, c), jnp.float32),
            pltpu.VMEM((axial, rows, c), jnp.float32),
        ],
        compiler_params=params,
        name="axial",
    )(back, axial_taps, consts)
    count = sum(h.shape[0] for h in slots)
    return pl.pallas_call(
        mlp_kernel,
        out_shape=jax.ShapeDtypeStruct(features.shape, jnp.bfloat16),
        in_specs=[vmem()] * 3 + [anywhere] * len(slots),
        out_specs=vmem(),
        scratch_shapes=[
            pltpu.VMEM((count,) + slot_shape, jnp.bfloat16),
            pltpu.VMEM((axial, rows, c), jnp.float32),
            pltpu.SemaphoreType.DMA((len(slots),)),
        ],
        compiler_params=params,
        name="mlp",
    )(normed, features, consts, *slots)


def solution(mesh):
    in_specs = (
        P("groups", "row", None, None),
        P(),
        P(),
        P(),
        P(),
        P(),
        P("row", None),
        P("row"),
        P("row", None),
        P(),
        P(),
    )
    out_specs = P("groups", "row", None, None)
    return jax.shard_map(partial(local, mesh.shape["groups"], mesh.shape["row"]), mesh=mesh, in_specs=in_specs, out_specs=out_specs, check_vma=False)
```

```python
from functools import partial

import jax
import jax.numpy as jnp
from jax import lax
from jax.experimental import pallas as pl
from jax.experimental.pallas import tpu as pltpu
from jax.sharding import PartitionSpec as P

SLOT = 64
EXTRA = 16


def vmem():
    return pl.BlockSpec(memory_space=pltpu.VMEM)


def pack_kernel(b_ref, w_in_ref, w_out_ref, taps_ref, *rest):
    vectors = rest[:5]
    slot_ref, taps_out, consts_out, staged, sems = rest[5:]
    copies = [
        pltpu.make_async_copy(w_in_ref, slot_ref.at[0, 0:SLOT], sems.at[0]),
        pltpu.make_async_copy(w_out_ref, slot_ref.at[0, SLOT : 2 * SLOT], sems.at[1]),
        pltpu.make_async_copy(taps_ref, taps_out, sems.at[2]),
    ]
    for i, vector in enumerate(vectors):
        copies.append(pltpu.make_async_copy(vector, staged.at[i], sems.at[3 + i]))
    for copy in copies:
        copy.start()
    bias = b_ref[...].astype(jnp.float32)[None, :]
    c = slot_ref.shape[2]
    wide = jnp.concatenate([bias] * (c // SLOT), axis=1)
    slot_ref[0, 2 * SLOT : 2 * SLOT + EXTRA, :] = jnp.broadcast_to(wide, (EXTRA, c)).astype(slot_ref.dtype)
    for copy in copies:
        copy.wait()
    for i in range(5):
        consts_out[i : i + 1, :] = staged[i]


def radial_kernel(x_ref, taps_ref, out_ref, even, odd):
    n, a_loc, _, theta, c = x_ref.shape
    taps = taps_ref.shape[0]
    pad = (taps + 1) // 4
    zeros = jnp.zeros((pad, a_loc, 2 * theta, c), jnp.float32)
    even[0:pad] = zeros
    even[pad + n : 2 * pad + n] = zeros
    odd[0:pad] = zeros
    odd[pad + n - 1 : 2 * pad + n - 1] = zeros
    odd[2 * pad + n - 1 :] = zeros[:1]
    first = x_ref[:, :, 0].astype(jnp.float32)
    second = x_ref[:, :, 1].astype(jnp.float32)
    even[pad : pad + n, :, 0:theta] = first
    even[pad : pad + n, :, theta:] = second
    odd[pad : pad + n, :, 0:theta] = second
    odd[pad - 1 : pad + n - 1, :, theta:] = first

    def step(s, carry):
        total = jnp.zeros((a_loc, 2 * theta, c), jnp.float32)
        for k in range(taps):
            shift = k - taps // 2
            source = even if shift % 2 == 0 else odd
            total = total + source[s + (pad + shift // 2)] * taps_ref[k : k + 1, :]
        out_ref[s] = total.astype(out_ref.dtype)
        return carry

    lax.fori_loop(0, n, step, 0)


def tail_kernel(z_ref, feat_ref, taps_ref, consts_ref, w_ref, out_ref, padded, branch, slots, sem):
    fetch = pltpu.make_async_copy(w_ref, slots, sem)
    fetch.start()
    axial, rows, c = z_ref.shape
    theta = rows // 2
    taps = taps_ref.shape[0]
    half = taps // 2
    zeros = jnp.zeros((half, rows, c), jnp.float32)
    padded[0:half] = zeros
    padded[half + axial :] = zeros
    padded[half : half + axial] = z_ref[...].astype(jnp.float32)
    block = 4

    def conv(i, carry):
        base = i * block
        total = jnp.zeros((block, rows, c), jnp.float32)
        for k in range(taps):
            total = total + padded[pl.ds(base + k, block)] * taps_ref[k : k + 1, :]
        branch[pl.ds(base, block)] = total
        return carry

    lax.fori_loop(0, axial // block, conv, 0)
    fetch.wait()
    per = c // SLOT
    lane_slot = lax.broadcasted_iota(jnp.int32, (1, c), 1) // SLOT
    planes = 32

    def mlp(i, carry):
        v = (branch[pl.ds(i * planes, planes)] + consts_ref[0:1, :]).reshape(planes * rows, c)
        v = v.astype(jnp.bfloat16).astype(jnp.float32)
        mean = jnp.mean(v, axis=-1, keepdims=True)
        centred = v - mean
        var = jnp.mean(centred * centred, axis=-1, keepdims=True)
        normed = (centred * lax.rsqrt(var + 1e-06) * consts_ref[1:2, :] + consts_ref[2:3, :]).astype(jnp.bfloat16)
        total = jnp.zeros((planes * rows, c), jnp.float32)
        for g in range(slots.shape[0] // per):
            own = slice(g * per, (g + 1) * per)
            w_in = slots[own, 0:SLOT, :].reshape(per * SLOT, c)
            w_out = slots[own, SLOT : 2 * SLOT, :].reshape(per * SLOT, c)
            bias = jnp.zeros((1, c), jnp.float32)
            for j in range(per):
                piece = slots[g * per + j, 2 * SLOT : 2 * SLOT + EXTRA, :].astype(jnp.float32)[0:1]
                bias = jnp.where(lane_slot == j, piece, bias)
            u = lax.dot_general(normed, w_in, (((1,), (1,)), ((), ())), preferred_element_type=jnp.float32)
            u = u + bias
            hidden = (0.5 * u * (1.0 + jnp.tanh(0.7978845608028654 * (u + 0.044715 * u * u * u)))).astype(jnp.bfloat16)
            total = total + jnp.dot(hidden, w_out, preferred_element_type=jnp.float32)
        result = (consts_ref[4:5, :] * (total + consts_ref[3:4, :])).astype(jnp.bfloat16).astype(jnp.float32)
        branch[pl.ds(i * planes, planes)] = result.reshape(planes, rows, c)
        return carry

    if axial == planes:
        mlp(0, 0)
    else:
        lax.fori_loop(0, axial // planes, mlp, 0)
    for r in range(2):
        got = branch[:, r * theta : (r + 1) * theta, :]
        out_ref[:, r] = (feat_ref[:, r].astype(jnp.float32) + got).astype(out_ref.dtype)


def local(n, features, axial_taps, radial_taps, conv_bias, ln_gain, ln_bias, w_in, b_in, w_out, b_out, layer_scale):
    axial, r_loc, theta, c = features.shape
    rows = r_loc * theta
    hid_loc = w_in.shape[0]
    a_loc = axial // n
    spread = hid_loc == SLOT
    params = pltpu.CompilerParams(vmem_limit_bytes=48 * 1024 * 1024)

    anywhere = pl.BlockSpec(memory_space=pl.ANY)
    vectors = [v[None, :] for v in (conv_bias, ln_gain, ln_bias, b_out, layer_scale)]
    slot_shape = (2 * SLOT + EXTRA, c)
    if spread:
        own, axial_taps, consts = pl.pallas_call(
            pack_kernel,
            out_shape=[
                jax.ShapeDtypeStruct((1,) + slot_shape, jnp.bfloat16),
                jax.ShapeDtypeStruct(axial_taps.shape, jnp.float32),
                jax.ShapeDtypeStruct((8, c), jnp.float32),
            ],
            in_specs=[vmem()] + [anywhere] * 8,
            out_specs=[vmem()] * 3,
            scratch_shapes=[pltpu.VMEM((5, 1, c), jnp.float32), pltpu.SemaphoreType.DMA((8,))],
            name="pack",
        )(b_in, w_in, w_out, axial_taps, *vectors)
        slots = lax.all_gather(own, "row", axis=0, tiled=True)
    else:
        consts = jnp.concatenate(vectors + [jnp.zeros((3, c), jnp.float32)], axis=0)
        w_all = lax.all_gather(w_in, "row", axis=0, tiled=True).reshape(-1, SLOT, c)
        o_all = lax.all_gather(w_out, "row", axis=0, tiled=True).reshape(-1, SLOT, c)
        b_all = lax.all_gather(b_in, "row", axis=0, tiled=True).reshape(-1, 1, SLOT)
        b_all = jnp.broadcast_to(jnp.tile(b_all, (1, 1, c // SLOT)), (w_all.shape[0], EXTRA, c))
        slots = jnp.concatenate([w_all, o_all, b_all], axis=1)

    got = lax.all_to_all(features, "row", split_axis=0, concat_axis=0, tiled=True)
    pad = (radial_taps.shape[0] + 1) // 4
    mixed = pl.pallas_call(
        radial_kernel,
        out_shape=jax.ShapeDtypeStruct((n, a_loc, rows, c), jnp.bfloat16),
        in_specs=[vmem()] * 2,
        out_specs=vmem(),
        scratch_shapes=[pltpu.VMEM((n + 2 * pad, a_loc, rows, c), jnp.float32)] * 2,
        compiler_params=params,
        name="radial",
    )(got.reshape(n, a_loc, r_loc, theta, c), radial_taps)
    back = lax.all_to_all(mixed.reshape(axial, rows, c), "row", split_axis=0, concat_axis=0, tiled=True)
    return pl.pallas_call(
        tail_kernel,
        out_shape=jax.ShapeDtypeStruct(features.shape, jnp.bfloat16),
        in_specs=[vmem()] * 4 + [anywhere],
        out_specs=vmem(),
        scratch_shapes=[
            pltpu.VMEM((axial + axial_taps.shape[0] - 1, rows, c), jnp.float32),
            pltpu.VMEM((axial, rows, c), jnp.float32),
            pltpu.VMEM(slots.shape, jnp.bfloat16),
            pltpu.SemaphoreType.DMA(()),
        ],
        compiler_params=params,
        name="tail",
    )(back, features, axial_taps, consts, slots)


def solution(mesh):
    in_specs = (
        P("groups", "row", None, None),
        P(),
        P(),
        P(),
        P(),
        P(),
        P("row", None),
        P("row"),
        P("row", None),
        P(),
        P(),
    )
    out_specs = P("groups", "row", None, None)
    return jax.shard_map(partial(local, mesh.shape["row"]), mesh=mesh, in_specs=in_specs, out_specs=out_specs, check_vma=False)
```

```python
import math
from functools import partial

import jax
import jax.numpy as jnp
from jax import lax
from jax.experimental import pallas as pl
from jax.experimental.pallas import tpu as pltpu
from jax.sharding import PartitionSpec as P

SLOT = 64
EXTRA = 16


def vmem():
    return pl.BlockSpec(memory_space=pltpu.VMEM)


def pack_kernel(b_ref, w_in_ref, w_out_ref, slot_ref, sems):
    copies = [
        pltpu.make_async_copy(w_in_ref, slot_ref.at[0, 0:SLOT], sems.at[0]),
        pltpu.make_async_copy(w_out_ref, slot_ref.at[0, SLOT : 2 * SLOT], sems.at[1]),
    ]
    for copy in copies:
        copy.start()
    bias = b_ref[...].astype(jnp.float32)[None, :]
    c = slot_ref.shape[2]
    wide = jnp.concatenate([bias] * (c // SLOT), axis=1)
    slot_ref[0, 2 * SLOT : 2 * SLOT + EXTRA, :] = jnp.broadcast_to(wide, (EXTRA, c)).astype(slot_ref.dtype)
    for copy in copies:
        copy.wait()


def gate_kernel(*refs):
    refs[-1][...] = jnp.zeros_like(refs[-1])


def radial_kernel(x_ref, taps_ref, out_ref, even, odd):
    n, a_loc, _, theta, c = x_ref.shape
    taps = taps_ref.shape[0]
    pad = (taps + 1) // 4
    zeros = jnp.zeros((pad, a_loc, 2 * theta, c), jnp.float32)
    even[0:pad] = zeros
    even[pad + n : 2 * pad + n] = zeros
    odd[0:pad] = zeros
    odd[pad + n - 1 : 2 * pad + n - 1] = zeros
    odd[2 * pad + n - 1 :] = zeros[:1]
    first = x_ref[:, :, 0].astype(jnp.float32)
    second = x_ref[:, :, 1].astype(jnp.float32)
    even[pad : pad + n, :, 0:theta] = first
    even[pad : pad + n, :, theta:] = second
    odd[pad : pad + n, :, 0:theta] = second
    odd[pad - 1 : pad + n - 1, :, theta:] = first

    def step(s, carry):
        total = jnp.zeros((a_loc, 2 * theta, c), jnp.float32)
        for k in range(taps):
            shift = k - taps // 2
            source = even if shift % 2 == 0 else odd
            total = total + source[s + (pad + shift // 2)] * taps_ref[k : k + 1, :]
        out_ref[s] = total.astype(out_ref.dtype)
        return carry

    lax.fori_loop(0, n, step, 0)


def tail_kernel(n_slots, z_ref, taps_ref, feat_ref, *rest):
    vectors, w_refs = rest[:5], rest[5 : 5 + n_slots]
    out_ref, padded, branch, field, consts, sems = rest[-6:]
    fetches = [pltpu.make_async_copy(feat_ref, field, sems.at[5])]
    for i, vector in enumerate(vectors):
        fetches.append(pltpu.make_async_copy(vector, consts.at[i], sems.at[i]))
    for fetch in fetches:
        fetch.start()
    axial, rows, c = z_ref.shape
    theta = rows // 2
    taps = taps_ref.shape[0]
    half = taps // 2
    zeros = jnp.zeros((half, rows, c), jnp.float32)
    padded[0:half] = zeros
    padded[half + axial :] = zeros
    padded[half : half + axial] = z_ref[...].astype(jnp.float32)
    block = 4

    def conv(i, carry):
        base = i * block
        total = jnp.zeros((block, rows, c), jnp.float32)
        for k in range(taps):
            total = total + padded[pl.ds(base + k, block)] * taps_ref[k : k + 1, :]
        branch[pl.ds(base, block)] = total
        return carry

    lax.fori_loop(0, axial // block, conv, 0)
    for fetch in fetches:
        fetch.wait()
    slots = [(w_ref, i) for w_ref in w_refs for i in range(w_ref.shape[0])]
    per = c // SLOT
    lane_slot = lax.broadcasted_iota(jnp.int32, (1, c), 1) // SLOT
    planes = 32

    def mlp(i, carry):
        v = (branch[pl.ds(i * planes, planes)] + consts[0]).reshape(planes * rows, c)
        v = v.astype(jnp.bfloat16).astype(jnp.float32)
        mean = jnp.mean(v, axis=-1, keepdims=True)
        centred = v - mean
        var = jnp.mean(centred * centred, axis=-1, keepdims=True)
        normed = (centred * lax.rsqrt(var + 1e-06) * consts[1] + consts[2]).astype(jnp.bfloat16)
        total = jnp.zeros((planes * rows, c), jnp.float32)
        for g in range(len(slots) // per):
            own = slots[g * per : (g + 1) * per]
            w_in = jnp.concatenate([w[j, 0:SLOT, :] for w, j in own], axis=0)
            w_out = jnp.concatenate([w[j, SLOT : 2 * SLOT, :] for w, j in own], axis=0)
            bias = jnp.zeros((1, c), jnp.float32)
            for at, (w, j) in enumerate(own):
                piece = w[j, 2 * SLOT : 2 * SLOT + EXTRA, :].astype(jnp.float32)[0:1]
                bias = jnp.where(lane_slot == at, piece, bias)
            u = lax.dot_general(normed, w_in, (((1,), (1,)), ((), ())), preferred_element_type=jnp.float32)
            u = u + bias
            hidden = (0.5 * u * (1.0 + jnp.tanh(0.7978845608028654 * (u + 0.044715 * u * u * u)))).astype(jnp.bfloat16)
            total = total + jnp.dot(hidden, w_out, preferred_element_type=jnp.float32)
        result = (consts[4] * (total + consts[3])).astype(jnp.bfloat16).astype(jnp.float32)
        branch[pl.ds(i * planes, planes)] = result.reshape(planes, rows, c)
        return carry

    if axial == planes:
        mlp(0, 0)
    else:
        lax.fori_loop(0, axial // planes, mlp, 0)
    for r in range(2):
        got = branch[:, r * theta : (r + 1) * theta, :]
        out_ref[:, r] = (field[:, r].astype(jnp.float32) + got).astype(out_ref.dtype)


def digits(n):
    chips = n // 2
    inner = 1
    while inner * inner * 4 <= chips:
        inner *= 2
    return chips // inner, inner, 2


def local(n, features, axial_taps, radial_taps, conv_bias, ln_gain, ln_bias, w_in, b_in, w_out, b_out, layer_scale):
    axial, r_loc, theta, c = features.shape
    rows = r_loc * theta
    hid_loc = w_in.shape[0]
    a_loc = axial // n
    outer, inner, _ = digits(n)
    spread = hid_loc == SLOT and n == 4 * outer
    params = pltpu.CompilerParams(vmem_limit_bytes=24 * 1024 * 1024)
    anywhere = pl.BlockSpec(memory_space=pl.ANY)

    def move(piece, digit, by):
        stride = math.prod(digits(n)[digit + 1 :])
        return lax.ppermute(piece, "row", [(i, i ^ (by * stride)) for i in range(n)])

    if spread:
        own = pl.pallas_call(
            pack_kernel,
            out_shape=jax.ShapeDtypeStruct((1, 2 * SLOT + EXTRA, c), jnp.bfloat16),
            in_specs=[vmem()] + [anywhere] * 2,
            out_specs=vmem(),
            scratch_shapes=[pltpu.SemaphoreType.DMA((2,))],
            name="pack",
        )(b_in, w_in, w_out)
        line = [move(own, 0, by) for by in range(1, outer)]
        across = [move(own, 1, 1)]
        twin = [move(own, 2, 1)]
    else:
        w_all = lax.all_gather(w_in, "row", axis=0, tiled=True).reshape(-1, SLOT, c)
        o_all = lax.all_gather(w_out, "row", axis=0, tiled=True).reshape(-1, SLOT, c)
        b_all = lax.all_gather(b_in, "row", axis=0, tiled=True).reshape(-1, 1, SLOT)
        b_all = jnp.broadcast_to(jnp.tile(b_all, (1, 1, c // SLOT)), (w_all.shape[0], EXTRA, c))
        slots, order = [jnp.concatenate([w_all, o_all, b_all], axis=1)], []

    got = lax.all_to_all(features, "row", split_axis=0, concat_axis=0, tiled=True)
    pad = (radial_taps.shape[0] + 1) // 4
    mixed = pl.pallas_call(
        radial_kernel,
        out_shape=jax.ShapeDtypeStruct((n, a_loc, rows, c), jnp.bfloat16),
        in_specs=[vmem()] * 2,
        out_specs=vmem(),
        scratch_shapes=[pltpu.VMEM((n + 2 * pad, a_loc, rows, c), jnp.float32)] * 2,
        compiler_params=params,
        name="radial",
    )(got.reshape(n, a_loc, r_loc, theta, c), radial_taps)
    if spread:
        gate = pl.pallas_call(
            gate_kernel,
            out_shape=jax.ShapeDtypeStruct((8, 128), jnp.float32),
            in_specs=[anywhere] * outer,
            out_specs=vmem(),
            cost_estimate=pl.CostEstimate(flops=10**10, bytes_accessed=2 * 10**7, transcendentals=0),
            name="gate",
        )(mixed, *line)
        line, *order = lax.optimization_barrier((line, gate))
        across = across + [move(h, 1, 1) for h in line]
        twin = twin + [move(h, 2, 1) for h in line]
    back = lax.all_to_all(mixed.reshape(axial, rows, c), "row", split_axis=0, concat_axis=0, tiled=True)
    if spread:
        across, back = lax.optimization_barrier((across, back))
        slots = [own] + line + across + twin + [move(h, 2, 1) for h in across]
    vectors = [v[None, :] for v in (conv_bias, ln_gain, ln_bias, b_out, layer_scale)]
    return pl.pallas_call(
        partial(tail_kernel, len(slots)),
        out_shape=jax.ShapeDtypeStruct(features.shape, jnp.bfloat16),
        in_specs=[vmem()] * 2 + [anywhere] * 6 + [vmem()] * len(slots) + [anywhere] * len(order),
        out_specs=vmem(),
        scratch_shapes=[
            pltpu.VMEM((axial + axial_taps.shape[0] - 1, rows, c), jnp.float32),
            pltpu.VMEM((axial, rows, c), jnp.float32),
            pltpu.VMEM(features.shape, jnp.bfloat16),
            pltpu.VMEM((5, 1, c), jnp.float32),
            pltpu.SemaphoreType.DMA((6,)),
        ],
        compiler_params=params,
        name="tail",
    )(back, axial_taps, features, *vectors, *slots, *order)


def solution(mesh):
    in_specs = (
        P("groups", "row", None, None),
        P(),
        P(),
        P(),
        P(),
        P(),
        P("row", None),
        P("row"),
        P("row", None),
        P(),
        P(),
    )
    out_specs = P("groups", "row", None, None)
    return jax.shard_map(partial(local, mesh.shape["row"]), mesh=mesh, in_specs=in_specs, out_specs=out_specs, check_vma=False)
```

```python
import math
from functools import partial

import jax
import jax.numpy as jnp
from jax import lax
from jax.experimental import pallas as pl
from jax.experimental.pallas import tpu as pltpu
from jax.sharding import PartitionSpec as P

SLOT = 64
EXTRA = 16


def vmem():
    return pl.BlockSpec(memory_space=pltpu.VMEM)


def pack_kernel(b_ref, w_in_ref, w_out_ref, slot_ref, bias_ref, sems):
    copies = [
        pltpu.make_async_copy(w_in_ref, slot_ref.at[0, 0:SLOT], sems.at[0]),
        pltpu.make_async_copy(w_out_ref, slot_ref.at[0, SLOT : 2 * SLOT], sems.at[1]),
        pltpu.make_async_copy(b_ref, bias_ref, sems.at[2]),
    ]
    for copy in copies:
        copy.start()
    for copy in copies:
        copy.wait()
    bias = bias_ref[...].astype(jnp.float32)[None, :]
    c = slot_ref.shape[2]
    wide = jnp.concatenate([bias] * (c // SLOT), axis=1)
    slot_ref[0, 2 * SLOT : 2 * SLOT + EXTRA, :] = jnp.broadcast_to(wide, (EXTRA, c)).astype(slot_ref.dtype)


def join_kernel(order_ref, *refs):
    *slots, early_ref, late_ref = refs
    for i, slot in enumerate(slots):
        out_ref, at = (early_ref, i) if i < early_ref.shape[0] else (late_ref, i - early_ref.shape[0])
        out_ref[at] = slot[0]


def radial_kernel(x_ref, taps_ref, out_ref, even, odd):
    n, a_loc, _, theta, c = x_ref.shape
    taps = taps_ref.shape[0]
    pad = (taps + 1) // 4
    zeros = jnp.zeros((pad, a_loc, 2 * theta, c), jnp.float32)
    even[0:pad] = zeros
    even[pad + n : 2 * pad + n] = zeros
    odd[0:pad] = zeros
    odd[pad + n - 1 : 2 * pad + n - 1] = zeros
    odd[2 * pad + n - 1 :] = zeros[:1]
    first = x_ref[:, :, 0].astype(jnp.float32)
    second = x_ref[:, :, 1].astype(jnp.float32)
    even[pad : pad + n, :, 0:theta] = first
    even[pad : pad + n, :, theta:] = second
    odd[pad : pad + n, :, 0:theta] = second
    odd[pad - 1 : pad + n - 1, :, theta:] = first

    def step(s, carry):
        total = jnp.zeros((a_loc, 2 * theta, c), jnp.float32)
        for k in range(taps):
            shift = k - taps // 2
            source = even if shift % 2 == 0 else odd
            total = total + source[s + (pad + shift // 2)] * taps_ref[k : k + 1, :]
        out_ref[s] = total.astype(out_ref.dtype)
        return carry

    lax.fori_loop(0, n, step, 0)


def tail_kernel(n_slots, z_ref, taps_ref, feat_ref, *rest):
    vectors, w_refs = rest[:5], rest[5 : 5 + n_slots]
    out_ref, padded, branch, field, consts, sems = rest[-6:]
    fetches = [pltpu.make_async_copy(feat_ref, field, sems.at[5])]
    for i, vector in enumerate(vectors):
        fetches.append(pltpu.make_async_copy(vector, consts.at[i], sems.at[i]))
    for fetch in fetches:
        fetch.start()
    axial, rows, c = z_ref.shape
    theta = rows // 2
    taps = taps_ref.shape[0]
    half = taps // 2
    zeros = jnp.zeros((half, rows, c), jnp.float32)
    padded[0:half] = zeros
    padded[half + axial :] = zeros
    padded[half : half + axial] = z_ref[...].astype(jnp.float32)
    block = 4

    def conv(i, carry):
        base = i * block
        total = jnp.zeros((block, rows, c), jnp.float32)
        for k in range(taps):
            total = total + padded[pl.ds(base + k, block)] * taps_ref[k : k + 1, :]
        branch[pl.ds(base, block)] = total
        return carry

    lax.fori_loop(0, axial // block, conv, 0)
    for fetch in fetches:
        fetch.wait()
    slots = [(w_ref, i) for w_ref in w_refs for i in range(w_ref.shape[0])]
    per = c // SLOT
    lane_slot = lax.broadcasted_iota(jnp.int32, (1, c), 1) // SLOT
    planes = 32

    def mlp(i, carry):
        v = (branch[pl.ds(i * planes, planes)] + consts[0]).reshape(planes * rows, c)
        v = v.astype(jnp.bfloat16).astype(jnp.float32)
        mean = jnp.mean(v, axis=-1, keepdims=True)
        centred = v - mean
        var = jnp.mean(centred * centred, axis=-1, keepdims=True)
        normed = (centred * lax.rsqrt(var + 1e-06) * consts[1] + consts[2]).astype(jnp.bfloat16)
        total = jnp.zeros((planes * rows, c), jnp.float32)
        for g in range(len(slots) // per):
            own = slots[g * per : (g + 1) * per]
            w_in = jnp.concatenate([w[j, 0:SLOT, :] for w, j in own], axis=0)
            w_out = jnp.concatenate([w[j, SLOT : 2 * SLOT, :] for w, j in own], axis=0)
            bias = jnp.zeros((1, c), jnp.float32)
            for at, (w, j) in enumerate(own):
                piece = w[j, 2 * SLOT : 2 * SLOT + EXTRA, :].astype(jnp.float32)[0:1]
                bias = jnp.where(lane_slot == at, piece, bias)
            u = lax.dot_general(normed, w_in, (((1,), (1,)), ((), ())), preferred_element_type=jnp.float32)
            u = u + bias
            hidden = (0.5 * u * (1.0 + jnp.tanh(0.7978845608028654 * (u + 0.044715 * u * u * u)))).astype(jnp.bfloat16)
            total = total + jnp.dot(hidden, w_out, preferred_element_type=jnp.float32)
        result = (consts[4] * (total + consts[3])).astype(jnp.bfloat16).astype(jnp.float32)
        branch[pl.ds(i * planes, planes)] = result.reshape(planes, rows, c)
        return carry

    if axial == planes:
        mlp(0, 0)
    else:
        lax.fori_loop(0, axial // planes, mlp, 0)
    for r in range(2):
        got = branch[:, r * theta : (r + 1) * theta, :]
        out_ref[:, r] = (field[:, r].astype(jnp.float32) + got).astype(out_ref.dtype)


def digits(n):
    chips = n // 2
    inner = 1
    while inner * inner * 4 <= chips:
        inner *= 2
    return chips // inner, inner, 2


def local(n, features, axial_taps, radial_taps, conv_bias, ln_gain, ln_bias, w_in, b_in, w_out, b_out, layer_scale):
    axial, r_loc, theta, c = features.shape
    rows = r_loc * theta
    hid_loc = w_in.shape[0]
    a_loc = axial // n
    outer, inner, _ = digits(n)
    spread = hid_loc == SLOT and n == 4 * outer and outer > 2
    small, middle, large = (pltpu.CompilerParams(vmem_limit_bytes=mib * 1024 * 1024) for mib in (2, 12, 24))
    anywhere = pl.BlockSpec(memory_space=pl.ANY)

    def move(piece, digit, by):
        stride = math.prod(digits(n)[digit + 1 :])
        return lax.ppermute(piece, "row", [(i, i ^ (by * stride)) for i in range(n)])

    if spread:
        own = pl.pallas_call(
            pack_kernel,
            out_shape=jax.ShapeDtypeStruct((1, 2 * SLOT + EXTRA, c), jnp.bfloat16),
            in_specs=[anywhere] * 3,
            out_specs=vmem(),
            scratch_shapes=[pltpu.VMEM(b_in.shape, jnp.bfloat16), pltpu.SemaphoreType.DMA((3,))],
            compiler_params=small,
            name="pack",
        )(b_in, w_in, w_out)
        line = [move(own, 0, by) for by in range(1, outer)]
        across = [move(own, 1, 1)]
        twin = [move(own, 2, 1)]
    else:
        w_all = lax.all_gather(w_in, "row", axis=0, tiled=True).reshape(-1, SLOT, c)
        o_all = lax.all_gather(w_out, "row", axis=0, tiled=True).reshape(-1, SLOT, c)
        b_all = lax.all_gather(b_in, "row", axis=0, tiled=True).reshape(-1, 1, SLOT)
        b_all = jnp.broadcast_to(jnp.tile(b_all, (1, 1, c // SLOT)), (w_all.shape[0], EXTRA, c))
        slots = [jnp.concatenate([w_all, o_all, b_all], axis=1)]

    got = lax.all_to_all(features, "row", split_axis=0, concat_axis=0, tiled=True)
    pad = (radial_taps.shape[0] + 1) // 4
    mixed = pl.pallas_call(
        radial_kernel,
        out_shape=jax.ShapeDtypeStruct((n, a_loc, rows, c), jnp.bfloat16),
        in_specs=[vmem()] * 2,
        out_specs=vmem(),
        scratch_shapes=[pltpu.VMEM((n + 2 * pad, a_loc, rows, c), jnp.float32)] * 2,
        compiler_params=middle,
        name="radial",
    )(got.reshape(n, a_loc, r_loc, theta, c), radial_taps)
    if spread:
        early = (outer - 1) // 2
        sizes = (outer - 1 - early, early)
        line = pl.pallas_call(
            join_kernel,
            out_shape=[jax.ShapeDtypeStruct((size,) + own.shape[1:], own.dtype) for size in sizes],
            in_specs=[anywhere] + [vmem()] * (outer - 1),
            out_specs=[vmem()] * 2,
            compiler_params=small,
            cost_estimate=pl.CostEstimate(flops=10**10, bytes_accessed=2 * 10**7, transcendentals=0),
            name="join",
        )(mixed, *line)
        line = list(line)
        across = across + [move(h, 1, 1) for h in line]
        twin = twin + [move(h, 2, 1) for h in line]
    back = lax.all_to_all(mixed.reshape(axial, rows, c), "row", split_axis=0, concat_axis=0, tiled=True)
    if spread:
        across, back = lax.optimization_barrier((across, back))
        slots = [own] + line + across + twin + [move(h, 2, 1) for h in across]
    vectors = [v[None, :] for v in (conv_bias, ln_gain, ln_bias, b_out, layer_scale)]
    return pl.pallas_call(
        partial(tail_kernel, len(slots)),
        out_shape=jax.ShapeDtypeStruct(features.shape, jnp.bfloat16),
        in_specs=[vmem()] * 2 + [anywhere] * 6 + [vmem()] * len(slots),
        out_specs=vmem(),
        scratch_shapes=[
            pltpu.VMEM((axial + axial_taps.shape[0] - 1, rows, c), jnp.float32),
            pltpu.VMEM((axial, rows, c), jnp.float32),
            pltpu.VMEM(features.shape, jnp.bfloat16),
            pltpu.VMEM((5, 1, c), jnp.float32),
            pltpu.SemaphoreType.DMA((6,)),
        ],
        compiler_params=large,
        name="tail",
    )(back, axial_taps, features, *vectors, *slots)


def solution(mesh):
    in_specs = (
        P("groups", "row", None, None),
        P(),
        P(),
        P(),
        P(),
        P(),
        P("row", None),
        P("row"),
        P("row", None),
        P(),
        P(),
    )
    out_specs = P("groups", "row", None, None)
    return jax.shard_map(partial(local, mesh.shape["row"]), mesh=mesh, in_specs=in_specs, out_specs=out_specs, check_vma=False)
```

```python
import math
from functools import partial

import jax
import jax.numpy as jnp
from jax import lax
from jax.experimental import pallas as pl
from jax.experimental.pallas import tpu as pltpu
from jax.sharding import PartitionSpec as P

SLOT = 64
EXTRA = 16


def vmem():
    return pl.BlockSpec(memory_space=pltpu.VMEM)


def pack_kernel(b_ref, w_in_ref, w_out_ref, *rest):
    *vectors, block_ref, consts_ref = rest
    block_ref[0:SLOT, :] = w_in_ref[...]
    block_ref[SLOT : 2 * SLOT, :] = w_out_ref[...]
    bias = b_ref[...].astype(jnp.float32)[None, :]
    c = block_ref.shape[1]
    wide = jnp.concatenate([bias] * (c // SLOT), axis=1)
    block_ref[2 * SLOT :, :] = jnp.broadcast_to(wide, (EXTRA, c)).astype(block_ref.dtype)
    for i, vector in enumerate(vectors):
        consts_ref[i : i + 1, :] = vector[...]


def join_kernel(*refs):
    blocks, out_ref = refs[2:-1], refs[-1]
    c = out_ref.shape[1]
    row = lax.broadcasted_iota(jnp.int32, (EXTRA, c), 0)
    biases = jnp.zeros((EXTRA, c), jnp.float32)
    for i, block in enumerate(blocks):
        out_ref[2 * SLOT * i : 2 * SLOT * (i + 1), :] = block[0 : 2 * SLOT, :]
        biases = jnp.where(row == i, block[2 * SLOT :, :].astype(jnp.float32), biases)
    out_ref[2 * SLOT * len(blocks) :, :] = biases.astype(out_ref.dtype)


def radial_kernel(x_ref, taps_ref, out_ref, even, odd):
    n, a_loc, _, theta, c = x_ref.shape
    taps = taps_ref.shape[0]
    pad = (taps + 1) // 4
    zeros = jnp.zeros((pad, a_loc, 2 * theta, c), jnp.float32)
    even[0:pad] = zeros
    even[pad + n : 2 * pad + n] = zeros
    odd[0:pad] = zeros
    odd[pad + n - 1 : 2 * pad + n - 1] = zeros
    odd[2 * pad + n - 1 :] = zeros[:1]
    first = x_ref[:, :, 0].astype(jnp.float32)
    second = x_ref[:, :, 1].astype(jnp.float32)
    even[pad : pad + n, :, 0:theta] = first
    even[pad : pad + n, :, theta:] = second
    odd[pad : pad + n, :, 0:theta] = second
    odd[pad - 1 : pad + n - 1, :, theta:] = first

    def step(s, carry):
        total = jnp.zeros((a_loc, 2 * theta, c), jnp.float32)
        for k in range(taps):
            shift = k - taps // 2
            source = even if shift % 2 == 0 else odd
            total = total + source[s + (pad + shift // 2)] * taps_ref[k : k + 1, :]
        out_ref[s] = total.astype(out_ref.dtype)
        return carry

    lax.fori_loop(0, n, step, 0)


def tail_kernel(z_ref, taps_ref, consts_ref, feat_ref, *rest):
    *blocks, out_ref, padded, branch, field, sem = rest
    fetch = pltpu.make_async_copy(feat_ref, field, sem)
    fetch.start()
    axial, rows, c = z_ref.shape
    theta = rows // 2
    taps = taps_ref.shape[0]
    half = taps // 2
    zeros = jnp.zeros((half, rows, c), jnp.float32)
    padded[0:half] = zeros
    padded[half + axial :] = zeros
    padded[half : half + axial] = z_ref[...].astype(jnp.float32)
    block = 4

    def conv(i, carry):
        base = i * block
        total = jnp.zeros((block, rows, c), jnp.float32)
        for k in range(taps):
            total = total + padded[pl.ds(base + k, block)] * taps_ref[k : k + 1, :]
        branch[pl.ds(base, block)] = total
        return carry

    lax.fori_loop(0, axial // block, conv, 0)
    fetch.wait()
    slots = [(block, i) for block in blocks for i in range(block.shape[0] // (2 * SLOT))]
    per = c // SLOT
    lane_slot = lax.broadcasted_iota(jnp.int32, (1, c), 1) // SLOT
    planes = 32

    def mlp(i, carry):
        v = (branch[pl.ds(i * planes, planes)] + consts_ref[0 : 1, :]).reshape(planes * rows, c)
        v = v.astype(jnp.bfloat16).astype(jnp.float32)
        mean = jnp.mean(v, axis=-1, keepdims=True)
        centred = v - mean
        var = jnp.mean(centred * centred, axis=-1, keepdims=True)
        normed = (centred * lax.rsqrt(var + 1e-06) * consts_ref[1 : 2, :] + consts_ref[2 : 3, :]).astype(jnp.bfloat16)
        total = jnp.zeros((planes * rows, c), jnp.float32)
        for g in range(len(slots) // per):
            own = slots[g * per : (g + 1) * per]
            w_in = jnp.concatenate([w[2 * SLOT * j : 2 * SLOT * j + SLOT, :] for w, j in own], axis=0)
            w_out = jnp.concatenate([w[2 * SLOT * j + SLOT : 2 * SLOT * (j + 1), :] for w, j in own], axis=0)
            bias = jnp.zeros((1, c), jnp.float32)
            for at, (w, j) in enumerate(own):
                piece = w[w.shape[0] - EXTRA :, :].astype(jnp.float32)[j : j + 1]
                bias = jnp.where(lane_slot == at, piece, bias)
            u = lax.dot_general(normed, w_in, (((1,), (1,)), ((), ())), preferred_element_type=jnp.float32)
            u = u + bias
            hidden = (0.5 * u * (1.0 + jnp.tanh(0.7978845608028654 * (u + 0.044715 * u * u * u)))).astype(jnp.bfloat16)
            total = total + jnp.dot(hidden, w_out, preferred_element_type=jnp.float32)
        result = (consts_ref[4 : 5, :] * (total + consts_ref[3 : 4, :])).astype(jnp.bfloat16).astype(jnp.float32)
        branch[pl.ds(i * planes, planes)] = result.reshape(planes, rows, c)
        return carry

    if axial == planes:
        mlp(0, 0)
    else:
        lax.fori_loop(0, axial // planes, mlp, 0)
    for r in range(2):
        got = branch[:, r * theta : (r + 1) * theta, :]
        out_ref[:, r] = (field[:, r].astype(jnp.float32) + got).astype(out_ref.dtype)


def digits(n):
    chips = n // 2
    inner = 1
    while inner * inner * 4 <= chips:
        inner *= 2
    return chips // inner, inner, 2


def local(n, features, axial_taps, radial_taps, conv_bias, ln_gain, ln_bias, w_in, b_in, w_out, b_out, layer_scale):
    axial, r_loc, theta, c = features.shape
    rows = r_loc * theta
    hid_loc = w_in.shape[0]
    a_loc = axial // n
    outer, inner, _ = digits(n)
    spread = hid_loc == SLOT and n == 4 * outer and 2 < outer <= EXTRA
    small, middle, large = (pltpu.CompilerParams(vmem_limit_bytes=mib * 1024 * 1024) for mib in (2, 12, 24))
    anywhere = pl.BlockSpec(memory_space=pl.ANY)

    def move(piece, digit, by):
        stride = math.prod(digits(n)[digit + 1 :])
        return lax.ppermute(piece, "row", [(i, i ^ (by * stride)) for i in range(n)])

    vectors = [v[None, :] for v in (conv_bias, ln_gain, ln_bias, b_out, layer_scale)]
    if spread:
        own, consts = pl.pallas_call(
            pack_kernel,
            out_shape=[
                jax.ShapeDtypeStruct((2 * SLOT + EXTRA, c), jnp.bfloat16),
                jax.ShapeDtypeStruct((8, c), jnp.float32),
            ],
            in_specs=[vmem()] * 8,
            out_specs=[vmem()] * 2,
            compiler_params=small,
            name="pack",
        )(b_in, w_in, w_out, *vectors)
        line = [move(own, 0, by) for by in range(1, outer)]
        side = move(own, 1, 1)
    else:
        consts = jnp.concatenate(vectors + [jnp.zeros((3, c), jnp.float32)], axis=0)
        w_all = lax.all_gather(w_in, "row", axis=0, tiled=True).reshape(-1, SLOT, c)
        o_all = lax.all_gather(w_out, "row", axis=0, tiled=True).reshape(-1, SLOT, c)
        b_all = jnp.tile(lax.all_gather(b_in, "row", axis=0, tiled=True).reshape(-1, SLOT), (1, c // SLOT))
        w_all = jnp.concatenate([w_all, o_all], axis=1).reshape(-1, c)
        blocks = [jnp.concatenate([w_all, jnp.pad(b_all, ((0, EXTRA - b_all.shape[0]), (0, 0)))], axis=0)]

    got = lax.all_to_all(features, "row", split_axis=0, concat_axis=0, tiled=True)
    pad = (radial_taps.shape[0] + 1) // 4
    mixed = pl.pallas_call(
        radial_kernel,
        out_shape=jax.ShapeDtypeStruct((n, a_loc, rows, c), jnp.bfloat16),
        in_specs=[vmem()] * 2,
        out_specs=vmem(),
        scratch_shapes=[pltpu.VMEM((n + 2 * pad, a_loc, rows, c), jnp.float32)] * 2,
        compiler_params=middle,
        name="radial",
    )(got.reshape(n, a_loc, r_loc, theta, c), radial_taps)
    if spread:
        joined = pl.pallas_call(
            join_kernel,
            out_shape=jax.ShapeDtypeStruct((2 * SLOT * (outer - 1) + EXTRA, c), jnp.bfloat16),
            in_specs=[anywhere] * 2 + [vmem()] * (outer - 1),
            out_specs=vmem(),
            compiler_params=small,
            cost_estimate=pl.CostEstimate(flops=10**10, bytes_accessed=2 * 10**7, transcendentals=0),
            name="join",
        )(mixed, side, *line)
        across = move(joined, 1, 1)
        twin = [move(h, 2, 1) for h in (own, side, joined)]
    back = lax.all_to_all(mixed.reshape(axial, rows, c), "row", split_axis=0, concat_axis=0, tiled=True)
    if spread:
        across, back = lax.optimization_barrier((across, back))
        blocks = [own, joined, side, across] + twin + [move(across, 2, 1)]
    return pl.pallas_call(
        tail_kernel,
        out_shape=jax.ShapeDtypeStruct(features.shape, jnp.bfloat16),
        in_specs=[vmem()] * 3 + [anywhere] + [vmem()] * len(blocks),
        out_specs=vmem(),
        scratch_shapes=[
            pltpu.VMEM((axial + axial_taps.shape[0] - 1, rows, c), jnp.float32),
            pltpu.VMEM((axial, rows, c), jnp.float32),
            pltpu.VMEM(features.shape, jnp.bfloat16),
            pltpu.SemaphoreType.DMA(()),
        ],
        compiler_params=large,
        name="tail",
    )(back, axial_taps, consts, features, *blocks)


def solution(mesh):
    in_specs = (
        P("groups", "row", None, None),
        P(),
        P(),
        P(),
        P(),
        P(),
        P("row", None),
        P("row"),
        P("row", None),
        P(),
        P(),
    )
    out_specs = P("groups", "row", None, None)
    return jax.shard_map(partial(local, mesh.shape["row"]), mesh=mesh, in_specs=in_specs, out_specs=out_specs, check_vma=False)
```

```python
import math
from functools import partial

import jax
import jax.numpy as jnp
from jax import lax
from jax.experimental import pallas as pl
from jax.experimental.pallas import tpu as pltpu
from jax.sharding import PartitionSpec as P

SLOT = 64
PLANES = 32
EXTRA = 16


def vmem():
    return pl.BlockSpec(memory_space=pltpu.VMEM)


def pack_kernel(b_ref, w_in_ref, w_out_ref, *rest):
    *vectors, block_ref, consts_ref = rest
    block_ref[0:SLOT, :] = w_in_ref[...]
    block_ref[SLOT : 2 * SLOT, :] = w_out_ref[...]
    bias = b_ref[...].astype(jnp.float32)[None, :]
    c = block_ref.shape[1]
    wide = jnp.concatenate([bias] * (c // SLOT), axis=1)
    block_ref[2 * SLOT :, :] = jnp.broadcast_to(wide, (EXTRA, c)).astype(block_ref.dtype)
    for i, vector in enumerate(vectors):
        consts_ref[i : i + 1, :] = vector[...]


def join_kernel(*refs):
    *blocks, all_ref, line_ref = refs[1:]
    c = all_ref.shape[1]
    row = lax.broadcasted_iota(jnp.int32, (EXTRA, c), 0)
    for out_ref in (all_ref, line_ref):
        count = out_ref.shape[0] // (2 * SLOT)
        biases = jnp.zeros((EXTRA, c), jnp.float32)
        for i, block in enumerate(blocks[:count]):
            out_ref[2 * SLOT * i : 2 * SLOT * (i + 1), :] = block[0 : 2 * SLOT, :]
            biases = jnp.where(row == i, block[2 * SLOT :, :].astype(jnp.float32), biases)
        out_ref[2 * SLOT * count :, :] = biases.astype(out_ref.dtype)


def radial_kernel(x_ref, taps_ref, out_ref, even, odd):
    n, a_loc, _, theta, c = x_ref.shape
    taps = taps_ref.shape[0]
    pad = (taps + 1) // 4
    zeros = jnp.zeros((pad, a_loc, 2 * theta, c), jnp.float32)
    even[0:pad] = zeros
    even[pad + n : 2 * pad + n] = zeros
    odd[0:pad] = zeros
    odd[pad + n - 1 : 2 * pad + n - 1] = zeros
    odd[2 * pad + n - 1 :] = zeros[:1]
    first = x_ref[:, :, 0].astype(jnp.float32)
    second = x_ref[:, :, 1].astype(jnp.float32)
    even[pad : pad + n, :, 0:theta] = first
    even[pad : pad + n, :, theta:] = second
    odd[pad : pad + n, :, 0:theta] = second
    odd[pad - 1 : pad + n - 1, :, theta:] = first

    block = 4

    def step(i, carry):
        base = i * block
        total = jnp.zeros((block, a_loc, 2 * theta, c), jnp.float32)
        for k in range(taps):
            shift = k - taps // 2
            source = even if shift % 2 == 0 else odd
            total = total + source[pl.ds(base + (pad + shift // 2), block)] * taps_ref[k : k + 1, :]
        out_ref[pl.ds(base, block)] = total.astype(out_ref.dtype)
        return carry

    lax.fori_loop(0, n // block, step, 0)


def axial_kernel(z_ref, taps_ref, consts_ref, out_ref, padded, summed):
    axial, rows, c = z_ref.shape
    taps = taps_ref.shape[0]
    half = taps // 2
    zeros = jnp.zeros((half, rows, c), jnp.float32)
    padded[0:half] = zeros
    padded[half + axial :] = zeros
    padded[half : half + axial] = z_ref[...].astype(jnp.float32)
    block = 8

    def conv(i, carry):
        base = i * block
        total = jnp.zeros((block, rows, c), jnp.float32)
        for k in range(taps):
            total = total + padded[pl.ds(base + k, block)] * taps_ref[k : k + 1, :]
        summed[pl.ds(base, block)] = total
        return carry

    lax.fori_loop(0, axial // block, conv, 0)

    def norm(i, carry):
        v = (summed[pl.ds(i * PLANES, PLANES)] + consts_ref[0:1, :]).reshape(PLANES * rows, c)
        v = v.astype(jnp.bfloat16).astype(jnp.float32)
        mean = jnp.mean(v, axis=-1, keepdims=True)
        centred = v - mean
        var = jnp.mean(centred * centred, axis=-1, keepdims=True)
        normed = centred * lax.rsqrt(var + 1e-06) * consts_ref[1:2, :] + consts_ref[2:3, :]
        at = pl.multiple_of(i * PLANES * rows, PLANES * rows)
        out_ref[pl.ds(at, PLANES * rows), :] = normed.astype(out_ref.dtype)
        return carry

    lax.fori_loop(0, axial // PLANES, norm, 0)


def mlp_kernel(normed_ref, consts_ref, feat_ref, *rest):
    *blocks, out_ref, branch = rest
    axial, _, theta, c = feat_ref.shape
    rows = 2 * theta
    slots = [(block, i) for block in blocks for i in range(block.shape[0] // (2 * SLOT))]
    per = c // SLOT
    lane_slot = lax.broadcasted_iota(jnp.int32, (1, c), 1) // SLOT

    def mlp(i, carry):
        at = pl.multiple_of(i * PLANES * rows, PLANES * rows)
        normed = normed_ref[pl.ds(at, PLANES * rows), :]
        total = jnp.zeros((PLANES * rows, c), jnp.float32)
        for g in range(len(slots) // per):
            own = slots[g * per : (g + 1) * per]
            w_in = jnp.concatenate([w[2 * SLOT * j : 2 * SLOT * j + SLOT, :] for w, j in own], axis=0)
            w_out = jnp.concatenate([w[2 * SLOT * j + SLOT : 2 * SLOT * (j + 1), :] for w, j in own], axis=0)
            bias = jnp.zeros((1, c), jnp.float32)
            for spot, (w, j) in enumerate(own):
                piece = w[w.shape[0] - EXTRA :, :].astype(jnp.float32)[j : j + 1]
                bias = jnp.where(lane_slot == spot, piece, bias)
            u = lax.dot_general(normed, w_in, (((1,), (1,)), ((), ())), preferred_element_type=jnp.float32)
            u = u + bias
            hidden = (0.5 * u * (1.0 + jnp.tanh(0.7978845608028654 * (u + 0.044715 * u * u * u)))).astype(jnp.bfloat16)
            total = total + jnp.dot(hidden, w_out, preferred_element_type=jnp.float32)
        result = (consts_ref[4 : 5, :] * (total + consts_ref[3 : 4, :])).astype(jnp.bfloat16).astype(jnp.float32)
        branch[pl.ds(i * PLANES, PLANES)] = result.reshape(PLANES, rows, c)
        return carry

    if axial == PLANES:
        mlp(0, 0)
    else:
        lax.fori_loop(0, axial // PLANES, mlp, 0)
    for r in range(2):
        got = branch[:, r * theta : (r + 1) * theta, :]
        out_ref[:, r] = (feat_ref[:, r].astype(jnp.float32) + got).astype(out_ref.dtype)


def digits(n):
    chips = n // 2
    inner = 1
    while inner * inner * 4 <= chips:
        inner *= 2
    return chips // inner, inner, 2


def local(n, features, axial_taps, radial_taps, conv_bias, ln_gain, ln_bias, w_in, b_in, w_out, b_out, layer_scale):
    axial, r_loc, theta, c = features.shape
    rows = r_loc * theta
    hid_loc = w_in.shape[0]
    a_loc = axial // n
    outer, inner, _ = digits(n)
    spread = hid_loc == SLOT and n == 4 * outer and 2 < outer <= EXTRA
    small, middle, large = (pltpu.CompilerParams(vmem_limit_bytes=mib * 1024 * 1024) for mib in (2, 12, 24))
    anywhere = pl.BlockSpec(memory_space=pl.ANY)

    def move(piece, digit, by):
        stride = math.prod(digits(n)[digit + 1 :])
        return lax.ppermute(piece, "row", [(i, i ^ (by * stride)) for i in range(n)])

    vectors = [v[None, :] for v in (conv_bias, ln_gain, ln_bias, b_out, layer_scale)]
    if spread:
        own, consts = pl.pallas_call(
            pack_kernel,
            out_shape=[
                jax.ShapeDtypeStruct((2 * SLOT + EXTRA, c), jnp.bfloat16),
                jax.ShapeDtypeStruct((8, c), jnp.float32),
            ],
            in_specs=[vmem()] * 8,
            out_specs=[vmem()] * 2,
            compiler_params=small,
            name="pack",
        )(b_in, w_in, w_out, *vectors)
        line = [move(own, 0, by) for by in range(1, outer)]
        side = move(own, 1, 1)
    else:
        consts = jnp.concatenate(vectors + [jnp.zeros((3, c), jnp.float32)], axis=0)
        w_all = lax.all_gather(w_in, "row", axis=0, tiled=True).reshape(-1, SLOT, c)
        o_all = lax.all_gather(w_out, "row", axis=0, tiled=True).reshape(-1, SLOT, c)
        b_all = jnp.tile(lax.all_gather(b_in, "row", axis=0, tiled=True).reshape(-1, SLOT), (1, c // SLOT))
        w_all = jnp.concatenate([w_all, o_all], axis=1).reshape(-1, c)
        blocks = [jnp.concatenate([w_all, jnp.pad(b_all, ((0, EXTRA - b_all.shape[0]), (0, 0)))], axis=0)]

    got = lax.all_to_all(features, "row", split_axis=0, concat_axis=0, tiled=True)
    pad = (radial_taps.shape[0] + 1) // 4
    mixed = pl.pallas_call(
        radial_kernel,
        out_shape=jax.ShapeDtypeStruct((n, a_loc, rows, c), jnp.bfloat16),
        in_specs=[vmem()] * 2,
        out_specs=vmem(),
        scratch_shapes=[pltpu.VMEM((n + 2 * pad, a_loc, rows, c), jnp.float32)] * 2,
        compiler_params=middle,
        name="radial",
    )(got.reshape(n, a_loc, r_loc, theta, c), radial_taps)
    if spread:
        joined, reach = pl.pallas_call(
            join_kernel,
            out_shape=[jax.ShapeDtypeStruct((2 * SLOT * size + EXTRA, c), jnp.bfloat16) for size in (outer + 1, outer - 1)],
            in_specs=[anywhere] + [vmem()] * (outer + 1),
            out_specs=[vmem()] * 2,
            compiler_params=small,
            cost_estimate=pl.CostEstimate(flops=10**10, bytes_accessed=2 * 10**7, transcendentals=0),
            name="join",
        )(mixed, *line, own, side)
        across = move(reach, 1, 1)
        twin = move(joined, 2, 1)
    back = lax.all_to_all(mixed.reshape(axial, rows, c), "row", split_axis=0, concat_axis=0, tiled=True)
    normed = pl.pallas_call(
        axial_kernel,
        out_shape=jax.ShapeDtypeStruct((axial * rows, c), jnp.bfloat16),
        in_specs=[vmem()] * 3,
        out_specs=vmem(),
        scratch_shapes=[
            pltpu.VMEM((axial + axial_taps.shape[0] - 1, rows, c), jnp.float32),
            pltpu.VMEM((axial, rows, c), jnp.float32),
        ],
        compiler_params=middle,
        name="axial",
    )(back, axial_taps, consts)
    if spread:
        across, normed = lax.optimization_barrier((across, normed))
        blocks = [joined, across, twin, move(across, 2, 1)]
    return pl.pallas_call(
        mlp_kernel,
        out_shape=jax.ShapeDtypeStruct(features.shape, jnp.bfloat16),
        in_specs=[vmem()] * (3 + len(blocks)),
        out_specs=vmem(),
        scratch_shapes=[pltpu.VMEM((axial, rows, c), jnp.float32)],
        compiler_params=large,
        name="mlp",
    )(normed, consts, features, *blocks)


def solution(mesh):
    in_specs = (
        P("groups", "row", None, None),
        P(),
        P(),
        P(),
        P(),
        P(),
        P("row", None),
        P("row"),
        P("row", None),
        P(),
        P(),
    )
    out_specs = P("groups", "row", None, None)
    return jax.shard_map(partial(local, mesh.shape["row"]), mesh=mesh, in_specs=in_specs, out_specs=out_specs, check_vma=False)
```

```python
import math
from functools import partial

import jax
import jax.numpy as jnp
from jax import lax
from jax.experimental import pallas as pl
from jax.experimental.pallas import tpu as pltpu
from jax.sharding import PartitionSpec as P

SLOT = 64
PLANES = 32
EXTRA = 16


def vmem():
    return pl.BlockSpec(memory_space=pltpu.VMEM)


def pack_kernel(b_ref, w_in_ref, w_out_ref, *rest):
    *vectors, block_ref, consts_ref = rest
    block_ref[0:SLOT, :] = w_in_ref[...]
    block_ref[SLOT : 2 * SLOT, :] = w_out_ref[...]
    bias = b_ref[...].astype(jnp.float32)[None, :]
    c = block_ref.shape[1]
    wide = jnp.concatenate([bias] * (c // SLOT), axis=1)
    block_ref[2 * SLOT :, :] = jnp.broadcast_to(wide, (EXTRA, c)).astype(block_ref.dtype)
    for i, vector in enumerate(vectors):
        consts_ref[i : i + 1, :] = vector[...]


def join_kernel(*refs):
    *blocks, all_ref, most_ref, last_ref = refs[1:]
    c = all_ref.shape[1]
    row = lax.broadcasted_iota(jnp.int32, (EXTRA, c), 0)
    for out_ref in (all_ref, most_ref):
        count = out_ref.shape[0] // (2 * SLOT)
        biases = jnp.zeros((EXTRA, c), jnp.float32)
        for i, block in enumerate(blocks[:count]):
            out_ref[2 * SLOT * i : 2 * SLOT * (i + 1), :] = block[0 : 2 * SLOT, :]
            biases = jnp.where(row == i, block[2 * SLOT :, :].astype(jnp.float32), biases)
        out_ref[2 * SLOT * count :, :] = biases.astype(out_ref.dtype)
    last_ref[...] = blocks[count][...]


def radial_kernel(x_ref, taps_ref, out_ref, even, odd):
    n, a_loc, _, theta, c = x_ref.shape
    taps = taps_ref.shape[0]
    pad = (taps + 1) // 4
    zeros = jnp.zeros((pad, a_loc, 2 * theta, c), jnp.float32)
    even[0:pad] = zeros
    even[pad + n : 2 * pad + n] = zeros
    odd[0:pad] = zeros
    odd[pad + n - 1 : 2 * pad + n - 1] = zeros
    odd[2 * pad + n - 1 :] = zeros[:1]
    first = x_ref[:, :, 0].astype(jnp.float32)
    second = x_ref[:, :, 1].astype(jnp.float32)
    even[pad : pad + n, :, 0:theta] = first
    even[pad : pad + n, :, theta:] = second
    odd[pad : pad + n, :, 0:theta] = second
    odd[pad - 1 : pad + n - 1, :, theta:] = first

    block = 4

    def step(i, carry):
        base = i * block
        total = jnp.zeros((block, a_loc, 2 * theta, c), jnp.float32)
        for k in range(taps):
            shift = k - taps // 2
            source = even if shift % 2 == 0 else odd
            total = total + source[pl.ds(base + (pad + shift // 2), block)] * taps_ref[k : k + 1, :]
        out_ref[pl.ds(base, block)] = total.astype(out_ref.dtype)
        return carry

    lax.fori_loop(0, n // block, step, 0)


def axial_kernel(z_ref, taps_ref, consts_ref, out_ref, padded, summed):
    axial, rows, c = z_ref.shape
    taps = taps_ref.shape[0]
    half = taps // 2
    zeros = jnp.zeros((half, rows, c), jnp.float32)
    padded[0:half] = zeros
    padded[half + axial :] = zeros
    padded[half : half + axial] = z_ref[...].astype(jnp.float32)
    block = 8

    def conv(i, carry):
        base = i * block
        total = jnp.zeros((block, rows, c), jnp.float32)
        for k in range(taps):
            total = total + padded[pl.ds(base + k, block)] * taps_ref[k : k + 1, :]
        summed[pl.ds(base, block)] = total
        return carry

    lax.fori_loop(0, axial // block, conv, 0)

    def norm(i, carry):
        v = (summed[pl.ds(i * PLANES, PLANES)] + consts_ref[0:1, :]).reshape(PLANES * rows, c)
        v = v.astype(jnp.bfloat16).astype(jnp.float32)
        mean = jnp.mean(v, axis=-1, keepdims=True)
        centred = v - mean
        var = jnp.mean(centred * centred, axis=-1, keepdims=True)
        normed = centred * lax.rsqrt(var + 1e-06) * consts_ref[1:2, :] + consts_ref[2:3, :]
        at = pl.multiple_of(i * PLANES * rows, PLANES * rows)
        out_ref[pl.ds(at, PLANES * rows), :] = normed.astype(out_ref.dtype)
        return carry

    lax.fori_loop(0, axial // PLANES, norm, 0)


def hidden_sum(normed, blocks):
    c = normed.shape[1]
    per = c // SLOT
    lane_slot = lax.broadcasted_iota(jnp.int32, (1, c), 1) // SLOT
    slots = [(block, i) for block in blocks for i in range(block.shape[0] // (2 * SLOT))]
    total = None
    for g in range(0, len(slots), per):
        own = slots[g : g + per]
        w_in = jnp.concatenate([w[2 * SLOT * j : 2 * SLOT * j + SLOT, :] for w, j in own], axis=0)
        w_out = jnp.concatenate([w[2 * SLOT * j + SLOT : 2 * SLOT * (j + 1), :] for w, j in own], axis=0)
        bias = jnp.zeros((1, c), jnp.float32)
        for spot, (w, j) in enumerate(own):
            piece = w[w.shape[0] - EXTRA :, :].astype(jnp.float32)[j : j + 1]
            bias = jnp.where(lane_slot == spot, piece, bias)
        u = lax.dot_general(normed, w_in, (((1,), (1,)), ((), ())), preferred_element_type=jnp.float32)
        u = u + bias[:, : len(own) * SLOT]
        hidden = (0.5 * u * (1.0 + jnp.tanh(0.7978845608028654 * (u + 0.044715 * u * u * u)))).astype(jnp.bfloat16)
        part = jnp.dot(hidden, w_out, preferred_element_type=jnp.float32)
        total = part if total is None else total + part
    return total


def over_tokens(count, size, body):
    if count == size:
        body(0)
    else:
        pl.loop(0, count // size)(lambda i: body(pl.multiple_of(i * size, size)))


def first_kernel(normed_ref, *rest):
    *blocks, out_ref = rest
    size = PLANES * 8

    def part(at):
        out_ref[pl.ds(at, size), :] = hidden_sum(normed_ref[pl.ds(at, size), :], blocks)

    over_tokens(normed_ref.shape[0], size, part)


def mlp_kernel(partials, normed_ref, consts_ref, feat_ref, *rest):
    *blocks, out_ref, branch = rest
    theta, c = feat_ref.shape[2:]
    rows = 2 * theta
    size = PLANES * rows

    def mlp(at):
        total = hidden_sum(normed_ref[pl.ds(at, size), :], blocks[partials:])
        for partial_ref in blocks[:partials]:
            total = total + partial_ref[pl.ds(at, size), :]
        result = (consts_ref[4:5, :] * (total + consts_ref[3:4, :])).astype(jnp.bfloat16).astype(jnp.float32)
        branch[pl.ds(at // rows, PLANES)] = result.reshape(PLANES, rows, c)

    over_tokens(normed_ref.shape[0], size, mlp)
    for r in range(2):
        got = branch[:, r * theta : (r + 1) * theta, :]
        out_ref[:, r] = (feat_ref[:, r].astype(jnp.float32) + got).astype(out_ref.dtype)


def digits(n):
    chips = n // 2
    inner = 1
    while inner * inner * 4 <= chips:
        inner *= 2
    return chips // inner, inner, 2


def local(n, features, axial_taps, radial_taps, conv_bias, ln_gain, ln_bias, w_in, b_in, w_out, b_out, layer_scale):
    axial, r_loc, theta, c = features.shape
    rows = r_loc * theta
    hid_loc = w_in.shape[0]
    a_loc = axial // n
    outer, inner, _ = digits(n)
    spread = hid_loc == SLOT and n == 4 * outer and 2 < outer <= EXTRA
    small, middle, large = (pltpu.CompilerParams(vmem_limit_bytes=mib * 1024 * 1024) for mib in (2, 12, 24))
    anywhere = pl.BlockSpec(memory_space=pl.ANY)

    def move(piece, digit, by):
        stride = math.prod(digits(n)[digit + 1 :])
        return lax.ppermute(piece, "row", [(i, i ^ (by * stride)) for i in range(n)])

    vectors = [v[None, :] for v in (conv_bias, ln_gain, ln_bias, b_out, layer_scale)]
    if spread:
        own, consts = pl.pallas_call(
            pack_kernel,
            out_shape=[
                jax.ShapeDtypeStruct((2 * SLOT + EXTRA, c), jnp.bfloat16),
                jax.ShapeDtypeStruct((8, c), jnp.float32),
            ],
            in_specs=[vmem()] * 8,
            out_specs=[vmem()] * 2,
            compiler_params=small,
            name="pack",
        )(b_in, w_in, w_out, *vectors)
        line = [move(own, 0, by) for by in range(1, outer)]
        side = move(own, 1, 1)
    else:
        consts = jnp.concatenate(vectors + [jnp.zeros((3, c), jnp.float32)], axis=0)
        w_all = lax.all_gather(w_in, "row", axis=0, tiled=True).reshape(-1, SLOT, c)
        o_all = lax.all_gather(w_out, "row", axis=0, tiled=True).reshape(-1, SLOT, c)
        b_all = jnp.tile(lax.all_gather(b_in, "row", axis=0, tiled=True).reshape(-1, SLOT), (1, c // SLOT))
        w_all = jnp.concatenate([w_all, o_all], axis=1).reshape(-1, c)
        blocks = [jnp.concatenate([w_all, jnp.pad(b_all, ((0, EXTRA - b_all.shape[0]), (0, 0)))], axis=0)]

    got = lax.all_to_all(features, "row", split_axis=0, concat_axis=0, tiled=True)
    pad = (radial_taps.shape[0] + 1) // 4
    mixed = pl.pallas_call(
        radial_kernel,
        out_shape=jax.ShapeDtypeStruct((n, a_loc, rows, c), jnp.bfloat16),
        in_specs=[vmem()] * 2,
        out_specs=vmem(),
        scratch_shapes=[pltpu.VMEM((n + 2 * pad, a_loc, rows, c), jnp.float32)] * 2,
        compiler_params=middle,
        name="radial",
    )(got.reshape(n, a_loc, r_loc, theta, c), radial_taps)
    if spread:
        joined, most, last = pl.pallas_call(
            join_kernel,
            out_shape=[jax.ShapeDtypeStruct((2 * SLOT * size + EXTRA, c), jnp.bfloat16) for size in (outer + 1, outer - 2, 1)],
            in_specs=[anywhere] + [vmem()] * (outer + 1),
            out_specs=[vmem()] * 3,
            compiler_params=small,
            cost_estimate=pl.CostEstimate(flops=10**10, bytes_accessed=2 * 10**7, transcendentals=0),
            name="join",
        )(mixed, *line, own, side)
        across = [move(most, 1, 1), move(last, 1, 1)]
        twin = move(joined, 2, 1)
    back = lax.all_to_all(mixed.reshape(axial, rows, c), "row", split_axis=0, concat_axis=0, tiled=True)
    normed = pl.pallas_call(
        axial_kernel,
        out_shape=jax.ShapeDtypeStruct((axial * rows, c), jnp.bfloat16),
        in_specs=[vmem()] * 3,
        out_specs=vmem(),
        scratch_shapes=[
            pltpu.VMEM((axial + axial_taps.shape[0] - 1, rows, c), jnp.float32),
            pltpu.VMEM((axial, rows, c), jnp.float32),
        ],
        compiler_params=middle,
        name="axial",
    )(back, axial_taps, consts)
    if spread:
        across, normed = lax.optimization_barrier((across, normed))
        blocks = across + [move(h, 2, 1) for h in across]
        partials = [
            pl.pallas_call(
                first_kernel,
                out_shape=jax.ShapeDtypeStruct((axial * rows, c), jnp.float32),
                in_specs=[vmem()] * 3,
                out_specs=vmem(),
                compiler_params=middle,
                name="first",
            )(normed, joined, twin)
        ]
    else:
        partials = []
    operands = partials + blocks
    return pl.pallas_call(
        partial(mlp_kernel, len(partials)),
        out_shape=jax.ShapeDtypeStruct(features.shape, jnp.bfloat16),
        in_specs=[vmem()] * (3 + len(operands)),
        out_specs=vmem(),
        scratch_shapes=[pltpu.VMEM((axial, rows, c), jnp.float32)],
        compiler_params=large,
        name="mlp",
    )(normed, consts, features, *operands)


def solution(mesh):
    in_specs = (
        P("groups", "row", None, None),
        P(),
        P(),
        P(),
        P(),
        P(),
        P("row", None),
        P("row"),
        P("row", None),
        P(),
        P(),
    )
    out_specs = P("groups", "row", None, None)
    return jax.shard_map(partial(local, mesh.shape["row"]), mesh=mesh, in_specs=in_specs, out_specs=out_specs, check_vma=False)
```

```python
import math
from functools import partial

import jax
import jax.numpy as jnp
from jax import lax
from jax.experimental import pallas as pl
from jax.experimental.pallas import tpu as pltpu
from jax.sharding import PartitionSpec as P

SLOT = 64
PLANES = 32
EXTRA = 16


def vmem():
    return pl.BlockSpec(memory_space=pltpu.VMEM)


def pack_kernel(b_ref, w_in_ref, w_out_ref, block_ref):
    block_ref[0:SLOT, :] = w_in_ref[...]
    block_ref[SLOT : 2 * SLOT, :] = w_out_ref[...]
    bias = b_ref[...].astype(jnp.float32)[None, :]
    c = block_ref.shape[1]
    wide = jnp.concatenate([bias] * (c // SLOT), axis=1)
    block_ref[2 * SLOT :, :] = jnp.broadcast_to(wide, (EXTRA, c)).astype(block_ref.dtype)


def join_kernel(*refs):
    *blocks, all_ref, most_ref, last_ref = refs[1:]
    c = all_ref.shape[1]
    row = lax.broadcasted_iota(jnp.int32, (EXTRA, c), 0)
    for out_ref in (all_ref, most_ref):
        count = out_ref.shape[0] // (2 * SLOT)
        biases = jnp.zeros((EXTRA, c), jnp.float32)
        for i, block in enumerate(blocks[:count]):
            out_ref[2 * SLOT * i : 2 * SLOT * (i + 1), :] = block[0 : 2 * SLOT, :]
            biases = jnp.where(row == i, block[2 * SLOT :, :].astype(jnp.float32), biases)
        out_ref[2 * SLOT * count :, :] = biases.astype(out_ref.dtype)
    last_ref[...] = blocks[count][...]


def radial_kernel(x_ref, taps_ref, *rest):
    vectors = rest[:5]
    out_ref, consts_ref, even, odd, done, sems = rest[5:]
    for i, vector in enumerate(vectors):
        consts_ref[i : i + 1, :] = vector[...]
    n, a_loc, _, theta, c = x_ref.shape
    taps = taps_ref.shape[0]
    pad = (taps + 1) // 4
    zeros = jnp.zeros((pad, a_loc, 2 * theta, c), jnp.float32)
    even[0:pad] = zeros
    even[pad + n : 2 * pad + n] = zeros
    odd[0:pad] = zeros
    odd[pad + n - 1 : 2 * pad + n - 1] = zeros
    odd[2 * pad + n - 1 :] = zeros[:1]
    first = x_ref[:, :, 0].astype(jnp.float32)
    second = x_ref[:, :, 1].astype(jnp.float32)
    even[pad : pad + n, :, 0:theta] = first
    even[pad : pad + n, :, theta:] = second
    odd[pad : pad + n, :, 0:theta] = second
    odd[pad - 1 : pad + n - 1, :, theta:] = first

    block = 4

    def step(base, wanted):
        total = jnp.zeros((block, a_loc, 2 * theta, c), jnp.float32)
        for shift in wanted:
            k = shift + taps // 2
            source = even if shift % 2 == 0 else odd
            total = total + source[pl.ds(base + (pad + shift // 2), block)] * taps_ref[k : k + 1, :]
        done[pl.ds(base, block)] = total.astype(done.dtype)

    every = range(-(taps // 2), taps // 2 + 1)
    if n <= 8 * block:
        copies = []
        for base in range(0, n, block):
            step(base, [s for s in every if base + block - 1 + s // 2 >= -(s % 2) and base + s // 2 < n])
            part = pl.ds(base, block)
            copies.append(pltpu.make_async_copy(done.at[part], out_ref.at[part], sems.at[base // block]))
            copies[-1].start()
    else:
        pl.loop(0, n // block)(lambda i: step(i * block, every))
        copies = [pltpu.make_async_copy(done, out_ref, sems.at[0])]
        copies[0].start()
    for copy in copies:
        copy.wait()


def axial_kernel(z_ref, taps_ref, consts_ref, out_ref, padded, summed):
    axial, rows, c = z_ref.shape
    taps = taps_ref.shape[0]
    half = taps // 2
    zeros = jnp.zeros((half, rows, c), jnp.float32)
    padded[0:half] = zeros
    padded[half + axial :] = zeros
    padded[half : half + axial] = z_ref[...].astype(jnp.float32)
    block = 8

    def conv(base, wanted):
        total = jnp.zeros((block, rows, c), jnp.float32)
        for k in wanted:
            total = total + padded[pl.ds(base + k, block)] * taps_ref[k : k + 1, :]
        summed[pl.ds(base, block)] = total

    if axial <= 8 * block:
        for base in range(0, axial, block):
            conv(base, [k for k in range(taps) if base + block - 1 + k >= half and base + k < half + axial])
    else:
        pl.loop(0, axial // block)(lambda i: conv(i * block, range(taps)))

    def norm(i, carry):
        v = (summed[pl.ds(i * PLANES, PLANES)] + consts_ref[0:1, :]).reshape(PLANES * rows, c)
        v = v.astype(jnp.bfloat16).astype(jnp.float32)
        mean = jnp.mean(v, axis=-1, keepdims=True)
        centred = v - mean
        var = jnp.mean(centred * centred, axis=-1, keepdims=True)
        normed = centred * lax.rsqrt(var + 1e-06) * consts_ref[1:2, :] + consts_ref[2:3, :]
        at = pl.multiple_of(i * PLANES * rows, PLANES * rows)
        out_ref[pl.ds(at, PLANES * rows), :] = normed.astype(out_ref.dtype)
        return carry

    lax.fori_loop(0, axial // PLANES, norm, 0)


def hidden_sum(normed, blocks):
    c = normed.shape[1]
    per = c // SLOT
    lane_slot = lax.broadcasted_iota(jnp.int32, (1, c), 1) // SLOT
    slots = [(block, i) for block in blocks for i in range(block.shape[0] // (2 * SLOT))]
    total = None
    for g in range(0, len(slots), per):
        own = slots[g : g + per]
        w_in = jnp.concatenate([w[2 * SLOT * j : 2 * SLOT * j + SLOT, :] for w, j in own], axis=0)
        w_out = jnp.concatenate([w[2 * SLOT * j + SLOT : 2 * SLOT * (j + 1), :] for w, j in own], axis=0)
        bias = jnp.zeros((1, c), jnp.float32)
        for spot, (w, j) in enumerate(own):
            piece = w[w.shape[0] - EXTRA :, :].astype(jnp.float32)[j : j + 1]
            bias = jnp.where(lane_slot == spot, piece, bias)
        u = lax.dot_general(normed, w_in, (((1,), (1,)), ((), ())), preferred_element_type=jnp.float32)
        u = u + bias[:, : len(own) * SLOT]
        hidden = (0.5 * u * (1.0 + jnp.tanh(0.7978845608028654 * (u + 0.044715 * u * u * u)))).astype(jnp.bfloat16)
        part = jnp.dot(hidden, w_out, preferred_element_type=jnp.float32)
        total = part if total is None else total + part
    return total


def over_tokens(count, size, body):
    if count == size:
        body(0)
    else:
        pl.loop(0, count // size)(lambda i: body(pl.multiple_of(i * size, size)))


def first_kernel(normed_ref, *rest):
    *blocks, out_ref = rest
    size = PLANES * 8

    def part(at):
        out_ref[pl.ds(at, size), :] = hidden_sum(normed_ref[pl.ds(at, size), :], blocks)

    over_tokens(normed_ref.shape[0], size, part)


def mlp_kernel(partials, normed_ref, consts_ref, feat_ref, *rest):
    *blocks, out_ref, branch, done, sems = rest
    axial, _, theta, c = feat_ref.shape
    rows = 2 * theta
    planes = PLANES // 2

    def mlp(at, size):
        tokens = pl.ds(at * rows, size * rows)
        total = hidden_sum(normed_ref[tokens, :], blocks[partials:])
        for partial_ref in blocks[:partials]:
            total = total + partial_ref[tokens, :]
        result = (consts_ref[4:5, :] * (total + consts_ref[3:4, :])).astype(jnp.bfloat16).astype(jnp.float32)
        branch[pl.ds(at, size)] = result.reshape(size, rows, c)
        for r in range(2):
            got = branch[pl.ds(at, size), r * theta : (r + 1) * theta, :]
            done[pl.ds(at, size), r] = (feat_ref[pl.ds(at, size), r].astype(jnp.float32) + got).astype(done.dtype)

    copies = []
    if axial == PLANES:
        for i in range(2):
            mlp(i * planes, planes)
            part = pl.ds(i * planes, planes)
            copies.append(pltpu.make_async_copy(done.at[part], out_ref.at[part], sems.at[i]))
            copies[-1].start()
    else:
        pl.loop(0, axial // PLANES)(lambda i: mlp(pl.multiple_of(i * PLANES, PLANES), PLANES))
        copies.append(pltpu.make_async_copy(done, out_ref, sems.at[0]))
        copies[-1].start()
    for copy in copies:
        copy.wait()


def digits(n):
    chips = n // 2
    inner = 1
    while inner * inner * 4 <= chips:
        inner *= 2
    return chips // inner, inner, 2


def local(n, features, axial_taps, radial_taps, conv_bias, ln_gain, ln_bias, w_in, b_in, w_out, b_out, layer_scale):
    axial, r_loc, theta, c = features.shape
    rows = r_loc * theta
    hid_loc = w_in.shape[0]
    a_loc = axial // n
    outer, inner, _ = digits(n)
    spread = hid_loc == SLOT and n == 4 * outer and 2 < outer <= EXTRA
    small, middle, large = (pltpu.CompilerParams(vmem_limit_bytes=mib * 1024 * 1024) for mib in (2, 12, 24))
    anywhere = pl.BlockSpec(memory_space=pl.ANY)

    def move(piece, digit, by):
        stride = math.prod(digits(n)[digit + 1 :])
        return lax.ppermute(piece, "row", [(i, i ^ (by * stride)) for i in range(n)])

    vectors = [v[None, :] for v in (conv_bias, ln_gain, ln_bias, b_out, layer_scale)]
    if spread:
        own = pl.pallas_call(
            pack_kernel,
            out_shape=jax.ShapeDtypeStruct((2 * SLOT + EXTRA, c), jnp.bfloat16),
            in_specs=[vmem()] * 3,
            out_specs=vmem(),
            compiler_params=small,
            name="pack",
        )(b_in, w_in, w_out)
        line = [move(own, 0, by) for by in range(1, outer)]
        side = move(own, 1, 1)
    else:
        w_all = lax.all_gather(w_in, "row", axis=0, tiled=True).reshape(-1, SLOT, c)
        o_all = lax.all_gather(w_out, "row", axis=0, tiled=True).reshape(-1, SLOT, c)
        b_all = jnp.tile(lax.all_gather(b_in, "row", axis=0, tiled=True).reshape(-1, SLOT), (1, c // SLOT))
        w_all = jnp.concatenate([w_all, o_all], axis=1).reshape(-1, c)
        blocks = [jnp.concatenate([w_all, jnp.pad(b_all, ((0, EXTRA - b_all.shape[0]), (0, 0)))], axis=0)]

    got = lax.all_to_all(features, "row", split_axis=0, concat_axis=0, tiled=True)
    pad = (radial_taps.shape[0] + 1) // 4
    mixed, consts = pl.pallas_call(
        radial_kernel,
        out_shape=[
            jax.ShapeDtypeStruct((n, a_loc, rows, c), jnp.bfloat16),
            jax.ShapeDtypeStruct((8, c), jnp.float32),
        ],
        in_specs=[vmem()] * 7,
        out_specs=[anywhere, vmem()],
        scratch_shapes=[pltpu.VMEM((n + 2 * pad, a_loc, rows, c), jnp.float32)] * 2
        + [pltpu.VMEM((n, a_loc, rows, c), jnp.bfloat16), pltpu.SemaphoreType.DMA((8,))],
        compiler_params=middle,
        name="radial",
    )(got.reshape(n, a_loc, r_loc, theta, c), radial_taps, *vectors)
    if spread:
        joined, most, last = pl.pallas_call(
            join_kernel,
            out_shape=[jax.ShapeDtypeStruct((2 * SLOT * size + EXTRA, c), jnp.bfloat16) for size in (outer + 1, outer - 2, 1)],
            in_specs=[anywhere] + [vmem()] * (outer + 1),
            out_specs=[vmem()] * 3,
            compiler_params=small,
            cost_estimate=pl.CostEstimate(flops=10**10, bytes_accessed=2 * 10**7, transcendentals=0),
            name="join",
        )(mixed, *line, own, side)
        across = [move(most, 1, 1), move(last, 1, 1)]
        twin = move(joined, 2, 1)
    back = lax.all_to_all(mixed.reshape(axial, rows, c), "row", split_axis=0, concat_axis=0, tiled=True)
    normed = pl.pallas_call(
        axial_kernel,
        out_shape=jax.ShapeDtypeStruct((axial * rows, c), jnp.bfloat16),
        in_specs=[vmem()] * 3,
        out_specs=vmem(),
        scratch_shapes=[
            pltpu.VMEM((axial + axial_taps.shape[0] - 1, rows, c), jnp.float32),
            pltpu.VMEM((axial, rows, c), jnp.float32),
        ],
        compiler_params=middle,
        name="axial",
    )(back, axial_taps, consts)
    if spread:
        across, normed = lax.optimization_barrier((across, normed))
        blocks = across + [move(h, 2, 1) for h in across]
        partials = [
            pl.pallas_call(
                first_kernel,
                out_shape=jax.ShapeDtypeStruct((axial * rows, c), jnp.float32),
                in_specs=[vmem()] * 3,
                out_specs=vmem(),
                compiler_params=middle,
                name="first",
            )(normed, joined, twin)
        ]
    else:
        partials = []
    operands = partials + blocks
    return pl.pallas_call(
        partial(mlp_kernel, len(partials)),
        out_shape=jax.ShapeDtypeStruct(features.shape, jnp.bfloat16),
        in_specs=[vmem()] * (3 + len(operands)),
        out_specs=anywhere,
        scratch_shapes=[
            pltpu.VMEM((axial, rows, c), jnp.float32),
            pltpu.VMEM(features.shape, jnp.bfloat16),
            pltpu.SemaphoreType.DMA((2,)),
        ],
        compiler_params=large,
        name="mlp",
    )(normed, consts, features, *operands)


def solution(mesh):
    in_specs = (
        P("groups", "row", None, None),
        P(),
        P(),
        P(),
        P(),
        P(),
        P("row", None),
        P("row"),
        P("row", None),
        P(),
        P(),
    )
    out_specs = P("groups", "row", None, None)
    return jax.shard_map(partial(local, mesh.shape["row"]), mesh=mesh, in_specs=in_specs, out_specs=out_specs, check_vma=False)
```

```python
import math
from functools import partial

import jax
import jax.numpy as jnp
from jax import lax
from jax.experimental import pallas as pl
from jax.experimental.pallas import tpu as pltpu
from jax.sharding import PartitionSpec as P

SLOT = 64
PLANES = 32
EXTRA = 16


def vmem():
    return pl.BlockSpec(memory_space=pltpu.VMEM)


def pack_kernel(b_ref, w_in_ref, w_out_ref, block_ref):
    block_ref[0:SLOT, :] = w_in_ref[...]
    block_ref[SLOT : 2 * SLOT, :] = w_out_ref[...]
    bias = b_ref[...].astype(jnp.float32)[None, :]
    c = block_ref.shape[1]
    wide = jnp.concatenate([bias] * (c // SLOT), axis=1)
    block_ref[2 * SLOT :, :] = jnp.broadcast_to(wide, (EXTRA, c)).astype(block_ref.dtype)


def join_kernel(*refs):
    *blocks, all_ref, most_ref, last_ref = refs[1:]
    c = all_ref.shape[1]
    row = lax.broadcasted_iota(jnp.int32, (EXTRA, c), 0)
    for out_ref in (all_ref, most_ref):
        count = out_ref.shape[0] // (2 * SLOT)
        biases = jnp.zeros((EXTRA, c), jnp.float32)
        for i, block in enumerate(blocks[:count]):
            out_ref[2 * SLOT * i : 2 * SLOT * (i + 1), :] = block[0 : 2 * SLOT, :]
            biases = jnp.where(row == i, block[2 * SLOT :, :].astype(jnp.float32), biases)
        out_ref[2 * SLOT * count :, :] = biases.astype(out_ref.dtype)
    last_ref[...] = blocks[count][...]


def radial_kernel(x_ref, taps_ref, out_ref, even, odd, done, sems):
    n, a_loc, _, theta, c = x_ref.shape
    taps = taps_ref.shape[0]
    pad = (taps + 1) // 4
    zeros = jnp.zeros((pad, a_loc, 2 * theta, c), jnp.float32)
    even[0:pad] = zeros
    even[pad + n : 2 * pad + n] = zeros
    odd[0:pad] = zeros
    odd[pad + n - 1 : 2 * pad + n - 1] = zeros
    odd[2 * pad + n - 1 :] = zeros[:1]
    first = x_ref[:, :, 0].astype(jnp.float32)
    second = x_ref[:, :, 1].astype(jnp.float32)
    even[pad : pad + n, :, 0:theta] = first
    even[pad : pad + n, :, theta:] = second
    odd[pad : pad + n, :, 0:theta] = second
    odd[pad - 1 : pad + n - 1, :, theta:] = first

    block = 4

    def step(base, wanted):
        total = jnp.zeros((block, a_loc, 2 * theta, c), jnp.float32)
        for shift in wanted:
            k = shift + taps // 2
            source = even if shift % 2 == 0 else odd
            total = total + source[pl.ds(base + (pad + shift // 2), block)] * taps_ref[k : k + 1, :]
        done[pl.ds(base, block)] = total.astype(done.dtype)

    every = range(-(taps // 2), taps // 2 + 1)
    if n <= 8 * block:
        copies = []
        for base in range(0, n, block):
            step(base, [s for s in every if base + block - 1 + s // 2 >= -(s % 2) and base + s // 2 < n])
            part = pl.ds(base, block)
            copies.append(pltpu.make_async_copy(done.at[part], out_ref.at[part], sems.at[base // block]))
            copies[-1].start()
    else:
        pl.loop(0, n // block)(lambda i: step(i * block, every))
        copies = [pltpu.make_async_copy(done, out_ref, sems.at[0])]
        copies[0].start()
    for copy in copies:
        copy.wait()


def axial_kernel(z_ref, taps_ref, conv_b_ref, gain_ref, lnb_ref, out_ref, padded, summed):
    axial, rows, c = z_ref.shape
    taps = taps_ref.shape[0]
    half = taps // 2
    zeros = jnp.zeros((half, rows, c), jnp.float32)
    padded[0:half] = zeros
    padded[half + axial :] = zeros
    padded[half : half + axial] = z_ref[...].astype(jnp.float32)
    block = 8

    def conv(base, wanted):
        total = jnp.zeros((block, rows, c), jnp.float32)
        for k in wanted:
            total = total + padded[pl.ds(base + k, block)] * taps_ref[k : k + 1, :]
        summed[pl.ds(base, block)] = total

    if axial <= 8 * block:
        for base in range(0, axial, block):
            conv(base, [k for k in range(taps) if base + block - 1 + k >= half and base + k < half + axial])
    else:
        pl.loop(0, axial // block)(lambda i: conv(i * block, range(taps)))

    def norm(i, carry):
        v = (summed[pl.ds(i * PLANES, PLANES)] + conv_b_ref[...]).reshape(PLANES * rows, c)
        v = v.astype(jnp.bfloat16).astype(jnp.float32)
        mean = jnp.mean(v, axis=-1, keepdims=True)
        centred = v - mean
        var = jnp.mean(centred * centred, axis=-1, keepdims=True)
        normed = centred * lax.rsqrt(var + 1e-06) * gain_ref[...] + lnb_ref[...]
        at = pl.multiple_of(i * PLANES * rows, PLANES * rows)
        out_ref[pl.ds(at, PLANES * rows), :] = normed.astype(out_ref.dtype)
        return carry

    lax.fori_loop(0, axial // PLANES, norm, 0)


def hidden_sum(normed, blocks):
    c = normed.shape[1]
    per = c // SLOT
    lane_slot = lax.broadcasted_iota(jnp.int32, (1, c), 1) // SLOT
    slots = [(block, i) for block in blocks for i in range(block.shape[0] // (2 * SLOT))]
    total = None
    for g in range(0, len(slots), per):
        own = slots[g : g + per]
        w_in = jnp.concatenate([w[2 * SLOT * j : 2 * SLOT * j + SLOT, :] for w, j in own], axis=0)
        w_out = jnp.concatenate([w[2 * SLOT * j + SLOT : 2 * SLOT * (j + 1), :] for w, j in own], axis=0)
        bias = jnp.zeros((1, c), jnp.float32)
        for spot, (w, j) in enumerate(own):
            piece = w[w.shape[0] - EXTRA :, :].astype(jnp.float32)[j : j + 1]
            bias = jnp.where(lane_slot == spot, piece, bias)
        u = lax.dot_general(normed, w_in, (((1,), (1,)), ((), ())), preferred_element_type=jnp.float32)
        u = u + bias[:, : len(own) * SLOT]
        hidden = (0.5 * u * (1.0 + jnp.tanh(0.7978845608028654 * (u + 0.044715 * u * u * u)))).astype(jnp.bfloat16)
        part = jnp.dot(hidden, w_out, preferred_element_type=jnp.float32)
        total = part if total is None else total + part
    return total


def over_tokens(count, size, body):
    if count == size:
        body(0)
    else:
        pl.loop(0, count // size)(lambda i: body(pl.multiple_of(i * size, size)))


def first_kernel(normed_ref, *rest):
    *blocks, out_ref = rest
    size = PLANES * 8

    def part(at):
        out_ref[pl.ds(at, size), :] = hidden_sum(normed_ref[pl.ds(at, size), :], blocks)

    over_tokens(normed_ref.shape[0], size, part)


def mlp_kernel(partials, normed_ref, b_out_ref, scale_ref, feat_ref, *rest):
    *blocks, out_ref, branch, done, sems = rest
    axial, _, theta, c = feat_ref.shape
    rows = 2 * theta
    planes = PLANES // 2

    def mlp(at, size):
        tokens = pl.ds(at * rows, size * rows)
        total = hidden_sum(normed_ref[tokens, :], blocks[partials:])
        for partial_ref in blocks[:partials]:
            total = total + partial_ref[tokens, :]
        result = (scale_ref[...] * (total + b_out_ref[...])).astype(jnp.bfloat16).astype(jnp.float32)
        branch[pl.ds(at, size)] = result.reshape(size, rows, c)
        for r in range(2):
            got = branch[pl.ds(at, size), r * theta : (r + 1) * theta, :]
            done[pl.ds(at, size), r] = (feat_ref[pl.ds(at, size), r].astype(jnp.float32) + got).astype(done.dtype)

    copies = []
    if axial == PLANES:
        for i in range(2):
            mlp(i * planes, planes)
            part = pl.ds(i * planes, planes)
            copies.append(pltpu.make_async_copy(done.at[part], out_ref.at[part], sems.at[i]))
            copies[-1].start()
    else:
        pl.loop(0, axial // PLANES)(lambda i: mlp(pl.multiple_of(i * PLANES, PLANES), PLANES))
        copies.append(pltpu.make_async_copy(done, out_ref, sems.at[0]))
        copies[-1].start()
    for copy in copies:
        copy.wait()


def digits(n):
    chips = n // 2
    inner = 1
    while inner * inner * 4 <= chips:
        inner *= 2
    return chips // inner, inner, 2


def local(n, features, axial_taps, radial_taps, conv_bias, ln_gain, ln_bias, w_in, b_in, w_out, b_out, layer_scale):
    axial, r_loc, theta, c = features.shape
    rows = r_loc * theta
    hid_loc = w_in.shape[0]
    a_loc = axial // n
    outer, inner, _ = digits(n)
    spread = hid_loc == SLOT and n == 4 * outer and 2 < outer <= EXTRA
    small, middle, large = (pltpu.CompilerParams(vmem_limit_bytes=mib * 1024 * 1024) for mib in (2, 12, 24))
    anywhere = pl.BlockSpec(memory_space=pl.ANY)

    def move(piece, digit, by):
        stride = math.prod(digits(n)[digit + 1 :])
        return lax.ppermute(piece, "row", [(i, i ^ (by * stride)) for i in range(n)])

    if spread:
        own = pl.pallas_call(
            pack_kernel,
            out_shape=jax.ShapeDtypeStruct((2 * SLOT + EXTRA, c), jnp.bfloat16),
            in_specs=[vmem()] * 3,
            out_specs=vmem(),
            compiler_params=small,
            name="pack",
        )(b_in, w_in, w_out)
        line = [move(own, 0, by) for by in range(1, outer)]
        side = move(own, 1, 1)
    else:
        w_all = lax.all_gather(w_in, "row", axis=0, tiled=True).reshape(-1, SLOT, c)
        o_all = lax.all_gather(w_out, "row", axis=0, tiled=True).reshape(-1, SLOT, c)
        b_all = jnp.tile(lax.all_gather(b_in, "row", axis=0, tiled=True).reshape(-1, SLOT), (1, c // SLOT))
        w_all = jnp.concatenate([w_all, o_all], axis=1).reshape(-1, c)
        blocks = [jnp.concatenate([w_all, jnp.pad(b_all, ((0, EXTRA - b_all.shape[0]), (0, 0)))], axis=0)]

    got = lax.all_to_all(features, "row", split_axis=0, concat_axis=0, tiled=True)
    pad = (radial_taps.shape[0] + 1) // 4
    mixed = pl.pallas_call(
        radial_kernel,
        out_shape=jax.ShapeDtypeStruct((n, a_loc, rows, c), jnp.bfloat16),
        in_specs=[vmem()] * 2,
        out_specs=anywhere,
        scratch_shapes=[pltpu.VMEM((n + 2 * pad, a_loc, rows, c), jnp.float32)] * 2
        + [pltpu.VMEM((n, a_loc, rows, c), jnp.bfloat16), pltpu.SemaphoreType.DMA((8,))],
        compiler_params=middle,
        name="radial",
    )(got.reshape(n, a_loc, r_loc, theta, c), radial_taps)
    if spread:
        joined, most, last = pl.pallas_call(
            join_kernel,
            out_shape=[jax.ShapeDtypeStruct((2 * SLOT * size + EXTRA, c), jnp.bfloat16) for size in (outer + 1, outer - 2, 1)],
            in_specs=[anywhere] + [vmem()] * (outer + 1),
            out_specs=[vmem()] * 3,
            compiler_params=small,
            cost_estimate=pl.CostEstimate(flops=10**10, bytes_accessed=2 * 10**7, transcendentals=0),
            name="join",
        )(mixed, *line, own, side)
        across = [move(most, 1, 1), move(last, 1, 1)]
        twin = move(joined, 2, 1)
    back = lax.all_to_all(mixed.reshape(axial, rows, c), "row", split_axis=0, concat_axis=0, tiled=True)
    normed = pl.pallas_call(
        axial_kernel,
        out_shape=jax.ShapeDtypeStruct((axial * rows, c), jnp.bfloat16),
        in_specs=[vmem()] * 5,
        out_specs=vmem(),
        scratch_shapes=[
            pltpu.VMEM((axial + axial_taps.shape[0] - 1, rows, c), jnp.float32),
            pltpu.VMEM((axial, rows, c), jnp.float32),
        ],
        compiler_params=middle,
        name="axial",
    )(back, axial_taps, conv_bias[None, :], ln_gain[None, :], ln_bias[None, :])
    if spread:
        across, normed = lax.optimization_barrier((across, normed))
        blocks = [move(h, 2, 1) for h in across]
        partials = [
            pl.pallas_call(
                first_kernel,
                out_shape=jax.ShapeDtypeStruct((axial * rows, c), jnp.float32),
                in_specs=[vmem()] * 5,
                out_specs=vmem(),
                compiler_params=middle,
                name="first",
            )(normed, joined, twin, *across)
        ]
    else:
        partials = []
    operands = partials + blocks
    return pl.pallas_call(
        partial(mlp_kernel, len(partials)),
        out_shape=jax.ShapeDtypeStruct(features.shape, jnp.bfloat16),
        in_specs=[vmem()] * (4 + len(operands)),
        out_specs=anywhere,
        scratch_shapes=[
            pltpu.VMEM((axial, rows, c), jnp.float32),
            pltpu.VMEM(features.shape, jnp.bfloat16),
            pltpu.SemaphoreType.DMA((2,)),
        ],
        compiler_params=large,
        name="mlp",
    )(normed, b_out[None, :], layer_scale[None, :], features, *operands)


def solution(mesh):
    in_specs = (
        P("groups", "row", None, None),
        P(),
        P(),
        P(),
        P(),
        P(),
        P("row", None),
        P("row"),
        P("row", None),
        P(),
        P(),
    )
    out_specs = P("groups", "row", None, None)
    return jax.shard_map(partial(local, mesh.shape["row"]), mesh=mesh, in_specs=in_specs, out_specs=out_specs, check_vma=False)
```

```python
import math
from functools import partial

import jax
import jax.numpy as jnp
from jax import lax
from jax.experimental import pallas as pl
from jax.experimental.pallas import tpu as pltpu
from jax.sharding import PartitionSpec as P

SLOT = 64
PLANES = 32
EXTRA = 16


def vmem():
    return pl.BlockSpec(memory_space=pltpu.VMEM)


def pack_kernel(b_ref, w_in_ref, w_out_ref, *rest):
    *vectors, block_ref, consts_ref = rest
    block_ref[0:SLOT, :] = w_in_ref[...]
    block_ref[SLOT : 2 * SLOT, :] = w_out_ref[...]
    bias = b_ref[...].astype(jnp.float32)[None, :]
    c = block_ref.shape[1]
    wide = jnp.concatenate([bias] * (c // SLOT), axis=1)
    block_ref[2 * SLOT :, :] = jnp.broadcast_to(wide, (EXTRA, c)).astype(block_ref.dtype)
    for i, vector in enumerate(vectors):
        consts_ref[i : i + 1, :] = vector[...]


def join_kernel(*refs):
    *blocks, all_ref, most_ref, last_ref = refs[1:]
    c = all_ref.shape[1]
    row = lax.broadcasted_iota(jnp.int32, (EXTRA, c), 0)
    for out_ref in (all_ref, most_ref):
        count = out_ref.shape[0] // (2 * SLOT)
        biases = jnp.zeros((EXTRA, c), jnp.float32)
        for i, block in enumerate(blocks[:count]):
            out_ref[2 * SLOT * i : 2 * SLOT * (i + 1), :] = block[0 : 2 * SLOT, :]
            biases = jnp.where(row == i, block[2 * SLOT :, :].astype(jnp.float32), biases)
        out_ref[2 * SLOT * count :, :] = biases.astype(out_ref.dtype)
    last_ref[...] = blocks[count][...]


def radial_kernel(x_ref, taps_ref, out_ref, even, odd, done, sems):
    n, a_loc, _, theta, c = x_ref.shape
    taps = taps_ref.shape[0]
    pad = (taps + 1) // 4
    zeros = jnp.zeros((pad, a_loc, 2 * theta, c), jnp.float32)
    even[0:pad] = zeros
    even[pad + n : 2 * pad + n] = zeros
    odd[0:pad] = zeros
    odd[pad + n - 1 : 2 * pad + n - 1] = zeros
    odd[2 * pad + n - 1 :] = zeros[:1]
    first = x_ref[:, :, 0].astype(jnp.float32)
    second = x_ref[:, :, 1].astype(jnp.float32)
    even[pad : pad + n, :, 0:theta] = first
    even[pad : pad + n, :, theta:] = second
    odd[pad : pad + n, :, 0:theta] = second
    odd[pad - 1 : pad + n - 1, :, theta:] = first

    block = 4

    def step(base, wanted):
        total = jnp.zeros((block, a_loc, 2 * theta, c), jnp.float32)
        for shift in wanted:
            k = shift + taps // 2
            source = even if shift % 2 == 0 else odd
            total = total + source[pl.ds(base + (pad + shift // 2), block)] * taps_ref[k : k + 1, :]
        done[pl.ds(base, block)] = total.astype(done.dtype)

    every = range(-(taps // 2), taps // 2 + 1)
    if n <= 8 * block:
        copies = []
        for base in range(0, n, block):
            step(base, [s for s in every if base + block - 1 + s // 2 >= -(s % 2) and base + s // 2 < n])
            part = pl.ds(base, block)
            copies.append(pltpu.make_async_copy(done.at[part], out_ref.at[part], sems.at[base // block]))
            copies[-1].start()
    else:
        pl.loop(0, n // block)(lambda i: step(i * block, every))
        copies = [pltpu.make_async_copy(done, out_ref, sems.at[0])]
        copies[0].start()
    for copy in copies:
        copy.wait()


def axial_kernel(z_ref, taps_ref, consts_ref, out_ref, padded, summed):
    axial, rows, c = z_ref.shape
    taps = taps_ref.shape[0]
    half = taps // 2
    zeros = jnp.zeros((half, rows, c), jnp.float32)
    padded[0:half] = zeros
    padded[half + axial :] = zeros
    padded[half : half + axial] = z_ref[...].astype(jnp.float32)
    block = 8

    def conv(base, wanted):
        total = jnp.zeros((block, rows, c), jnp.float32)
        for k in wanted:
            total = total + padded[pl.ds(base + k, block)] * taps_ref[k : k + 1, :]
        summed[pl.ds(base, block)] = total

    if axial <= 8 * block:
        for base in range(0, axial, block):
            conv(base, [k for k in range(taps) if base + block - 1 + k >= half and base + k < half + axial])
    else:
        pl.loop(0, axial // block)(lambda i: conv(i * block, range(taps)))

    def norm(i, carry):
        v = (summed[pl.ds(i * PLANES, PLANES)] + consts_ref[0 : 1, :]).reshape(PLANES * rows, c)
        v = v.astype(jnp.bfloat16).astype(jnp.float32)
        mean = jnp.mean(v, axis=-1, keepdims=True)
        centred = v - mean
        var = jnp.mean(centred * centred, axis=-1, keepdims=True)
        normed = centred * lax.rsqrt(var + 1e-06) * consts_ref[1 : 2, :] + consts_ref[2 : 3, :]
        at = pl.multiple_of(i * PLANES * rows, PLANES * rows)
        out_ref[pl.ds(at, PLANES * rows), :] = normed.astype(out_ref.dtype)
        return carry

    lax.fori_loop(0, axial // PLANES, norm, 0)


def hidden_sum(normed, blocks):
    c = normed.shape[1]
    per = c // SLOT
    lane_slot = lax.broadcasted_iota(jnp.int32, (1, c), 1) // SLOT
    slots = [(block, i) for block in blocks for i in range(block.shape[0] // (2 * SLOT))]
    total = None
    for g in range(0, len(slots), per):
        own = slots[g : g + per]
        w_in = jnp.concatenate([w[2 * SLOT * j : 2 * SLOT * j + SLOT, :] for w, j in own], axis=0)
        w_out = jnp.concatenate([w[2 * SLOT * j + SLOT : 2 * SLOT * (j + 1), :] for w, j in own], axis=0)
        bias = jnp.zeros((1, c), jnp.float32)
        for spot, (w, j) in enumerate(own):
            piece = w[w.shape[0] - EXTRA :, :].astype(jnp.float32)[j : j + 1]
            bias = jnp.where(lane_slot == spot, piece, bias)
        u = lax.dot_general(normed, w_in, (((1,), (1,)), ((), ())), preferred_element_type=jnp.float32)
        u = u + bias[:, : len(own) * SLOT]
        hidden = (0.5 * u * (1.0 + jnp.tanh(0.7978845608028654 * (u + 0.044715 * u * u * u)))).astype(jnp.bfloat16)
        part = jnp.dot(hidden, w_out, preferred_element_type=jnp.float32)
        total = part if total is None else total + part
    return total


def over_tokens(count, size, body):
    if count == size:
        body(0)
    else:
        pl.loop(0, count // size)(lambda i: body(pl.multiple_of(i * size, size)))


def first_kernel(normed_ref, *rest):
    *blocks, out_ref = rest
    size = PLANES * 8

    def part(at):
        out_ref[pl.ds(at, size), :] = hidden_sum(normed_ref[pl.ds(at, size), :], blocks)

    over_tokens(normed_ref.shape[0], size, part)


def mlp_kernel(partials, normed_ref, consts_ref, feat_ref, *rest):
    *blocks, out_ref, branch, done, sems = rest
    axial, _, theta, c = feat_ref.shape
    rows = 2 * theta
    planes = PLANES // 2

    def mlp(at, size):
        tokens = pl.ds(at * rows, size * rows)
        total = hidden_sum(normed_ref[tokens, :], blocks[partials:])
        for partial_ref in blocks[:partials]:
            total = total + partial_ref[tokens, :]
        result = (consts_ref[4 : 5, :] * (total + consts_ref[3 : 4, :])).astype(jnp.bfloat16).astype(jnp.float32)
        branch[pl.ds(at, size)] = result.reshape(size, rows, c)
        for r in range(2):
            got = branch[pl.ds(at, size), r * theta : (r + 1) * theta, :]
            done[pl.ds(at, size), r] = (feat_ref[pl.ds(at, size), r].astype(jnp.float32) + got).astype(done.dtype)

    copies = []
    if axial == PLANES:
        for i in range(2):
            mlp(i * planes, planes)
            part = pl.ds(i * planes, planes)
            copies.append(pltpu.make_async_copy(done.at[part], out_ref.at[part], sems.at[i]))
            copies[-1].start()
    else:
        pl.loop(0, axial // PLANES)(lambda i: mlp(pl.multiple_of(i * PLANES, PLANES), PLANES))
        copies.append(pltpu.make_async_copy(done, out_ref, sems.at[0]))
        copies[-1].start()
    for copy in copies:
        copy.wait()


def digits(n):
    chips = n // 2
    inner = 1
    while inner * inner * 4 <= chips:
        inner *= 2
    return chips // inner, inner, 2


def local(n, features, axial_taps, radial_taps, conv_bias, ln_gain, ln_bias, w_in, b_in, w_out, b_out, layer_scale):
    axial, r_loc, theta, c = features.shape
    rows = r_loc * theta
    hid_loc = w_in.shape[0]
    a_loc = axial // n
    outer, inner, _ = digits(n)
    spread = hid_loc == SLOT and n == 4 * outer and 2 < outer <= EXTRA
    small, middle, large = (pltpu.CompilerParams(vmem_limit_bytes=mib * 1024 * 1024) for mib in (2, 12, 24))
    anywhere = pl.BlockSpec(memory_space=pl.ANY)

    def move(piece, digit, by):
        stride = math.prod(digits(n)[digit + 1 :])
        return lax.ppermute(piece, "row", [(i, i ^ (by * stride)) for i in range(n)])

    vectors = [v[None, :] for v in (conv_bias, ln_gain, ln_bias, b_out, layer_scale)]
    if spread:
        own, consts = pl.pallas_call(
            pack_kernel,
            out_shape=[
                jax.ShapeDtypeStruct((2 * SLOT + EXTRA, c), jnp.bfloat16),
                jax.ShapeDtypeStruct((8, c), jnp.float32),
            ],
            in_specs=[vmem()] * 8,
            out_specs=[vmem()] * 2,
            compiler_params=small,
            name="pack",
        )(b_in, w_in, w_out, *vectors)
        line = [move(own, 0, by) for by in range(1, outer)]
        side = move(own, 1, 1)
    else:
        consts = jnp.concatenate(vectors + [jnp.zeros((3, c), jnp.float32)], axis=0)
        w_all = lax.all_gather(w_in, "row", axis=0, tiled=True).reshape(-1, SLOT, c)
        o_all = lax.all_gather(w_out, "row", axis=0, tiled=True).reshape(-1, SLOT, c)
        b_all = jnp.tile(lax.all_gather(b_in, "row", axis=0, tiled=True).reshape(-1, SLOT), (1, c // SLOT))
        w_all = jnp.concatenate([w_all, o_all], axis=1).reshape(-1, c)
        blocks = [jnp.concatenate([w_all, jnp.pad(b_all, ((0, EXTRA - b_all.shape[0]), (0, 0)))], axis=0)]

    got = lax.all_to_all(features, "row", split_axis=0, concat_axis=0, tiled=True)
    pad = (radial_taps.shape[0] + 1) // 4
    mixed = pl.pallas_call(
        radial_kernel,
        out_shape=jax.ShapeDtypeStruct((n, a_loc, rows, c), jnp.bfloat16),
        in_specs=[vmem()] * 2,
        out_specs=anywhere,
        scratch_shapes=[pltpu.VMEM((n + 2 * pad, a_loc, rows, c), jnp.float32)] * 2
        + [pltpu.VMEM((n, a_loc, rows, c), jnp.bfloat16), pltpu.SemaphoreType.DMA((8,))],
        compiler_params=middle,
        name="radial",
    )(got.reshape(n, a_loc, r_loc, theta, c), radial_taps)
    if spread:
        joined, most, last = pl.pallas_call(
            join_kernel,
            out_shape=[jax.ShapeDtypeStruct((2 * SLOT * size + EXTRA, c), jnp.bfloat16) for size in (outer + 1, outer - 2, 1)],
            in_specs=[anywhere] + [vmem()] * (outer + 1),
            out_specs=[vmem()] * 3,
            compiler_params=small,
            cost_estimate=pl.CostEstimate(flops=10**10, bytes_accessed=2 * 10**7, transcendentals=0),
            name="join",
        )(mixed, *line, own, side)
        across = [move(most, 1, 1), move(last, 1, 1)]
        twin = move(joined, 2, 1)
    back = lax.all_to_all(mixed.reshape(axial, rows, c), "row", split_axis=0, concat_axis=0, tiled=True)
    normed = pl.pallas_call(
        axial_kernel,
        out_shape=jax.ShapeDtypeStruct((axial * rows, c), jnp.bfloat16),
        in_specs=[vmem()] * 3,
        out_specs=vmem(),
        scratch_shapes=[
            pltpu.VMEM((axial + axial_taps.shape[0] - 1, rows, c), jnp.float32),
            pltpu.VMEM((axial, rows, c), jnp.float32),
        ],
        compiler_params=middle,
        name="axial",
    )(back, axial_taps, consts)
    if spread:
        across, normed = lax.optimization_barrier((across, normed))
        blocks = [move(h, 2, 1) for h in across]
        partials = [
            pl.pallas_call(
                first_kernel,
                out_shape=jax.ShapeDtypeStruct((axial * rows, c), jnp.float32),
                in_specs=[vmem()] * 5,
                out_specs=vmem(),
                compiler_params=middle,
                name="first",
            )(normed, joined, twin, *across)
        ]
    else:
        partials = []
    operands = partials + blocks
    return pl.pallas_call(
        partial(mlp_kernel, len(partials)),
        out_shape=jax.ShapeDtypeStruct(features.shape, jnp.bfloat16),
        in_specs=[vmem()] * (3 + len(operands)),
        out_specs=anywhere,
        scratch_shapes=[
            pltpu.VMEM((axial, rows, c), jnp.float32),
            pltpu.VMEM(features.shape, jnp.bfloat16),
            pltpu.SemaphoreType.DMA((2,)),
        ],
        compiler_params=large,
        name="mlp",
    )(normed, consts, features, *operands)


def solution(mesh):
    in_specs = (
        P("groups", "row", None, None),
        P(),
        P(),
        P(),
        P(),
        P(),
        P("row", None),
        P("row"),
        P("row", None),
        P(),
        P(),
    )
    out_specs = P("groups", "row", None, None)
    return jax.shard_map(partial(local, mesh.shape["row"]), mesh=mesh, in_specs=in_specs, out_specs=out_specs, check_vma=False)
```

```python
import math
from functools import partial

import jax
import jax.numpy as jnp
from jax import lax
from jax.experimental import pallas as pl
from jax.experimental.pallas import tpu as pltpu
from jax.sharding import PartitionSpec as P

SLOT = 64
PLANES = 32
EXTRA = 16


def vmem():
    return pl.BlockSpec(memory_space=pltpu.VMEM)


def pack_kernel(b_ref, w_in_ref, w_out_ref, *rest):
    *vectors, block_ref, consts_ref = rest
    block_ref[0:SLOT, :] = w_in_ref[...]
    block_ref[SLOT : 2 * SLOT, :] = w_out_ref[...]
    bias = b_ref[...].astype(jnp.float32)[None, :]
    c = block_ref.shape[1]
    wide = jnp.concatenate([bias] * (c // SLOT), axis=1)
    block_ref[2 * SLOT :, :] = jnp.broadcast_to(wide, (EXTRA, c)).astype(block_ref.dtype)
    for i, vector in enumerate(vectors):
        consts_ref[i : i + 1, :] = vector[...]


def join_kernel(*refs):
    *blocks, all_ref, most_ref = refs[1:]
    c = all_ref.shape[1]
    row = lax.broadcasted_iota(jnp.int32, (EXTRA, c), 0)
    for out_ref in (all_ref, most_ref):
        count = out_ref.shape[0] // (2 * SLOT)
        biases = jnp.zeros((EXTRA, c), jnp.float32)
        for i, block in enumerate(blocks[:count]):
            out_ref[2 * SLOT * i : 2 * SLOT * (i + 1), :] = block[0 : 2 * SLOT, :]
            biases = jnp.where(row == i, block[2 * SLOT :, :].astype(jnp.float32), biases)
        out_ref[2 * SLOT * count :, :] = biases.astype(out_ref.dtype)


def radial_kernel(x_ref, taps_ref, out_ref, even, odd, done, sems):
    n, a_loc, _, theta, c = x_ref.shape
    taps = taps_ref.shape[0]
    pad = (taps + 1) // 4
    zeros = jnp.zeros((pad, a_loc, 2 * theta, c), jnp.float32)
    even[0:pad] = zeros
    even[pad + n : 2 * pad + n] = zeros
    odd[0:pad] = zeros
    odd[pad + n - 1 : 2 * pad + n - 1] = zeros
    odd[2 * pad + n - 1 :] = zeros[:1]
    first = x_ref[:, :, 0].astype(jnp.float32)
    second = x_ref[:, :, 1].astype(jnp.float32)
    even[pad : pad + n, :, 0:theta] = first
    even[pad : pad + n, :, theta:] = second
    odd[pad : pad + n, :, 0:theta] = second
    odd[pad - 1 : pad + n - 1, :, theta:] = first

    block = 4

    def step(base, wanted):
        total = jnp.zeros((block, a_loc, 2 * theta, c), jnp.float32)
        for shift in wanted:
            k = shift + taps // 2
            source = even if shift % 2 == 0 else odd
            total = total + source[pl.ds(base + (pad + shift // 2), block)] * taps_ref[k : k + 1, :]
        done[pl.ds(base, block)] = total.astype(done.dtype)

    every = range(-(taps // 2), taps // 2 + 1)
    if n <= 8 * block:
        copies = []
        for base in range(0, n, block):
            step(base, [s for s in every if base + block - 1 + s // 2 >= -(s % 2) and base + s // 2 < n])
            part = pl.ds(base, block)
            copies.append(pltpu.make_async_copy(done.at[part], out_ref.at[part], sems.at[base // block]))
            copies[-1].start()
    else:
        pl.loop(0, n // block)(lambda i: step(i * block, every))
        copies = [pltpu.make_async_copy(done, out_ref, sems.at[0])]
        copies[0].start()
    for copy in copies:
        copy.wait()


def axial_kernel(z_ref, taps_ref, consts_ref, out_ref, padded, summed):
    axial, rows, c = z_ref.shape
    taps = taps_ref.shape[0]
    half = taps // 2
    zeros = jnp.zeros((half, rows, c), jnp.float32)
    padded[0:half] = zeros
    padded[half + axial :] = zeros
    padded[half : half + axial] = z_ref[...].astype(jnp.float32)
    block = 8

    def conv(base, wanted):
        total = jnp.zeros((block, rows, c), jnp.float32)
        for k in wanted:
            total = total + padded[pl.ds(base + k, block)] * taps_ref[k : k + 1, :]
        summed[pl.ds(base, block)] = total

    if axial <= 8 * block:
        for base in range(0, axial, block):
            conv(base, [k for k in range(taps) if base + block - 1 + k >= half and base + k < half + axial])
    else:
        pl.loop(0, axial // block)(lambda i: conv(i * block, range(taps)))

    def norm(i, carry):
        v = (summed[pl.ds(i * PLANES, PLANES)] + consts_ref[0 : 1, :]).reshape(PLANES * rows, c)
        v = v.astype(jnp.bfloat16).astype(jnp.float32)
        mean = jnp.mean(v, axis=-1, keepdims=True)
        centred = v - mean
        var = jnp.mean(centred * centred, axis=-1, keepdims=True)
        normed = centred * lax.rsqrt(var + 1e-06) * consts_ref[1 : 2, :] + consts_ref[2 : 3, :]
        at = pl.multiple_of(i * PLANES * rows, PLANES * rows)
        out_ref[pl.ds(at, PLANES * rows), :] = normed.astype(out_ref.dtype)
        return carry

    lax.fori_loop(0, axial // PLANES, norm, 0)


def hidden_sum(normed, blocks):
    c = normed.shape[1]
    per = c // SLOT
    lane_slot = lax.broadcasted_iota(jnp.int32, (1, c), 1) // SLOT
    slots = [(block, i) for block in blocks for i in range(block.shape[0] // (2 * SLOT))]
    total = None
    for g in range(0, len(slots), per):
        own = slots[g : g + per]
        w_in = jnp.concatenate([w[2 * SLOT * j : 2 * SLOT * j + SLOT, :] for w, j in own], axis=0)
        w_out = jnp.concatenate([w[2 * SLOT * j + SLOT : 2 * SLOT * (j + 1), :] for w, j in own], axis=0)
        bias = jnp.zeros((1, c), jnp.float32)
        for spot, (w, j) in enumerate(own):
            piece = w[w.shape[0] - EXTRA :, :].astype(jnp.float32)[j : j + 1]
            bias = jnp.where(lane_slot == spot, piece, bias)
        u = lax.dot_general(normed, w_in, (((1,), (1,)), ((), ())), preferred_element_type=jnp.float32)
        u = u + bias[:, : len(own) * SLOT]
        hidden = (0.5 * u * (1.0 + jnp.tanh(0.7978845608028654 * (u + 0.044715 * u * u * u)))).astype(jnp.bfloat16)
        part = jnp.dot(hidden, w_out, preferred_element_type=jnp.float32)
        total = part if total is None else total + part
    return total


def over_tokens(count, size, body):
    if count == size:
        body(0)
    else:
        pl.loop(0, count // size)(lambda i: body(pl.multiple_of(i * size, size)))


def first_kernel(normed_ref, *rest):
    *blocks, out_ref = rest
    size = PLANES * 8

    def part(at):
        out_ref[pl.ds(at, size), :] = hidden_sum(normed_ref[pl.ds(at, size), :], blocks)

    over_tokens(normed_ref.shape[0], size, part)


def mlp_kernel(partials, normed_ref, consts_ref, feat_ref, *rest):
    *blocks, out_ref, branch, done, sems = rest
    axial, _, theta, c = feat_ref.shape
    rows = 2 * theta
    planes = PLANES // 2

    def mlp(at, size):
        tokens = pl.ds(at * rows, size * rows)
        total = hidden_sum(normed_ref[tokens, :], blocks[partials:])
        for partial_ref in blocks[:partials]:
            total = total + partial_ref[tokens, :]
        result = (consts_ref[4 : 5, :] * (total + consts_ref[3 : 4, :])).astype(jnp.bfloat16).astype(jnp.float32)
        branch[pl.ds(at, size)] = result.reshape(size, rows, c)
        for r in range(2):
            got = branch[pl.ds(at, size), r * theta : (r + 1) * theta, :]
            done[pl.ds(at, size), r] = (feat_ref[pl.ds(at, size), r].astype(jnp.float32) + got).astype(done.dtype)

    copies = []
    if axial == PLANES:
        for i in range(2):
            mlp(i * planes, planes)
            part = pl.ds(i * planes, planes)
            copies.append(pltpu.make_async_copy(done.at[part], out_ref.at[part], sems.at[i]))
            copies[-1].start()
    else:
        pl.loop(0, axial // PLANES)(lambda i: mlp(pl.multiple_of(i * PLANES, PLANES), PLANES))
        copies.append(pltpu.make_async_copy(done, out_ref, sems.at[0]))
        copies[-1].start()
    for copy in copies:
        copy.wait()


def digits(n):
    chips = n // 2
    inner = 1
    while inner * inner * 4 <= chips:
        inner *= 2
    return chips // inner, inner, 2


def local(n, features, axial_taps, radial_taps, conv_bias, ln_gain, ln_bias, w_in, b_in, w_out, b_out, layer_scale):
    axial, r_loc, theta, c = features.shape
    rows = r_loc * theta
    hid_loc = w_in.shape[0]
    a_loc = axial // n
    outer, inner, _ = digits(n)
    spread = hid_loc == SLOT and n == 4 * outer and 2 < outer <= EXTRA
    small, middle, large = (pltpu.CompilerParams(vmem_limit_bytes=mib * 1024 * 1024) for mib in (2, 12, 24))
    anywhere = pl.BlockSpec(memory_space=pl.ANY)

    def move(piece, digit, by):
        stride = math.prod(digits(n)[digit + 1 :])
        return lax.ppermute(piece, "row", [(i, i ^ (by * stride)) for i in range(n)])

    vectors = [v[None, :] for v in (conv_bias, ln_gain, ln_bias, b_out, layer_scale)]
    if spread:
        own, consts = pl.pallas_call(
            pack_kernel,
            out_shape=[
                jax.ShapeDtypeStruct((2 * SLOT + EXTRA, c), jnp.bfloat16),
                jax.ShapeDtypeStruct((8, c), jnp.float32),
            ],
            in_specs=[vmem()] * 8,
            out_specs=[vmem()] * 2,
            compiler_params=small,
            name="pack",
        )(b_in, w_in, w_out, *vectors)
        line = [move(own, 0, by) for by in range(1, outer)]
        side = move(own, 1, 1)
    else:
        consts = jnp.concatenate(vectors + [jnp.zeros((3, c), jnp.float32)], axis=0)
        w_all = lax.all_gather(w_in, "row", axis=0, tiled=True).reshape(-1, SLOT, c)
        o_all = lax.all_gather(w_out, "row", axis=0, tiled=True).reshape(-1, SLOT, c)
        b_all = jnp.tile(lax.all_gather(b_in, "row", axis=0, tiled=True).reshape(-1, SLOT), (1, c // SLOT))
        w_all = jnp.concatenate([w_all, o_all], axis=1).reshape(-1, c)
        blocks = [jnp.concatenate([w_all, jnp.pad(b_all, ((0, EXTRA - b_all.shape[0]), (0, 0)))], axis=0)]

    got = lax.all_to_all(features, "row", split_axis=0, concat_axis=0, tiled=True)
    pad = (radial_taps.shape[0] + 1) // 4
    mixed = pl.pallas_call(
        radial_kernel,
        out_shape=jax.ShapeDtypeStruct((n, a_loc, rows, c), jnp.bfloat16),
        in_specs=[vmem()] * 2,
        out_specs=anywhere,
        scratch_shapes=[pltpu.VMEM((n + 2 * pad, a_loc, rows, c), jnp.float32)] * 2
        + [pltpu.VMEM((n, a_loc, rows, c), jnp.bfloat16), pltpu.SemaphoreType.DMA((8,))],
        compiler_params=middle,
        name="radial",
    )(got.reshape(n, a_loc, r_loc, theta, c), radial_taps)
    if spread:
        joined, most = pl.pallas_call(
            join_kernel,
            out_shape=[jax.ShapeDtypeStruct((2 * SLOT * size + EXTRA, c), jnp.bfloat16) for size in (outer + 1, outer - 2)],
            in_specs=[anywhere] + [vmem()] * (outer + 1),
            out_specs=[vmem()] * 2,
            compiler_params=small,
            cost_estimate=pl.CostEstimate(flops=10**10, bytes_accessed=2 * 10**7, transcendentals=0),
            name="join",
        )(mixed, *line[1:], line[0], own, side)
        across = [move(most, 1, 1), move(side, 0, 1)]
        twin = move(joined, 2, 1)
    back = lax.all_to_all(mixed.reshape(axial, rows, c), "row", split_axis=0, concat_axis=0, tiled=True)
    normed = pl.pallas_call(
        axial_kernel,
        out_shape=jax.ShapeDtypeStruct((axial * rows, c), jnp.bfloat16),
        in_specs=[vmem()] * 3,
        out_specs=vmem(),
        scratch_shapes=[
            pltpu.VMEM((axial + axial_taps.shape[0] - 1, rows, c), jnp.float32),
            pltpu.VMEM((axial, rows, c), jnp.float32),
        ],
        compiler_params=middle,
        name="axial",
    )(back, axial_taps, consts)
    if spread:
        across, normed = lax.optimization_barrier((across, normed))
        blocks = [move(h, 2, 1) for h in across]
        partials = [
            pl.pallas_call(
                first_kernel,
                out_shape=jax.ShapeDtypeStruct((axial * rows, c), jnp.float32),
                in_specs=[vmem()] * 5,
                out_specs=vmem(),
                compiler_params=middle,
                name="first",
            )(normed, joined, twin, *across)
        ]
    else:
        partials = []
    operands = partials + blocks
    return pl.pallas_call(
        partial(mlp_kernel, len(partials)),
        out_shape=jax.ShapeDtypeStruct(features.shape, jnp.bfloat16),
        in_specs=[vmem()] * (3 + len(operands)),
        out_specs=anywhere,
        scratch_shapes=[
            pltpu.VMEM((axial, rows, c), jnp.float32),
            pltpu.VMEM(features.shape, jnp.bfloat16),
            pltpu.SemaphoreType.DMA((2,)),
        ],
        compiler_params=large,
        name="mlp",
    )(normed, consts, features, *operands)


def solution(mesh):
    in_specs = (
        P("groups", "row", None, None),
        P(),
        P(),
        P(),
        P(),
        P(),
        P("row", None),
        P("row"),
        P("row", None),
        P(),
        P(),
    )
    out_specs = P("groups", "row", None, None)
    return jax.shard_map(partial(local, mesh.shape["row"]), mesh=mesh, in_specs=in_specs, out_specs=out_specs, check_vma=False)
```

```python
import math
from functools import partial

import jax
import jax.numpy as jnp
from jax import lax
from jax.experimental import pallas as pl
from jax.experimental.pallas import tpu as pltpu
from jax.sharding import PartitionSpec as P

SLOT = 64
PLANES = 32
EXTRA = 16


def vmem():
    return pl.BlockSpec(memory_space=pltpu.VMEM)


def pack_kernel(b_ref, w_in_ref, w_out_ref, *rest):
    *vectors, block_ref, consts_ref = rest
    block_ref[0:SLOT, :] = w_in_ref[...]
    block_ref[SLOT : 2 * SLOT, :] = w_out_ref[...]
    bias = b_ref[...].astype(jnp.float32)[None, :]
    c = block_ref.shape[1]
    wide = jnp.concatenate([bias] * (c // SLOT), axis=1)
    block_ref[2 * SLOT :, :] = jnp.broadcast_to(wide, (EXTRA, c)).astype(block_ref.dtype)
    for i, vector in enumerate(vectors):
        consts_ref[i : i + 1, :] = vector[...]


def join_kernel(*refs):
    *blocks, all_ref, line_ref = refs[1:]
    c = all_ref.shape[1]
    row = lax.broadcasted_iota(jnp.int32, (EXTRA, c), 0)
    for out_ref in (all_ref, line_ref):
        count = out_ref.shape[0] // (2 * SLOT)
        biases = jnp.zeros((EXTRA, c), jnp.float32)
        for i, block in enumerate(blocks[:count]):
            out_ref[2 * SLOT * i : 2 * SLOT * (i + 1), :] = block[0 : 2 * SLOT, :]
            biases = jnp.where(row == i, block[2 * SLOT :, :].astype(jnp.float32), biases)
        out_ref[2 * SLOT * count :, :] = biases.astype(out_ref.dtype)


def radial_kernel(x_ref, taps_ref, out_ref, even, odd, done, sems):
    n, a_loc, _, theta, c = x_ref.shape
    taps = taps_ref.shape[0]
    pad = (taps + 1) // 4
    zeros = jnp.zeros((pad, a_loc, 2 * theta, c), jnp.float32)
    even[0:pad] = zeros
    even[pad + n : 2 * pad + n] = zeros
    odd[0:pad] = zeros
    odd[pad + n - 1 : 2 * pad + n - 1] = zeros
    odd[2 * pad + n - 1 :] = zeros[:1]
    first = x_ref[:, :, 0].astype(jnp.float32)
    second = x_ref[:, :, 1].astype(jnp.float32)
    even[pad : pad + n, :, 0:theta] = first
    even[pad : pad + n, :, theta:] = second
    odd[pad : pad + n, :, 0:theta] = second
    odd[pad - 1 : pad + n - 1, :, theta:] = first

    block = 4

    def step(base, wanted):
        total = jnp.zeros((block, a_loc, 2 * theta, c), jnp.float32)
        for shift in wanted:
            k = shift + taps // 2
            source = even if shift % 2 == 0 else odd
            total = total + source[pl.ds(base + (pad + shift // 2), block)] * taps_ref[k : k + 1, :]
        done[pl.ds(base, block)] = total.astype(done.dtype)

    every = range(-(taps // 2), taps // 2 + 1)
    if n <= 8 * block:
        copies = []
        for base in range(0, n, block):
            step(base, [s for s in every if base + block - 1 + s // 2 >= -(s % 2) and base + s // 2 < n])
            part = pl.ds(base, block)
            copies.append(pltpu.make_async_copy(done.at[part], out_ref.at[part], sems.at[base // block]))
            copies[-1].start()
    else:
        pl.loop(0, n // block)(lambda i: step(i * block, every))
        copies = [pltpu.make_async_copy(done, out_ref, sems.at[0])]
        copies[0].start()
    for copy in copies:
        copy.wait()


def axial_kernel(z_ref, taps_ref, consts_ref, out_ref, padded, summed):
    axial, rows, c = z_ref.shape
    taps = taps_ref.shape[0]
    half = taps // 2
    zeros = jnp.zeros((half, rows, c), jnp.float32)
    padded[0:half] = zeros
    padded[half + axial :] = zeros
    padded[half : half + axial] = z_ref[...].astype(jnp.float32)
    block = 8

    def conv(base, wanted):
        total = jnp.zeros((block, rows, c), jnp.float32)
        for k in wanted:
            total = total + padded[pl.ds(base + k, block)] * taps_ref[k : k + 1, :]
        summed[pl.ds(base, block)] = total

    if axial <= 8 * block:
        for base in range(0, axial, block):
            conv(base, [k for k in range(taps) if base + block - 1 + k >= half and base + k < half + axial])
    else:
        pl.loop(0, axial // block)(lambda i: conv(i * block, range(taps)))

    def norm(i, carry):
        v = (summed[pl.ds(i * PLANES, PLANES)] + consts_ref[0 : 1, :]).reshape(PLANES * rows, c)
        v = v.astype(jnp.bfloat16).astype(jnp.float32)
        mean = jnp.mean(v, axis=-1, keepdims=True)
        centred = v - mean
        var = jnp.mean(centred * centred, axis=-1, keepdims=True)
        normed = centred * lax.rsqrt(var + 1e-06) * consts_ref[1 : 2, :] + consts_ref[2 : 3, :]
        at = pl.multiple_of(i * PLANES * rows, PLANES * rows)
        out_ref[pl.ds(at, PLANES * rows), :] = normed.astype(out_ref.dtype)
        return carry

    lax.fori_loop(0, axial // PLANES, norm, 0)


def hidden_sum(normed, blocks):
    c = normed.shape[1]
    per = c // SLOT
    lane_slot = lax.broadcasted_iota(jnp.int32, (1, c), 1) // SLOT
    slots = [(block, i) for block in blocks for i in range(block.shape[0] // (2 * SLOT))]
    total = None
    for g in range(0, len(slots), per):
        own = slots[g : g + per]
        w_in = jnp.concatenate([w[2 * SLOT * j : 2 * SLOT * j + SLOT, :] for w, j in own], axis=0)
        w_out = jnp.concatenate([w[2 * SLOT * j + SLOT : 2 * SLOT * (j + 1), :] for w, j in own], axis=0)
        bias = jnp.zeros((1, c), jnp.float32)
        for spot, (w, j) in enumerate(own):
            piece = w[w.shape[0] - EXTRA :, :].astype(jnp.float32)[j : j + 1]
            bias = jnp.where(lane_slot == spot, piece, bias)
        u = lax.dot_general(normed, w_in, (((1,), (1,)), ((), ())), preferred_element_type=jnp.float32)
        u = u + bias[:, : len(own) * SLOT]
        hidden = (0.5 * u * (1.0 + jnp.tanh(0.7978845608028654 * (u + 0.044715 * u * u * u)))).astype(jnp.bfloat16)
        part = jnp.dot(hidden, w_out, preferred_element_type=jnp.float32)
        total = part if total is None else total + part
    return total


def over_tokens(count, size, body):
    if count == size:
        body(0)
    else:
        pl.loop(0, count // size)(lambda i: body(pl.multiple_of(i * size, size)))


def first_kernel(normed_ref, *rest):
    *blocks, out_ref = rest
    size = PLANES * 8

    def part(at):
        out_ref[pl.ds(at, size), :] = hidden_sum(normed_ref[pl.ds(at, size), :], blocks)

    over_tokens(normed_ref.shape[0], size, part)


def mlp_kernel(partials, normed_ref, consts_ref, feat_ref, *rest):
    *blocks, out_ref, branch, done, sems = rest
    axial, _, theta, c = feat_ref.shape
    rows = 2 * theta
    planes = PLANES // 2

    def mlp(at, size):
        tokens = pl.ds(at * rows, size * rows)
        total = hidden_sum(normed_ref[tokens, :], blocks[partials:])
        for partial_ref in blocks[:partials]:
            total = total + partial_ref[tokens, :]
        result = (consts_ref[4 : 5, :] * (total + consts_ref[3 : 4, :])).astype(jnp.bfloat16).astype(jnp.float32)
        branch[pl.ds(at, size)] = result.reshape(size, rows, c)
        for r in range(2):
            got = branch[pl.ds(at, size), r * theta : (r + 1) * theta, :]
            done[pl.ds(at, size), r] = (feat_ref[pl.ds(at, size), r].astype(jnp.float32) + got).astype(done.dtype)

    copies = []
    if axial == PLANES:
        for i in range(2):
            mlp(i * planes, planes)
            part = pl.ds(i * planes, planes)
            copies.append(pltpu.make_async_copy(done.at[part], out_ref.at[part], sems.at[i]))
            copies[-1].start()
    else:
        pl.loop(0, axial // PLANES)(lambda i: mlp(pl.multiple_of(i * PLANES, PLANES), PLANES))
        copies.append(pltpu.make_async_copy(done, out_ref, sems.at[0]))
        copies[-1].start()
    for copy in copies:
        copy.wait()


def digits(n):
    chips = n // 2
    inner = 1
    while inner * inner * 4 <= chips:
        inner *= 2
    return chips // inner, inner, 2


def local(n, features, axial_taps, radial_taps, conv_bias, ln_gain, ln_bias, w_in, b_in, w_out, b_out, layer_scale):
    axial, r_loc, theta, c = features.shape
    rows = r_loc * theta
    hid_loc = w_in.shape[0]
    a_loc = axial // n
    outer, inner, _ = digits(n)
    spread = hid_loc == SLOT and n == 4 * outer and 2 < outer <= EXTRA
    small, middle, large = (pltpu.CompilerParams(vmem_limit_bytes=mib * 1024 * 1024) for mib in (2, 12, 24))
    anywhere = pl.BlockSpec(memory_space=pl.ANY)

    def move(piece, digit, by):
        stride = math.prod(digits(n)[digit + 1 :])
        return lax.ppermute(piece, "row", [(i, i ^ (by * stride)) for i in range(n)])

    vectors = [v[None, :] for v in (conv_bias, ln_gain, ln_bias, b_out, layer_scale)]
    if spread:
        own, consts = pl.pallas_call(
            pack_kernel,
            out_shape=[
                jax.ShapeDtypeStruct((2 * SLOT + EXTRA, c), jnp.bfloat16),
                jax.ShapeDtypeStruct((8, c), jnp.float32),
            ],
            in_specs=[vmem()] * 8,
            out_specs=[vmem()] * 2,
            compiler_params=small,
            name="pack",
        )(b_in, w_in, w_out, *vectors)
        line = [move(own, 0, by) for by in range(1, outer)]
        side = move(own, 1, 1)
    else:
        consts = jnp.concatenate(vectors + [jnp.zeros((3, c), jnp.float32)], axis=0)
        w_all = lax.all_gather(w_in, "row", axis=0, tiled=True).reshape(-1, SLOT, c)
        o_all = lax.all_gather(w_out, "row", axis=0, tiled=True).reshape(-1, SLOT, c)
        b_all = jnp.tile(lax.all_gather(b_in, "row", axis=0, tiled=True).reshape(-1, SLOT), (1, c // SLOT))
        w_all = jnp.concatenate([w_all, o_all], axis=1).reshape(-1, c)
        blocks = [jnp.concatenate([w_all, jnp.pad(b_all, ((0, EXTRA - b_all.shape[0]), (0, 0)))], axis=0)]

    got = lax.all_to_all(features, "row", split_axis=0, concat_axis=0, tiled=True)
    pad = (radial_taps.shape[0] + 1) // 4
    mixed = pl.pallas_call(
        radial_kernel,
        out_shape=jax.ShapeDtypeStruct((n, a_loc, rows, c), jnp.bfloat16),
        in_specs=[vmem()] * 2,
        out_specs=anywhere,
        scratch_shapes=[pltpu.VMEM((n + 2 * pad, a_loc, rows, c), jnp.float32)] * 2
        + [pltpu.VMEM((n, a_loc, rows, c), jnp.bfloat16), pltpu.SemaphoreType.DMA((8,))],
        compiler_params=middle,
        name="radial",
    )(got.reshape(n, a_loc, r_loc, theta, c), radial_taps)
    if spread:
        joined, reach = pl.pallas_call(
            join_kernel,
            out_shape=[jax.ShapeDtypeStruct((2 * SLOT * size + EXTRA, c), jnp.bfloat16) for size in (outer + 1, outer - 1)],
            in_specs=[anywhere] + [vmem()] * (outer + 1),
            out_specs=[vmem()] * 2,
            compiler_params=small,
            cost_estimate=pl.CostEstimate(flops=10**10, bytes_accessed=2 * 10**7, transcendentals=0),
            name="join",
        )(mixed, *line, own, side)
        across = [move(reach, 1, 1)]
        twin = move(joined, 2, 1)
    back = lax.all_to_all(mixed.reshape(axial, rows, c), "row", split_axis=0, concat_axis=0, tiled=True)
    normed = pl.pallas_call(
        axial_kernel,
        out_shape=jax.ShapeDtypeStruct((axial * rows, c), jnp.bfloat16),
        in_specs=[vmem()] * 3,
        out_specs=vmem(),
        scratch_shapes=[
            pltpu.VMEM((axial + axial_taps.shape[0] - 1, rows, c), jnp.float32),
            pltpu.VMEM((axial, rows, c), jnp.float32),
        ],
        compiler_params=middle,
        name="axial",
    )(back, axial_taps, consts)
    if spread:
        across, normed = lax.optimization_barrier((across, normed))
        blocks = [move(h, 2, 1) for h in across]
        partials = [
            pl.pallas_call(
                first_kernel,
                out_shape=jax.ShapeDtypeStruct((axial * rows, c), jnp.float32),
                in_specs=[vmem()] * (3 + len(across)),
                out_specs=vmem(),
                compiler_params=middle,
                name="first",
            )(normed, joined, twin, *across)
        ]
    else:
        partials = []
    operands = partials + blocks
    return pl.pallas_call(
        partial(mlp_kernel, len(partials)),
        out_shape=jax.ShapeDtypeStruct(features.shape, jnp.bfloat16),
        in_specs=[vmem()] * (3 + len(operands)),
        out_specs=anywhere,
        scratch_shapes=[
            pltpu.VMEM((axial, rows, c), jnp.float32),
            pltpu.VMEM(features.shape, jnp.bfloat16),
            pltpu.SemaphoreType.DMA((2,)),
        ],
        compiler_params=large,
        name="mlp",
    )(normed, consts, features, *operands)


def solution(mesh):
    in_specs = (
        P("groups", "row", None, None),
        P(),
        P(),
        P(),
        P(),
        P(),
        P("row", None),
        P("row"),
        P("row", None),
        P(),
        P(),
    )
    out_specs = P("groups", "row", None, None)
    return jax.shard_map(partial(local, mesh.shape["row"]), mesh=mesh, in_specs=in_specs, out_specs=out_specs, check_vma=False)
```

```python
import math
from functools import partial

import jax
import jax.numpy as jnp
from jax import lax
from jax.experimental import pallas as pl
from jax.experimental.pallas import tpu as pltpu
from jax.sharding import PartitionSpec as P

SLOT = 64
PLANES = 32
EXTRA = 16


def vmem():
    return pl.BlockSpec(memory_space=pltpu.VMEM)


def pack_kernel(b_ref, w_in_ref, w_out_ref, *rest):
    *vectors, block_ref, consts_ref = rest
    block_ref[0:SLOT, :] = w_in_ref[...]
    block_ref[SLOT : 2 * SLOT, :] = w_out_ref[...]
    bias = b_ref[...].astype(jnp.float32)[None, :]
    c = block_ref.shape[1]
    wide = jnp.concatenate([bias] * (c // SLOT), axis=1)
    block_ref[2 * SLOT :, :] = jnp.broadcast_to(wide, (EXTRA, c)).astype(block_ref.dtype)
    for i, vector in enumerate(vectors):
        consts_ref[i : i + 1, :] = vector[...]


def join_kernel(*refs):
    *blocks, all_ref, line_ref = refs[1:]
    c = all_ref.shape[1]
    row = lax.broadcasted_iota(jnp.int32, (EXTRA, c), 0)
    for out_ref in (all_ref, line_ref):
        count = out_ref.shape[0] // (2 * SLOT)
        biases = jnp.zeros((EXTRA, c), jnp.float32)
        for i, block in enumerate(blocks[:count]):
            out_ref[2 * SLOT * i : 2 * SLOT * (i + 1), :] = block[0 : 2 * SLOT, :]
            biases = jnp.where(row == i, block[2 * SLOT :, :].astype(jnp.float32), biases)
        out_ref[2 * SLOT * count :, :] = biases.astype(out_ref.dtype)


def radial_kernel(x_ref, taps_ref, out_ref, even, odd, done, sems):
    n, a_loc, _, theta, c = x_ref.shape
    taps = taps_ref.shape[0]
    pad = (taps + 1) // 4
    zeros = jnp.zeros((pad, a_loc, 2 * theta, c), jnp.float32)
    even[0:pad] = zeros
    even[pad + n : 2 * pad + n] = zeros
    odd[0:pad] = zeros
    odd[pad + n - 1 : 2 * pad + n - 1] = zeros
    odd[2 * pad + n - 1 :] = zeros[:1]
    first = x_ref[:, :, 0].astype(jnp.float32)
    second = x_ref[:, :, 1].astype(jnp.float32)
    even[pad : pad + n, :, 0:theta] = first
    even[pad : pad + n, :, theta:] = second
    odd[pad : pad + n, :, 0:theta] = second
    odd[pad - 1 : pad + n - 1, :, theta:] = first

    block = 4

    def step(base, wanted):
        total = jnp.zeros((block, a_loc, 2 * theta, c), jnp.float32)
        for shift in wanted:
            k = shift + taps // 2
            source = even if shift % 2 == 0 else odd
            total = total + source[pl.ds(base + (pad + shift // 2), block)] * taps_ref[k : k + 1, :]
        done[pl.ds(base, block)] = total.astype(done.dtype)

    every = range(-(taps // 2), taps // 2 + 1)
    if n <= 8 * block:
        copies = []
        for base in range(0, n, block):
            step(base, [s for s in every if base + block - 1 + s // 2 >= -(s % 2) and base + s // 2 < n])
            part = pl.ds(base, block)
            copies.append(pltpu.make_async_copy(done.at[part], out_ref.at[part], sems.at[base // block]))
            copies[-1].start()
    else:
        pl.loop(0, n // block)(lambda i: step(i * block, every))
        copies = [pltpu.make_async_copy(done, out_ref, sems.at[0])]
        copies[0].start()
    for copy in copies:
        copy.wait()


def axial_kernel(z_ref, taps_ref, consts_ref, out_ref, padded, summed):
    axial, rows, c = z_ref.shape
    taps = taps_ref.shape[0]
    half = taps // 2
    zeros = jnp.zeros((half, rows, c), jnp.float32)
    padded[0:half] = zeros
    padded[half + axial :] = zeros
    padded[half : half + axial] = z_ref[...].astype(jnp.float32)
    block = 8

    def conv(base, wanted):
        total = jnp.zeros((block, rows, c), jnp.float32)
        for k in wanted:
            total = total + padded[pl.ds(base + k, block)] * taps_ref[k : k + 1, :]
        summed[pl.ds(base, block)] = total

    if axial <= 8 * block:
        for base in range(0, axial, block):
            conv(base, [k for k in range(taps) if base + block - 1 + k >= half and base + k < half + axial])
    else:
        pl.loop(0, axial // block)(lambda i: conv(i * block, range(taps)))

    def norm(i, carry):
        v = (summed[pl.ds(i * PLANES, PLANES)] + consts_ref[0 : 1, :]).reshape(PLANES * rows, c)
        v = v.astype(jnp.bfloat16).astype(jnp.float32)
        mean = jnp.mean(v, axis=-1, keepdims=True)
        centred = v - mean
        var = jnp.mean(centred * centred, axis=-1, keepdims=True)
        normed = centred * lax.rsqrt(var + 1e-06) * consts_ref[1 : 2, :] + consts_ref[2 : 3, :]
        at = pl.multiple_of(i * PLANES * rows, PLANES * rows)
        out_ref[pl.ds(at, PLANES * rows), :] = normed.astype(out_ref.dtype)
        return carry

    lax.fori_loop(0, axial // PLANES, norm, 0)


def hidden_sum(normed, blocks):
    c = normed.shape[1]
    per = c // SLOT
    lane_slot = lax.broadcasted_iota(jnp.int32, (1, c), 1) // SLOT
    slots = [(block, i) for block in blocks for i in range(block.shape[0] // (2 * SLOT))]
    total = None
    for g in range(0, len(slots), per):
        own = slots[g : g + per]
        w_in = jnp.concatenate([w[2 * SLOT * j : 2 * SLOT * j + SLOT, :] for w, j in own], axis=0)
        w_out = jnp.concatenate([w[2 * SLOT * j + SLOT : 2 * SLOT * (j + 1), :] for w, j in own], axis=0)
        bias = jnp.zeros((1, c), jnp.float32)
        for spot, (w, j) in enumerate(own):
            piece = w[w.shape[0] - EXTRA :, :].astype(jnp.float32)[j : j + 1]
            bias = jnp.where(lane_slot == spot, piece, bias)
        u = lax.dot_general(normed, w_in, (((1,), (1,)), ((), ())), preferred_element_type=jnp.float32)
        u = u + bias[:, : len(own) * SLOT]
        hidden = (0.5 * u * (1.0 + jnp.tanh(0.7978845608028654 * (u + 0.044715 * u * u * u)))).astype(jnp.bfloat16)
        part = jnp.dot(hidden, w_out, preferred_element_type=jnp.float32)
        total = part if total is None else total + part
    return total


def over_tokens(count, size, body):
    if count == size:
        body(0)
    else:
        pl.loop(0, count // size)(lambda i: body(pl.multiple_of(i * size, size)))


def first_kernel(normed_ref, *rest):
    *blocks, out_ref = rest
    size = PLANES * 8

    def part(at):
        out_ref[pl.ds(at, size), :] = hidden_sum(normed_ref[pl.ds(at, size), :], blocks)

    over_tokens(normed_ref.shape[0], size, part)


def mlp_kernel(partials, normed_ref, consts_ref, feat_ref, *rest):
    *blocks, out_ref, branch, done, sems = rest
    axial, _, theta, c = feat_ref.shape
    rows = 2 * theta
    parts = 4

    def product(at):
        tokens = pl.ds(at * rows, PLANES * rows)
        total = hidden_sum(normed_ref[tokens, :], blocks[partials:])
        for partial_ref in blocks[:partials]:
            total = total + partial_ref[tokens, :]
        result = (consts_ref[4:5, :] * (total + consts_ref[3:4, :])).astype(jnp.bfloat16).astype(jnp.float32)
        branch[pl.ds(at, PLANES)] = result.reshape(PLANES, rows, c)

    if axial == PLANES:
        product(0)
    else:
        pl.loop(0, axial // PLANES)(lambda i: product(pl.multiple_of(i * PLANES, PLANES)))
    copies = []
    for i in range(parts):
        part = pl.ds(i * (axial // parts), axial // parts)
        for r in range(2):
            got = branch[part, r * theta : (r + 1) * theta, :]
            done[part, r] = (feat_ref[part, r].astype(jnp.float32) + got).astype(done.dtype)
        copies.append(pltpu.make_async_copy(done.at[part], out_ref.at[part], sems.at[i]))
        copies[-1].start()
    for copy in copies:
        copy.wait()


def digits(n):
    chips = n // 2
    inner = 1
    while inner * inner * 4 <= chips:
        inner *= 2
    return chips // inner, inner, 2


def local(n, features, axial_taps, radial_taps, conv_bias, ln_gain, ln_bias, w_in, b_in, w_out, b_out, layer_scale):
    axial, r_loc, theta, c = features.shape
    rows = r_loc * theta
    hid_loc = w_in.shape[0]
    a_loc = axial // n
    outer, inner, _ = digits(n)
    spread = hid_loc == SLOT and n == 4 * outer and 2 < outer <= EXTRA
    small, middle, large = (pltpu.CompilerParams(vmem_limit_bytes=mib * 1024 * 1024) for mib in (2, 12, 24))
    anywhere = pl.BlockSpec(memory_space=pl.ANY)

    def move(piece, digit, by):
        stride = math.prod(digits(n)[digit + 1 :])
        return lax.ppermute(piece, "row", [(i, i ^ (by * stride)) for i in range(n)])

    vectors = [v[None, :] for v in (conv_bias, ln_gain, ln_bias, b_out, layer_scale)]
    if spread:
        own, consts = pl.pallas_call(
            pack_kernel,
            out_shape=[
                jax.ShapeDtypeStruct((2 * SLOT + EXTRA, c), jnp.bfloat16),
                jax.ShapeDtypeStruct((8, c), jnp.float32),
            ],
            in_specs=[vmem()] * 8,
            out_specs=[vmem()] * 2,
            compiler_params=small,
            name="pack",
        )(b_in, w_in, w_out, *vectors)
        line = [move(own, 0, by) for by in range(1, outer)]
        side = move(own, 1, 1)
    else:
        consts = jnp.concatenate(vectors + [jnp.zeros((3, c), jnp.float32)], axis=0)
        w_all = lax.all_gather(w_in, "row", axis=0, tiled=True).reshape(-1, SLOT, c)
        o_all = lax.all_gather(w_out, "row", axis=0, tiled=True).reshape(-1, SLOT, c)
        b_all = jnp.tile(lax.all_gather(b_in, "row", axis=0, tiled=True).reshape(-1, SLOT), (1, c // SLOT))
        w_all = jnp.concatenate([w_all, o_all], axis=1).reshape(-1, c)
        blocks = [jnp.concatenate([w_all, jnp.pad(b_all, ((0, EXTRA - b_all.shape[0]), (0, 0)))], axis=0)]

    got = lax.all_to_all(features, "row", split_axis=0, concat_axis=0, tiled=True)
    pad = (radial_taps.shape[0] + 1) // 4
    mixed = pl.pallas_call(
        radial_kernel,
        out_shape=jax.ShapeDtypeStruct((n, a_loc, rows, c), jnp.bfloat16),
        in_specs=[vmem()] * 2,
        out_specs=anywhere,
        scratch_shapes=[pltpu.VMEM((n + 2 * pad, a_loc, rows, c), jnp.float32)] * 2
        + [pltpu.VMEM((n, a_loc, rows, c), jnp.bfloat16), pltpu.SemaphoreType.DMA((8,))],
        compiler_params=middle,
        name="radial",
    )(got.reshape(n, a_loc, r_loc, theta, c), radial_taps)
    if spread:
        joined, reach = pl.pallas_call(
            join_kernel,
            out_shape=[jax.ShapeDtypeStruct((2 * SLOT * size + EXTRA, c), jnp.bfloat16) for size in (outer + 1, outer - 1)],
            in_specs=[anywhere] + [vmem()] * (outer + 1),
            out_specs=[vmem()] * 2,
            compiler_params=small,
            cost_estimate=pl.CostEstimate(flops=10**10, bytes_accessed=2 * 10**7, transcendentals=0),
            name="join",
        )(mixed, *line, own, side)
        across = [move(reach, 1, 1)]
        twin = move(joined, 2, 1)
    back = lax.all_to_all(mixed.reshape(axial, rows, c), "row", split_axis=0, concat_axis=0, tiled=True)
    normed = pl.pallas_call(
        axial_kernel,
        out_shape=jax.ShapeDtypeStruct((axial * rows, c), jnp.bfloat16),
        in_specs=[vmem()] * 3,
        out_specs=vmem(),
        scratch_shapes=[
            pltpu.VMEM((axial + axial_taps.shape[0] - 1, rows, c), jnp.float32),
            pltpu.VMEM((axial, rows, c), jnp.float32),
        ],
        compiler_params=middle,
        name="axial",
    )(back, axial_taps, consts)
    if spread:
        across, normed = lax.optimization_barrier((across, normed))
        blocks = [move(h, 2, 1) for h in across]
        partials = [
            pl.pallas_call(
                first_kernel,
                out_shape=jax.ShapeDtypeStruct((axial * rows, c), jnp.float32),
                in_specs=[vmem()] * (3 + len(across)),
                out_specs=vmem(),
                compiler_params=middle,
                name="first",
            )(normed, joined, twin, *across)
        ]
    else:
        partials = []
    operands = partials + blocks
    return pl.pallas_call(
        partial(mlp_kernel, len(partials)),
        out_shape=jax.ShapeDtypeStruct(features.shape, jnp.bfloat16),
        in_specs=[vmem()] * (3 + len(operands)),
        out_specs=anywhere,
        scratch_shapes=[
            pltpu.VMEM((axial, rows, c), jnp.float32),
            pltpu.VMEM(features.shape, jnp.bfloat16),
            pltpu.SemaphoreType.DMA((4,)),
        ],
        compiler_params=large,
        name="mlp",
    )(normed, consts, features, *operands)


def solution(mesh):
    in_specs = (
        P("groups", "row", None, None),
        P(),
        P(),
        P(),
        P(),
        P(),
        P("row", None),
        P("row"),
        P("row", None),
        P(),
        P(),
    )
    out_specs = P("groups", "row", None, None)
    return jax.shard_map(partial(local, mesh.shape["row"]), mesh=mesh, in_specs=in_specs, out_specs=out_specs, check_vma=False)
```

```python
import math
from functools import partial

import jax
import jax.numpy as jnp
from jax import lax
from jax.experimental import pallas as pl
from jax.experimental.pallas import tpu as pltpu
from jax.sharding import PartitionSpec as P

SLOT = 64
PLANES = 32
EXTRA = 16


def vmem():
    return pl.BlockSpec(memory_space=pltpu.VMEM)


def pack_kernel(b_ref, w_in_ref, w_out_ref, *rest):
    *vectors, block_ref, consts_ref = rest
    block_ref[0:SLOT, :] = w_in_ref[...]
    block_ref[SLOT : 2 * SLOT, :] = w_out_ref[...]
    bias = b_ref[...].astype(jnp.float32)[None, :]
    c = block_ref.shape[1]
    wide = jnp.concatenate([bias] * (c // SLOT), axis=1)
    block_ref[2 * SLOT :, :] = jnp.broadcast_to(wide, (EXTRA, c)).astype(block_ref.dtype)
    for i, vector in enumerate(vectors):
        consts_ref[i : i + 1, :] = vector[...]


def join_kernel(*refs):
    *blocks, all_ref, line_ref = refs[1:]
    c = all_ref.shape[1]
    row = lax.broadcasted_iota(jnp.int32, (EXTRA, c), 0)
    for out_ref in (all_ref, line_ref):
        count = out_ref.shape[0] // (2 * SLOT)
        biases = jnp.zeros((EXTRA, c), jnp.float32)
        for i, block in enumerate(blocks[:count]):
            out_ref[2 * SLOT * i : 2 * SLOT * (i + 1), :] = block[0 : 2 * SLOT, :]
            biases = jnp.where(row == i, block[2 * SLOT :, :].astype(jnp.float32), biases)
        out_ref[2 * SLOT * count :, :] = biases.astype(out_ref.dtype)


def radial_kernel(x_ref, taps_ref, out_ref, even, odd, done, sems):
    n, a_loc, _, theta, c = x_ref.shape
    taps = taps_ref.shape[0]
    pad = (taps + 1) // 4
    zeros = jnp.zeros((pad, a_loc, 2 * theta, c), jnp.float32)
    even[0:pad] = zeros
    even[pad + n : 2 * pad + n] = zeros
    odd[0:pad] = zeros
    odd[pad + n - 1 : 2 * pad + n - 1] = zeros
    odd[2 * pad + n - 1 :] = zeros[:1]
    first = x_ref[:, :, 0].astype(jnp.float32)
    second = x_ref[:, :, 1].astype(jnp.float32)
    even[pad : pad + n, :, 0:theta] = first
    even[pad : pad + n, :, theta:] = second
    odd[pad : pad + n, :, 0:theta] = second
    odd[pad - 1 : pad + n - 1, :, theta:] = first

    block = 2

    def step(base, wanted):
        total = jnp.zeros((block, a_loc, 2 * theta, c), jnp.float32)
        for shift in wanted:
            k = shift + taps // 2
            source = even if shift % 2 == 0 else odd
            total = total + source[pl.ds(base + (pad + shift // 2), block)] * taps_ref[k : k + 1, :]
        done[pl.ds(base, block)] = total.astype(done.dtype)

    every = range(-(taps // 2), taps // 2 + 1)
    if n <= 8 * block:
        copies = []
        for base in range(0, n, block):
            step(base, [s for s in every if base + block - 1 + s // 2 >= -(s % 2) and base + s // 2 < n])
            part = pl.ds(base, block)
            copies.append(pltpu.make_async_copy(done.at[part], out_ref.at[part], sems.at[base // block]))
            copies[-1].start()
    else:
        pl.loop(0, n // block)(lambda i: step(i * block, every))
        copies = [pltpu.make_async_copy(done, out_ref, sems.at[0])]
        copies[0].start()
    for copy in copies:
        copy.wait()


def axial_kernel(z_ref, taps_ref, consts_ref, out_ref, padded, summed):
    axial, rows, c = z_ref.shape
    taps = taps_ref.shape[0]
    half = taps // 2
    zeros = jnp.zeros((half, rows, c), jnp.float32)
    padded[0:half] = zeros
    padded[half + axial :] = zeros
    padded[half : half + axial] = z_ref[...].astype(jnp.float32)
    block = 4

    def conv(base, wanted):
        total = jnp.zeros((block, rows, c), jnp.float32)
        for k in wanted:
            total = total + padded[pl.ds(base + k, block)] * taps_ref[k : k + 1, :]
        summed[pl.ds(base, block)] = total

    if axial <= 8 * block:
        for base in range(0, axial, block):
            conv(base, [k for k in range(taps) if base + block - 1 + k >= half and base + k < half + axial])
    else:
        pl.loop(0, axial // block)(lambda i: conv(i * block, range(taps)))

    def norm(i, carry):
        v = (summed[pl.ds(i * PLANES, PLANES)] + consts_ref[0 : 1, :]).reshape(PLANES * rows, c)
        v = v.astype(jnp.bfloat16).astype(jnp.float32)
        mean = jnp.mean(v, axis=-1, keepdims=True)
        centred = v - mean
        var = jnp.mean(centred * centred, axis=-1, keepdims=True)
        normed = centred * lax.rsqrt(var + 1e-06) * consts_ref[1 : 2, :] + consts_ref[2 : 3, :]
        at = pl.multiple_of(i * PLANES * rows, PLANES * rows)
        out_ref[pl.ds(at, PLANES * rows), :] = normed.astype(out_ref.dtype)
        return carry

    lax.fori_loop(0, axial // PLANES, norm, 0)


def hidden_sum(normed, blocks):
    c = normed.shape[1]
    per = c // SLOT
    lane_slot = lax.broadcasted_iota(jnp.int32, (1, c), 1) // SLOT
    slots = [(block, i) for block in blocks for i in range(block.shape[0] // (2 * SLOT))]
    total = None
    for g in range(0, len(slots), per):
        own = slots[g : g + per]
        w_in = jnp.concatenate([w[2 * SLOT * j : 2 * SLOT * j + SLOT, :] for w, j in own], axis=0)
        w_out = jnp.concatenate([w[2 * SLOT * j + SLOT : 2 * SLOT * (j + 1), :] for w, j in own], axis=0)
        bias = jnp.zeros((1, c), jnp.float32)
        for spot, (w, j) in enumerate(own):
            piece = w[w.shape[0] - EXTRA :, :].astype(jnp.float32)[j : j + 1]
            bias = jnp.where(lane_slot == spot, piece, bias)
        u = lax.dot_general(normed, w_in, (((1,), (1,)), ((), ())), preferred_element_type=jnp.float32)
        u = u + bias[:, : len(own) * SLOT]
        hidden = (0.5 * u * (1.0 + jnp.tanh(0.7978845608028654 * (u + 0.044715 * u * u * u)))).astype(jnp.bfloat16)
        part = jnp.dot(hidden, w_out, preferred_element_type=jnp.float32)
        total = part if total is None else total + part
    return total


def over_tokens(count, size, body):
    if count == size:
        body(0)
    else:
        pl.loop(0, count // size)(lambda i: body(pl.multiple_of(i * size, size)))


def first_kernel(normed_ref, *rest):
    *blocks, out_ref = rest
    size = PLANES * 8

    def part(at):
        out_ref[pl.ds(at, size), :] = hidden_sum(normed_ref[pl.ds(at, size), :], blocks)

    over_tokens(normed_ref.shape[0], size, part)


def mlp_kernel(partials, normed_ref, consts_ref, feat_ref, *rest):
    *blocks, out_ref, branch, done, sems = rest
    axial, _, theta, c = feat_ref.shape
    rows = 2 * theta
    parts = 4

    def product(at):
        tokens = pl.ds(at * rows, PLANES * rows)
        total = hidden_sum(normed_ref[tokens, :], blocks[partials:])
        for partial_ref in blocks[:partials]:
            total = total + partial_ref[tokens, :]
        result = (consts_ref[4:5, :] * (total + consts_ref[3:4, :])).astype(jnp.bfloat16).astype(jnp.float32)
        branch[pl.ds(at, PLANES)] = result.reshape(PLANES, rows, c)

    if axial == PLANES:
        product(0)
    else:
        pl.loop(0, axial // PLANES)(lambda i: product(pl.multiple_of(i * PLANES, PLANES)))
    copies = []
    for i in range(parts):
        part = pl.ds(i * (axial // parts), axial // parts)
        for r in range(2):
            got = branch[part, r * theta : (r + 1) * theta, :]
            done[part, r] = (feat_ref[part, r].astype(jnp.float32) + got).astype(done.dtype)
        copies.append(pltpu.make_async_copy(done.at[part], out_ref.at[part], sems.at[i]))
        copies[-1].start()
    for copy in copies:
        copy.wait()


def digits(n):
    chips = n // 2
    inner = 1
    while inner * inner * 4 <= chips:
        inner *= 2
    return chips // inner, inner, 2


def local(n, features, axial_taps, radial_taps, conv_bias, ln_gain, ln_bias, w_in, b_in, w_out, b_out, layer_scale):
    axial, r_loc, theta, c = features.shape
    rows = r_loc * theta
    hid_loc = w_in.shape[0]
    a_loc = axial // n
    outer, inner, _ = digits(n)
    spread = hid_loc == SLOT and n == 4 * outer and 2 < outer <= EXTRA
    small, middle, large = (pltpu.CompilerParams(vmem_limit_bytes=mib * 1024 * 1024) for mib in (2, 12, 24))
    anywhere = pl.BlockSpec(memory_space=pl.ANY)

    def move(piece, digit, by):
        stride = math.prod(digits(n)[digit + 1 :])
        return lax.ppermute(piece, "row", [(i, i ^ (by * stride)) for i in range(n)])

    vectors = [v[None, :] for v in (conv_bias, ln_gain, ln_bias, b_out, layer_scale)]
    if spread:
        own, consts = pl.pallas_call(
            pack_kernel,
            out_shape=[
                jax.ShapeDtypeStruct((2 * SLOT + EXTRA, c), jnp.bfloat16),
                jax.ShapeDtypeStruct((8, c), jnp.float32),
            ],
            in_specs=[vmem()] * 8,
            out_specs=[vmem()] * 2,
            compiler_params=small,
            name="pack",
        )(b_in, w_in, w_out, *vectors)
        line = [move(own, 0, by) for by in range(1, outer)]
        side = move(own, 1, 1)
    else:
        consts = jnp.concatenate(vectors + [jnp.zeros((3, c), jnp.float32)], axis=0)
        w_all = lax.all_gather(w_in, "row", axis=0, tiled=True).reshape(-1, SLOT, c)
        o_all = lax.all_gather(w_out, "row", axis=0, tiled=True).reshape(-1, SLOT, c)
        b_all = jnp.tile(lax.all_gather(b_in, "row", axis=0, tiled=True).reshape(-1, SLOT), (1, c // SLOT))
        w_all = jnp.concatenate([w_all, o_all], axis=1).reshape(-1, c)
        blocks = [jnp.concatenate([w_all, jnp.pad(b_all, ((0, EXTRA - b_all.shape[0]), (0, 0)))], axis=0)]

    got = lax.all_to_all(features, "row", split_axis=0, concat_axis=0, tiled=True)
    pad = (radial_taps.shape[0] + 1) // 4
    mixed = pl.pallas_call(
        radial_kernel,
        out_shape=jax.ShapeDtypeStruct((n, a_loc, rows, c), jnp.bfloat16),
        in_specs=[vmem()] * 2,
        out_specs=anywhere,
        scratch_shapes=[pltpu.VMEM((n + 2 * pad, a_loc, rows, c), jnp.float32)] * 2
        + [pltpu.VMEM((n, a_loc, rows, c), jnp.bfloat16), pltpu.SemaphoreType.DMA((8,))],
        compiler_params=middle,
        name="radial",
    )(got.reshape(n, a_loc, r_loc, theta, c), radial_taps)
    if spread:
        joined, reach = pl.pallas_call(
            join_kernel,
            out_shape=[jax.ShapeDtypeStruct((2 * SLOT * size + EXTRA, c), jnp.bfloat16) for size in (outer + 1, outer - 1)],
            in_specs=[anywhere] + [vmem()] * (outer + 1),
            out_specs=[vmem()] * 2,
            compiler_params=small,
            cost_estimate=pl.CostEstimate(flops=10**10, bytes_accessed=2 * 10**7, transcendentals=0),
            name="join",
        )(mixed, *line, own, side)
        across = [move(reach, 1, 1)]
        twin = move(joined, 2, 1)
    back = lax.all_to_all(mixed.reshape(axial, rows, c), "row", split_axis=0, concat_axis=0, tiled=True)
    normed = pl.pallas_call(
        axial_kernel,
        out_shape=jax.ShapeDtypeStruct((axial * rows, c), jnp.bfloat16),
        in_specs=[vmem()] * 3,
        out_specs=vmem(),
        scratch_shapes=[
            pltpu.VMEM((axial + axial_taps.shape[0] - 1, rows, c), jnp.float32),
            pltpu.VMEM((axial, rows, c), jnp.float32),
        ],
        compiler_params=middle,
        name="axial",
    )(back, axial_taps, consts)
    if spread:
        across, normed = lax.optimization_barrier((across, normed))
        blocks = [move(h, 2, 1) for h in across]
        partials = [
            pl.pallas_call(
                first_kernel,
                out_shape=jax.ShapeDtypeStruct((axial * rows, c), jnp.float32),
                in_specs=[vmem()] * (3 + len(across)),
                out_specs=vmem(),
                compiler_params=middle,
                name="first",
            )(normed, joined, twin, *across)
        ]
    else:
        partials = []
    operands = partials + blocks
    return pl.pallas_call(
        partial(mlp_kernel, len(partials)),
        out_shape=jax.ShapeDtypeStruct(features.shape, jnp.bfloat16),
        in_specs=[vmem()] * (3 + len(operands)),
        out_specs=anywhere,
        scratch_shapes=[
            pltpu.VMEM((axial, rows, c), jnp.float32),
            pltpu.VMEM(features.shape, jnp.bfloat16),
            pltpu.SemaphoreType.DMA((4,)),
        ],
        compiler_params=large,
        name="mlp",
    )(normed, consts, features, *operands)


def solution(mesh):
    in_specs = (
        P("groups", "row", None, None),
        P(),
        P(),
        P(),
        P(),
        P(),
        P("row", None),
        P("row"),
        P("row", None),
        P(),
        P(),
    )
    out_specs = P("groups", "row", None, None)
    return jax.shard_map(partial(local, mesh.shape["row"]), mesh=mesh, in_specs=in_specs, out_specs=out_specs, check_vma=False)
```
